256 devices in a mesh: rows: 32 (over x_lo, z, core), cols: 8 (over y, x_hi).
Axes of the slice: x: 4 (x_hi: 2, x_lo: 2; x = x_hi * 2 + x_lo), y: 4, z: 8, core: 2. Of those that a mesh axis runs over, the one named last changes fastest.
Arguments:
- density: float32 [8192, 8192], P('rows', 'cols'), may hold values from 0.25 to 4
- value_field: float32 [8192, 8192], P('rows', 'cols'), may hold values from -6 to 6
- potential: float32 [8192, 8192], P('rows', 'cols'), may hold values from -6 to 6
- kern_rows: float32 [256], replicated, may hold values from -0.375 to 0.375
- kern_cols: float32 [256], replicated, may hold values from -0.375 to 0.375
Outputs:
- density_out: float32 [8192, 8192], P('rows', 'cols')
- value_out: float32 [8192, 8192], P('rows', 'cols')
The draws below stay inside these ranges and needn't reach their ends.
All inputs are finite; a program needn't handle non-finite values.
Results may differ from the reference program's by a relative error of at most 0.0001.
Values sent between devices are 32-bit elements; how exact they have to be, the bound alone decides.
No kernel may reach another device: no remote copies, remote signals or barrier semaphores. Data moves between devices by JAX's collectives and lax.ppermute only.
A program may use at most 64 MiB of HBM per device.

```python
import math
import jax
import jax.numpy as jnp

KW = 256
STEPS = 2
NX = 8192
NY = 8192


def levels(own_key, dims, split, smallest, top_value):
    level = 1.0
    for position, parts in split:
        draws = jax.random.uniform(jax.random.fold_in(jax.random.fold_in(own_key, 6), position), (parts,), jnp.float32, smallest / len(split), top_value / len(split))
        level = level * jnp.repeat(jnp.exp(draws), dims[position] // parts).reshape((-1,) + (1,) * (len(dims) - 1 - position))
    return level


def gaussian(stream_key, dims, width, limit, split=(), kind=jnp.bfloat16):
    array = width * jax.random.normal(stream_key, dims, jnp.float32)
    if split:
        array = array * levels(stream_key, dims, split, -0.22, 0.18)
    return jnp.clip(array, -limit, limit).astype(kind)


def setup_inputs(seed: int = 0) -> dict:
    key_of = jax.random.split(jax.random.key(seed), 6)
    density = jnp.clip(jnp.exp(math.log(4.0) - 2.7725887 * jax.random.uniform(key_of[0], (NX, NY), jnp.float32) ** levels(key_of[0], (NX, NY), ((0, 32), (1, 8)), -0.2, 0.2)), 0.25, 4.0)
    value_field = gaussian(key_of[1], (NX, NY), 1.0, 6.0, ((0, 32), (1, 8)), jnp.float32)
    potential = gaussian(key_of[2], (NX, NY), 1.0, 6.0, ((0, 32), (1, 8)), jnp.float32)
    kern_rows = gaussian(key_of[3], (KW,), KW ** -0.5, 0.375, (), jnp.float32)
    kern_cols = gaussian(key_of[4], (KW,), KW ** -0.5, 0.375, (), jnp.float32)
    return {"density": density, "value_field": value_field, "potential": potential, "kern_rows": kern_rows, "kern_cols": kern_cols}


diffusion = 0.5
time_step = 0.1


def offset_view(padded, row_step, col_step):
    row_count = padded.shape[0] - 2
    col_count = padded.shape[1] - 2
    return padded[1 + row_step:1 + row_step + row_count, 1 + col_step:1 + col_step + col_count]


def density_step(dens_pad, value_pad):
    here_cell = offset_view(dens_pad, 0, 0)
    cell_up = offset_view(dens_pad, -1, 0)
    cell_down = offset_view(dens_pad, 1, 0)
    cell_left = offset_view(dens_pad, 0, -1)
    cell_right = offset_view(dens_pad, 0, 1)
    level_here = offset_view(value_pad, 0, 0)
    level_up = offset_view(value_pad, -1, 0)
    level_down = offset_view(value_pad, 1, 0)
    level_left = offset_view(value_pad, 0, -1)
    level_right = offset_view(value_pad, 0, 1)
    speed_down = level_here - level_down
    flux_down = jnp.maximum(speed_down, 0.0) * here_cell + jnp.minimum(speed_down, 0.0) * cell_down
    speed_up = level_up - level_here
    flux_up = jnp.maximum(speed_up, 0.0) * cell_up + jnp.minimum(speed_up, 0.0) * here_cell
    speed_right = level_here - level_right
    flux_right = jnp.maximum(speed_right, 0.0) * here_cell + jnp.minimum(speed_right, 0.0) * cell_right
    speed_left = level_left - level_here
    flux_left = jnp.maximum(speed_left, 0.0) * cell_left + jnp.minimum(speed_left, 0.0) * here_cell
    laplace = cell_up + cell_down + cell_left + cell_right - 4.0 * here_cell
    return here_cell + time_step * (diffusion * laplace - (flux_down - flux_up) - (flux_right - flux_left))


def value_step(value_pad, running_cost):
    level_here = offset_view(value_pad, 0, 0)
    level_up = offset_view(value_pad, -1, 0)
    level_down = offset_view(value_pad, 1, 0)
    level_left = offset_view(value_pad, 0, -1)
    level_right = offset_view(value_pad, 0, 1)
    grad_sq = jnp.square(jnp.maximum(level_here - level_up, 0.0)) + jnp.square(jnp.minimum(level_down - level_here, 0.0))
    grad_sq = grad_sq + jnp.square(jnp.maximum(level_here - level_left, 0.0)) + jnp.square(jnp.minimum(level_right - level_here, 0.0))
    laplace = level_up + level_down + level_left + level_right - 4.0 * level_here
    return level_here + time_step * (diffusion * laplace - 0.5 * grad_sq + running_cost)


def cyclic_conv(field, kernel, axis_number):
    length = field.shape[axis_number]
    half_width = kernel.shape[0] // 2
    zero_fill = jnp.zeros((length - kernel.shape[0],), jnp.float32)
    kernel_full = jnp.concatenate((kernel[half_width:], zero_fill, kernel[:half_width]))
    spectrum = jnp.fft.rfft(kernel_full)
    if axis_number == 1:
        shaped = spectrum[None, :]
    else:
        shaped = spectrum[:, None]
    result = jnp.fft.irfft(jnp.fft.rfft(field, axis=axis_number) * shaped, n=length, axis=axis_number)
    return result.astype(jnp.float32)


def reference(density, value_field, potential, kern_rows, kern_cols):
    for step_index in range(STEPS):
        dens_pad = jnp.pad(density, 1, mode="wrap")
        value_pad = jnp.pad(value_field, 1, mode="wrap")
        density = density_step(dens_pad, value_pad)
        spread = cyclic_conv(density, kern_cols, 1)
        congestion = cyclic_conv(spread, kern_rows, 0)
        value_field = value_step(value_pad, potential + congestion)
    return density, value_field
```

```python
import functools

import jax
import jax.numpy as jnp
from jax import lax
from jax.experimental import pallas as pl
from jax.experimental.pallas import tpu as pltpu
from jax.sharding import PartitionSpec as P

STEPS = 2
NU = 0.5
DT = 0.1

ROWS = 256
COLS = 1024
KW = 256
HR = 136
HL = 128
NR = ROWS + 2 * HR
NL = COLS + 2 * HL + 128
PAD = 8
SR = NR + 2 * PAD
LAST = ROWS - HR
EDGE_C = COLS - HL
BOTTOM = NR - HR

VMEM = pl.BlockSpec(memory_space=pltpu.VMEM)
F32 = jnp.float32
BF16 = jnp.bfloat16


def call(kernel, out_shapes, scratch, flops, byte_count, *operands):
    return pl.pallas_call(
        kernel,
        out_shape=out_shapes,
        in_specs=[VMEM] * len(operands),
        out_specs=[VMEM] * len(out_shapes),
        scratch_shapes=scratch,
        compiler_params=pltpu.CompilerParams(vmem_limit_bytes=40 * 1024 * 1024),
        cost_estimate=pl.CostEstimate(
            flops=flops, bytes_accessed=byte_count, transcendentals=0
        ),
    )(*operands)


def edge_starts():
    core = lax.rem(lax.axis_index("rows"), 2)
    far = pl.multiple_of(core * LAST, 8)
    near = pl.multiple_of((1 - core) * LAST, 8)
    return far, near


def table_kernel(v_ref, w_ref, rows_hi, rows_lo, cols_hi, cols_lo):
    v = jnp.broadcast_to(v_ref[0:1, :], (KW, 2 * KW))
    table = pltpu.roll(v, 0, 1, stride=1, stride_axis=0)
    hi = table.astype(BF16)
    rows_hi[...] = hi
    rows_lo[...] = (table - hi.astype(F32)).astype(BF16)
    w = jnp.broadcast_to(w_ref[0:1, :], (2 * KW, 3 * KW))
    table = pltpu.roll(w, 0, 1, stride=1, stride_axis=0)[:, :KW]
    hi = table.astype(BF16)
    cols_hi[...] = hi
    cols_lo[...] = (table - hi.astype(F32)).astype(BF16)


def tables(kern_rows, kern_cols):
    v = jnp.concatenate([jnp.zeros((1,), F32), kern_rows[::-1], jnp.zeros((KW - 1,), F32)])
    w = jnp.concatenate([jnp.zeros((2 * KW,), F32), kern_cols])
    v = jnp.broadcast_to(v[None], (8, 2 * KW))
    w = jnp.broadcast_to(w[None], (8, 3 * KW))
    shapes = [
        jax.ShapeDtypeStruct((KW, 2 * KW), BF16),
        jax.ShapeDtypeStruct((KW, 2 * KW), BF16),
        jax.ShapeDtypeStruct((2 * KW, KW), BF16),
        jax.ShapeDtypeStruct((2 * KW, KW), BF16),
    ]
    return call(table_kernel, shapes, [], 10**7, 10**6, v, w)


def pack_kernel(count, *refs):
    arrays = refs[:count]
    far_buf, near_buf, left_buf, right_buf = refs[count:]
    far, near = edge_starts()
    base = count * ROWS
    for n, ref in enumerate(arrays):
        far_buf[n * HR : (n + 1) * HR, :] = ref[pl.ds(far, HR), :]
        near_buf[n * HR : (n + 1) * HR, :] = ref[pl.ds(near, HR), :]
        left_buf[n * ROWS : (n + 1) * ROWS, :] = ref[:, 0:HL]
        right_buf[n * ROWS : (n + 1) * ROWS, :] = ref[:, EDGE_C:COLS]
        turned = ref[:, HL : HL + 128].T
        for half in range(2):
            rows = slice(base + 8 * half + 2 * n, base + 8 * half + 2 * n + 2)
            left_buf[rows, :] = turned[0:2, half * 128 : half * 128 + 128]
        turned = ref[:, EDGE_C - 128 : EDGE_C].T
        for half in range(2):
            rows = slice(base + 8 * half + 2 * n, base + 8 * half + 2 * n + 2)
            right_buf[rows, :] = turned[126:128, half * 128 : half * 128 + 128]


def pack(*arrays):
    count = len(arrays)
    shapes = [
        jax.ShapeDtypeStruct((count * HR, COLS), F32),
        jax.ShapeDtypeStruct((count * HR, COLS), F32),
        jax.ShapeDtypeStruct((count * ROWS + 16, HL), F32),
        jax.ShapeDtypeStruct((count * ROWS + 16, HL), F32),
    ]
    return call(functools.partial(pack_kernel, count), shapes, [], 10**6, 10**6, *arrays)


def corner_kernel(count, left_halo, right_halo, far_buf, near_buf):
    base = count * ROWS
    for buf, start in zip((far_buf, near_buf), edge_starts()):
        for side, halo in enumerate((left_halo, right_halo)):
            for n in range(count):
                at = (side * count + n) * HR
                buf[at : at + HR, :] = halo[pl.ds(n * ROWS + start, HR), :]
            at = 2 * count * HR + 16 * side
            buf[at : at + 16, :] = halo[base : base + 16, :]


def corners(count, left_halo, right_halo):
    shape = jax.ShapeDtypeStruct((2 * count * HR + 32, HL), F32)
    return call(
        functools.partial(corner_kernel, count), [shape, shape], [], 10**6, 10**6, left_halo, right_halo
    )


def row_pairs(count, first):
    pairs = []
    for a in range(first, count, 2):
        b = (a + 1) % count
        pairs += [(a, b), (b, a)]
    return pairs


def exchange(*arrays):
    count = len(arrays)
    far_buf, near_buf, left_buf, right_buf = pack(*arrays)
    n_rows = lax.axis_size("rows")
    n_cols = lax.axis_size("cols")
    to_right = [(c, (c + 1) % n_cols) for c in range(n_cols)]
    to_left = [(c, (c - 1) % n_cols) for c in range(n_cols)]
    far = lax.ppermute(far_buf, "rows", row_pairs(n_rows, 1))
    left = lax.ppermute(right_buf, "cols", to_right)
    right = lax.ppermute(left_buf, "cols", to_left)
    near = lax.ppermute(near_buf, "rows", row_pairs(n_rows, 0))
    far_corner, near_corner = corners(count, left, right)
    far_corner = lax.ppermute(far_corner, "rows", row_pairs(n_rows, 1))
    near_corner = lax.ppermute(near_corner, "rows", row_pairs(n_rows, 0))
    return far, near, left, right, far_corner, near_corner


def assemble(count, own, halos, extended, turn):
    far, near, left, right, far_corner, near_corner = halos
    core = lax.rem(lax.axis_index("rows"), 2)
    far_at = pl.multiple_of(PAD + core * BOTTOM, 8)
    near_at = pl.multiple_of(PAD + (1 - core) * BOTTOM, 8)
    far_from = pl.multiple_of((1 - core) * LAST, 8)
    near_from = pl.multiple_of(core * LAST, 8)
    zeros = jnp.zeros((128, ROWS), F32)
    mid = slice(PAD + HR, PAD + HR + ROWS)
    for n in range(count):
        ext = extended[n]
        ext[mid, HL : HL + COLS] = own[n][...]
        ext[mid, 0:HL] = left[n * ROWS : (n + 1) * ROWS, :]
        ext[mid, HL + COLS : 2 * HL + COLS] = right[n * ROWS : (n + 1) * ROWS, :]
        base = count * ROWS
        turn[...] = zeros
        for half in range(2):
            lanes = slice(half * 128, half * 128 + 128)
            at = base + 8 * half + 2 * n
            turn[0:2, lanes] = right[at : at + 2, :]
            turn[126:128, lanes] = left[at : at + 2, :]
        ext[mid, 2 * HL + COLS : NL] = turn[...].T
        for rows_buf, corner, at_row, from_row in (
            (far, far_corner, far_at, far_from),
            (near, near_corner, near_at, near_from),
        ):
            ext[pl.ds(at_row, HR), HL : HL + COLS] = rows_buf[n * HR : (n + 1) * HR, :]
            ext[pl.ds(at_row, HR), 0:HL] = corner[n * HR : (n + 1) * HR, :]
            right_rows = slice((count + n) * HR, (count + n + 1) * HR)
            ext[pl.ds(at_row, HR), HL + COLS : 2 * HL + COLS] = corner[right_rows, :]
            base_t = 2 * count * HR
            for half in range(2):
                lanes = slice(half * 128, half * 128 + 128)
                at = base_t + 8 * half + 2 * n
                turn[126:128, lanes] = corner[at : at + 2, :]
                turn[0:2, lanes] = corner[at + 16 : at + 18, :]
            turned = turn[...].T
            ext[pl.ds(at_row, HR), 2 * HL + COLS : NL] = jnp.where(
                core == (0 if rows_buf is far else 1), turned[LAST:ROWS, :], turned[0:HR, :]
            )


def advance_density(dens, value, out):
    shape = (8, NL)
    sub = lax.broadcasted_iota(jnp.int32, shape, 0)
    top = sub == 0
    end = sub == 7
    c = DT * NU

    def flux(a, here, there):
        a = DT * a
        return here * jnp.maximum(a + c, c) + there * jnp.minimum(a - c, -c)

    def step(i, carry):
        flux_before, m, u = carry
        r = pl.multiple_of(8 * i, 8)
        m_next = dens[pl.ds(r + 8, 8), :]
        u_next = value[pl.ds(r + 8, 8), :]
        m_down = pltpu.roll(jnp.where(top, m_next, m), 7, 0)
        u_down = pltpu.roll(jnp.where(top, u_next, u), 7, 0)
        flux_x = flux(u - u_down, m, m_down)
        flux_up = pltpu.roll(jnp.where(end, flux_before, flux_x), 1, 0)
        m_right = pltpu.roll(m, NL - 1, 1)
        u_right = pltpu.roll(u, NL - 1, 1)
        flux_y = flux(u - u_right, m, m_right)
        flux_left = pltpu.roll(flux_y, 1, 1)

        @pl.when(i > 0)
        def _():
            out[pl.ds(pl.multiple_of(r - 8, 8), 8), :] = m - (
                (flux_x - flux_up) + (flux_y - flux_left)
            )

        return flux_x, m_next, u_next

    start = (jnp.zeros(shape, F32), dens[0:8, :], value[0:8, :])
    lax.fori_loop(0, NR // 8 + 1, step, start)


def split(x):
    hi = x.astype(BF16)
    return hi, (x - hi.astype(F32)).astype(BF16)


def dot(a, b):
    return jnp.dot(a, b, preferred_element_type=F32)


def convolve(dens, rows_hi, rows_lo, cols_hi, cols_lo, mix_hi, mix_lo, out):
    for b in range((COLS + 2 * HL) // 256):
        lanes = slice(256 * b, 256 * b + 256)
        hi, lo = split(dens[HR - 128 : HR - 128 + 2 * KW, lanes])
        mixed = dot(rows_hi[...], hi) + dot(rows_hi[...], lo) + dot(rows_lo[...], hi)
        hi, lo = split(mixed)
        mix_hi[:, lanes] = hi
        mix_lo[:, lanes] = lo
    for b in range(COLS // 256):
        lanes = slice(256 * b, 256 * b + 2 * KW)
        hi = mix_hi[:, lanes]
        lo = mix_lo[:, lanes]
        out[:, 256 * b : 256 * b + 256] = (
            dot(hi, cols_hi[...]) + dot(lo, cols_hi[...]) + dot(hi, cols_lo[...])
        )


def advance_value(value, potential, cong, out):
    width = COLS + 2 * HL
    shape = (8, width)
    sub = lax.broadcasted_iota(jnp.int32, shape, 0)
    top = sub == 0
    end = sub == 7
    own = slice(HL, HL + COLS)

    def step(i, carry):
        before, u = carry
        r = pl.multiple_of(PAD + HR + 8 * i, 8)
        u_next = value[pl.ds(r + 8, 8), 0:width]
        down = pltpu.roll(jnp.where(top, u_next, u), 7, 0) - u
        up = pltpu.roll(jnp.where(end, before, down), 1, 0)
        right = pltpu.roll(u, width - 1, 1) - u
        left = pltpu.roll(right, 1, 1)
        down_o, up_o, right_o, left_o = down[:, own], up[:, own], right[:, own], left[:, own]
        grad_sq = (
            jnp.square(jnp.maximum(up_o, 0.0))
            + jnp.square(jnp.minimum(down_o, 0.0))
            + jnp.square(jnp.maximum(left_o, 0.0))
            + jnp.square(jnp.minimum(right_o, 0.0))
        )
        lap = (down_o - up_o) + (right_o - left_o)
        rows = pl.ds(pl.multiple_of(8 * i, 8), 8)
        cost = potential[rows, :] + cong[rows, :]
        out[rows, :] = u[:, own] + DT * (NU * lap - 0.5 * grad_sq + cost)
        return down, u_next

    first = PAD + HR
    u_before = value[first - 8 : first, 0:width]
    u_first = value[first : first + 8, 0:width]
    before = pltpu.roll(jnp.where(top, u_first, u_before), 7, 0) - u_before
    lax.fori_loop(0, ROWS // 8, step, (before, u_first))


def first_kernel(*refs):
    dens, value, potential = refs[:3]
    table = refs[3:7]
    halos = refs[7:13]
    dens_ext, value_out = refs[13:15]
    dens_pad, value_pad, mix_hi, mix_lo, cong, turn = refs[15:]
    assemble(2, (dens, value), halos, (dens_pad, value_pad), turn)
    advance_density(dens_pad, value_pad, dens_ext.at[PAD : PAD + NR])
    dens_ext[0:PAD, :] = jnp.zeros((PAD, NL), F32)
    dens_ext[PAD + NR : SR, :] = jnp.zeros((PAD, NL), F32)
    convolve(dens_ext.at[PAD : PAD + NR], *table, mix_hi, mix_lo, cong)
    advance_value(value_pad, potential, cong, value_out)


def second_kernel(*refs):
    dens_ext, value, potential = refs[:3]
    table = refs[3:7]
    halos = refs[7:13]
    dens_out, value_out = refs[13:15]
    dens_new, value_pad, mix_hi, mix_lo, cong, turn = refs[15:]
    assemble(1, (value,), halos, (value_pad,), turn)
    advance_density(dens_ext, value_pad, dens_new)
    dens_out[...] = dens_new[HR : HR + ROWS, HL : HL + COLS]
    convolve(dens_new, *table, mix_hi, mix_lo, cong)
    advance_value(value_pad, potential, cong, value_out)


def body(density, value_field, potential, kern_rows, kern_cols):
    block = jax.ShapeDtypeStruct((ROWS, COLS), F32)
    mix = [
        pltpu.VMEM((ROWS, COLS + 2 * HL), BF16),
        pltpu.VMEM((ROWS, COLS + 2 * HL), BF16),
        pltpu.VMEM((ROWS, COLS), F32),
        pltpu.VMEM((128, ROWS), F32),
    ]
    table = tables(kern_rows, kern_cols)
    halos = exchange(density, value_field)
    dens_ext, value = call(
        first_kernel,
        [jax.ShapeDtypeStruct((SR, NL), F32), block],
        [pltpu.VMEM((SR, NL), F32), pltpu.VMEM((SR, NL), F32)] + mix,
        2 * 10**9,
        10**7,
        density,
        value_field,
        potential,
        *table,
        *halos,
    )
    halos = exchange(value)
    return tuple(
        call(
            second_kernel,
            [block, block],
            [pltpu.VMEM((NR, NL), F32), pltpu.VMEM((SR, NL), F32)] + mix,
            2 * 10**9,
            10**7,
            dens_ext,
            value,
            potential,
            *table,
            *halos,
        )
    )


def solution(mesh):
    placed = (P("rows", "cols"), P("rows", "cols"), P("rows", "cols"), P(), P())
    return jax.shard_map(
        body,
        mesh=mesh,
        in_specs=placed,
        out_specs=(P("rows", "cols"), P("rows", "cols")),
        check_vma=False,
    )
```

```python
import functools

import jax
import jax.numpy as jnp
from jax import lax
from jax.experimental import pallas as pl
from jax.experimental.pallas import tpu as pltpu
from jax.sharding import PartitionSpec as P

STEPS = 2
NU = 0.5
DT = 0.1

ROWS = 256
COLS = 1024
KW = 256
HALF = KW // 2
EDGE = 128
MID = COLS - 2 * EDGE
FROM_R = COLS - EDGE
RAW_AT = HALF
TURNED_AT = RAW_AT + 16
FIRST_ROWS = TURNED_AT + 8
TALL = 3 * ROWS
SEGMENTS = TALL // EDGE
COL_ROWS = ROWS + 4 * SEGMENTS

VMEM = pl.BlockSpec(memory_space=pltpu.VMEM)
F32 = jnp.float32
BF16 = jnp.bfloat16


def shape(*dims, kind=F32):
    return jax.ShapeDtypeStruct(dims, kind)


def call(kernel, out_shapes, scratch, micros, *operands):
    return pl.pallas_call(
        kernel,
        out_shape=out_shapes,
        in_specs=[VMEM] * len(operands),
        out_specs=[VMEM] * len(out_shapes),
        scratch_shapes=scratch,
        compiler_params=pltpu.CompilerParams(vmem_limit_bytes=32 * 1024 * 1024),
        cost_estimate=pl.CostEstimate(
            flops=int(micros * 10**9), bytes_accessed=int(micros * 3 * 10**6), transcendentals=0
        ),
    )(*operands)


def core_index():
    return lax.rem(lax.axis_index("rows"), 2)


def split(x):
    hi = x.astype(BF16)
    return hi, (x - hi.astype(F32)).astype(BF16)


def product(left, right):
    dot = functools.partial(jnp.dot, preferred_element_type=F32)
    return dot(left[0], right[0]) + (dot(left[1], right[0]) + dot(left[0], right[1]))


def put_split(refs, x):
    refs[0][...], refs[1][...] = split(x)


def table_kernel(v_ref, w_ref, rows_hi, rows_lo, turned_hi, turned_lo, cols_hi, cols_lo):
    v = jnp.broadcast_to(v_ref[0:1, :], (KW, 2 * KW))
    put_split((rows_hi, rows_lo), pltpu.roll(v, 0, 1, stride=1, stride_axis=0))
    for n, refs in enumerate(((turned_hi, turned_lo), (cols_hi, cols_lo))):
        w = jnp.broadcast_to(w_ref[n : n + 1, :], (2 * KW, 3 * KW))
        put_split(refs, pltpu.roll(w, 0, 1, stride=1, stride_axis=0)[:, :KW])


def tables(kern_rows, kern_cols):
    v = jnp.concatenate([jnp.zeros((1,), F32), kern_rows[::-1], jnp.zeros((KW - 1,), F32)])
    w = jnp.pad(jnp.stack([kern_rows, kern_cols]), ((0, 6), (2 * KW, 0)))
    v = jnp.broadcast_to(v[None], (8, 2 * KW))
    shapes = [shape(KW, 2 * KW, kind=BF16)] * 2 + [shape(2 * KW, KW, kind=BF16)] * 4
    out = call(table_kernel, shapes, [], 0.3, v, w)
    return out[0:2], out[2:4], out[4:6]


def flux(a, here, there):
    c = DT * NU
    a = DT * a
    return here * jnp.maximum(a + c, c) + there * jnp.minimum(a - c, -c)


def eight_rows(m, u):
    width = m.shape[1]
    flux_x = flux(u - pltpu.roll(u, 7, 0), m, pltpu.roll(m, 7, 0))
    flux_y = flux(u - pltpu.roll(u, width - 1, 1), m, pltpu.roll(m, width - 1, 1))
    return m - ((flux_x - pltpu.roll(flux_x, 1, 0)) + (flux_y - pltpu.roll(flux_y, 1, 1)))


def inner_density(dens, value, out):
    dims = (8, COLS)
    sub = lax.broadcasted_iota(jnp.int32, dims, 0)
    top = sub == 0
    end = sub == 7

    def step(i, flux_before):
        rows = pl.ds(pl.multiple_of(8 * i, 8), 8)
        after = pl.ds(pl.multiple_of(jnp.minimum(8 * i + 8, ROWS - 8), 8), 8)
        m = dens[rows, :]
        u = value[rows, :]
        m_down = pltpu.roll(jnp.where(top, dens[after, :], m), 7, 0)
        u_down = pltpu.roll(jnp.where(top, value[after, :], u), 7, 0)
        flux_x = flux(u - u_down, m, m_down)
        flux_up = pltpu.roll(jnp.where(end, flux_before, flux_x), 1, 0)
        flux_y = flux(u - pltpu.roll(u, COLS - 1, 1), m, pltpu.roll(m, COLS - 1, 1))
        out[rows, :] = m - ((flux_x - flux_up) + (flux_y - pltpu.roll(flux_y, 1, 1)))
        return flux_x

    lax.fori_loop(0, ROWS // 8, step, jnp.zeros(dims, F32), unroll=4)


def inner_value(value, potential, around, out):
    dims = (8, COLS)
    sub = lax.broadcasted_iota(jnp.int32, dims, 0)
    top = sub == 0
    end = sub == 7
    below = jnp.broadcast_to(around[6:7, :], dims)
    above = jnp.broadcast_to(around[1:2, :], dims)
    first = value[0:8, :] - above

    def step(i, before):
        rows = pl.ds(pl.multiple_of(8 * i, 8), 8)
        after = pl.ds(pl.multiple_of(jnp.minimum(8 * i + 8, ROWS - 8), 8), 8)
        u = value[rows, :]
        u_next = jnp.where(i == ROWS // 8 - 1, below, value[after, :])
        down = pltpu.roll(jnp.where(top, u_next, u), 7, 0) - u
        up = pltpu.roll(jnp.where(end, before, down), 1, 0)
        right = pltpu.roll(u, COLS - 1, 1) - u
        left = pltpu.roll(right, 1, 1)
        out[rows, :] = value_formula(u, down, up, right, left, potential[rows, :])
        return down

    start = jnp.broadcast_to(first[0:1, :], dims)
    lax.fori_loop(0, ROWS // 8, step, start, unroll=4)


def value_formula(u, down, up, right, left, cost):
    grad_sq = (
        jnp.square(jnp.maximum(up, 0.0))
        + jnp.square(jnp.minimum(down, 0.0))
        + jnp.square(jnp.maximum(left, 0.0))
        + jnp.square(jnp.minimum(right, 0.0))
    )
    lap = (down - up) + (right - left)
    return u + DT * (NU * lap - 0.5 * grad_sq + cost)


def prepare(dens, value, new, own_t, far_1, near_1, far_2, near_2):
    core = core_index()
    inner_density(dens, value, new)
    own_t[0:2, :] = dens[:, 0:EDGE].T[0:2, :]
    own_t[2:4, :] = dens[:, FROM_R:COLS].T[EDGE - 2 : EDGE, :]
    own_t[4:6, :] = value[:, 0:EDGE].T[0:2, :]
    own_t[6:8, :] = value[:, FROM_R:COLS].T[EDGE - 2 : EDGE, :]
    for one, two, bottom in ((far_1, far_2, core), (near_1, near_2, 1 - core)):
        rows = pl.ds(pl.multiple_of(bottom * HALF, 8), HALF)
        one[0:HALF, 0:EDGE] = new[rows, 0:EDGE]
        one[0:HALF, EDGE : 2 * EDGE] = new[rows, FROM_R:COLS]
        two[...] = new[rows, EDGE:FROM_R]
        tile = pl.ds(pl.multiple_of(bottom * (ROWS - 8), 8), 8)
        for n, ref in enumerate((dens, value)):
            eight = ref[tile, :]
            pair = jnp.where(bottom == 1, eight[6:8, :], eight[0:2, :])
            for q in range(COLS // 256):
                at = RAW_AT + 4 * q + 2 * n
                one[at : at + 2, :] = pair[:, 256 * q : 256 * q + 256]
        one[TURNED_AT:FIRST_ROWS, :] = own_t[...]


MESSAGES = [
    shape(ROWS, COLS),
    shape(8, ROWS),
    shape(FIRST_ROWS, 2 * EDGE),
    shape(FIRST_ROWS, 2 * EDGE),
    shape(HALF, MID),
    shape(HALF, MID),
]


def halo_rows(ext, far, near):
    core = core_index()
    ext[pl.ds(pl.multiple_of(core * (HALF + ROWS), 8), HALF), :] = far
    ext[pl.ds(pl.multiple_of((1 - core) * (HALF + ROWS), 8), HALF), :] = near


def edge_kernel(
    dens, value, new, own_t, far, near, rows_hi, rows_lo,
    to_left, to_right, seams, around, tall, mixed, dens_8, ext,
):
    core = core_index()
    for ref, own, n in ((dens_8, dens, 0), (around, value, 1)):
        for q in range(COLS // 256):
            lanes = slice(256 * q, 256 * q + 256)
            at = RAW_AT + 4 * q + 2 * n
            f = far[at : at + 2, :]
            g = near[at : at + 2, :]
            ref[0:2, lanes] = jnp.where(core == 0, f, g)
            ref[6:8, lanes] = jnp.where(core == 0, g, f)
        ref[2:4, :] = own[0:2, :]
        ref[4:6, :] = own[ROWS - 2 : ROWS, :]
    seam = eight_rows(dens_8[...], around[...])
    seams[...] = seam
    f = far[TURNED_AT:FIRST_ROWS, :]
    g = near[TURNED_AT:FIRST_ROWS, :]
    tall[:, 0:ROWS] = jnp.where(core == 0, f, g)
    tall[:, ROWS : 2 * ROWS] = own_t[...]
    tall[:, 2 * ROWS : TALL] = jnp.where(core == 0, g, f)

    halo_rows(ext, far[0:HALF, :], near[0:HALF, :])
    ext[HALF : HALF + ROWS, 0:EDGE] = new[:, 0:EDGE]
    ext[HALF : HALF + ROWS, EDGE : 2 * EDGE] = new[:, FROM_R:COLS]
    put_seams(ext, seams, ((slice(0, EDGE), slice(0, EDGE)), (slice(EDGE, 2 * EDGE), slice(FROM_R, COLS))))
    result = product((rows_hi[...], rows_lo[...]), split(ext[...]))
    mixed[...] = result
    for ref, lanes, at in ((to_left, slice(0, EDGE), 0), (to_right, slice(EDGE, 2 * EDGE), 2)):
        ref[0:ROWS, :] = result[:, lanes]
        for q in range(SEGMENTS):
            segment = slice(EDGE * q, EDGE * q + EDGE)
            ref[ROWS + 4 * q : ROWS + 4 * q + 2, :] = tall[at : at + 2, segment]
            ref[ROWS + 4 * q + 2 : ROWS + 4 * q + 4, :] = tall[at + 4 : at + 6, segment]


def put_seams(ext, seams, lane_pairs):
    for to, source in lane_pairs:
        ext[HALF - 1 : HALF, to] = seams[1:2, source]
        ext[HALF : HALF + 1, to] = seams[2:3, source]
        ext[HALF + ROWS - 1 : HALF + ROWS, to] = seams[5:6, source]
        ext[HALF + ROWS : HALF + ROWS + 1, to] = seams[6:7, source]


def middle_kernel(
    new, value, potential, seams, around, far, near, rows_hi, rows_lo, cols_hi, cols_lo,
    cong, inner, ext, mix_hi, mix_lo,
):
    halo_rows(ext, far[...], near[...])
    ext[HALF : HALF + ROWS, :] = new[:, EDGE:FROM_R]
    put_seams(ext, seams, ((slice(0, MID), slice(EDGE, FROM_R)),))
    rows = (rows_hi[...], rows_lo[...])
    for b in range(MID // 256):
        lanes = slice(256 * b, 256 * b + 256)
        mix_hi[:, lanes], mix_lo[:, lanes] = split(product(rows, split(ext[:, lanes])))
    before = (cols_hi[0:KW, :], cols_lo[0:KW, :])
    after = (cols_hi[KW : 2 * KW, :], cols_lo[KW : 2 * KW, :])
    for b in range(COLS // 256):
        total = None
        for block, table in ((b - 1, before), (b, after)):
            if 0 <= block < MID // 256:
                lanes = slice(256 * block, 256 * block + 256)
                part = product((mix_hi[:, lanes], mix_lo[:, lanes]), table)
                total = part if total is None else total + part
        cong[:, 256 * b : 256 * b + 256] = total
    inner_value(value, potential, around, inner)


def finish(
    potential, new, seams, tall, left, right, mixed, cong, inner, turned_table, cols_hi, cols_lo,
    dens_out, value_out, dens_t, value_t, turn,
):
    for ref, n in ((dens_t, 0), (value_t, 1)):
        for q in range(SEGMENTS):
            lanes = slice(EDGE * q, EDGE * q + EDGE)
            at = ROWS + 4 * q + 2 * n
            ref[0:2, lanes] = left[at : at + 2, :]
            ref[6:8, lanes] = right[at : at + 2, :]
        ref[2:6, :] = tall[4 * n : 4 * n + 4, :]
    u = value_t[...]
    new_t = eight_rows(dens_t[...], u)
    window = new_t[:, HALF : HALF + 2 * KW]
    window = jnp.concatenate([window, window], axis=0)
    turn[0:8, :] = product(split(window), (turned_table[0][...], turned_table[1][...]))[0:8, :]
    own = slice(ROWS, 2 * ROWS)
    turn[8:16, :] = new_t[:, own]
    right_t = pltpu.roll(u, 7, 0) - u
    left_t = u - pltpu.roll(u, 1, 0)
    down_t = pltpu.roll(u, TALL - 1, 1) - u
    up_t = u - pltpu.roll(u, 1, 1)
    turn[24:26, :] = potential[:, 0:EDGE].T[0:2, :]
    turn[26:28, :] = potential[:, FROM_R:COLS].T[EDGE - 2 : EDGE, :]
    cost_t = jnp.concatenate([turn[24:26, :], turn[24:28, :], turn[26:28, :]], axis=0)
    turn[16:24, :] = value_formula(
        u[:, own], down_t[:, own], up_t[:, own], right_t[:, own], left_t[:, own], cost_t
    )
    columns = turn[...].T

    def column(n):
        return columns[:, n : n + 1]

    lane = lax.broadcasted_iota(jnp.int32, (ROWS, 2 * EDGE), 1)
    before = (cols_hi[0:KW, :], cols_lo[0:KW, :])
    after = (cols_hi[KW : 2 * KW, :], cols_lo[KW : 2 * KW, :])
    low = jnp.concatenate([left[0:ROWS, :], mixed[:, 0:EDGE]], axis=1)
    low = jnp.where(lane == EDGE - 1, column(1), jnp.where(lane == EDGE, column(2), low))
    low = cong[:, 0:256] + product(split(low), before)
    high = jnp.concatenate([mixed[:, EDGE : 2 * EDGE], right[0:ROWS, :]], axis=1)
    high = jnp.where(lane == EDGE - 1, column(5), jnp.where(lane == EDGE, column(6), high))
    high = cong[:, COLS - 256 : COLS] + product(split(high), after)

    lane = lax.broadcasted_iota(jnp.int32, (ROWS, EDGE), 1)
    inside = slice(256, COLS - 256)
    value_out[:, inside] = inner[:, inside] + DT * cong[:, inside]
    value_out[:, EDGE:256] = inner[:, EDGE:256] + DT * low[:, EDGE:256]
    value_out[:, COLS - 256 : FROM_R] = inner[:, COLS - 256 : FROM_R] + DT * high[:, 0:EDGE]
    value_out[:, 0:EDGE] = jnp.where(lane == 0, column(18), inner[:, 0:EDGE]) + DT * low[:, 0:EDGE]
    value_out[:, FROM_R:COLS] = (
        jnp.where(lane == EDGE - 1, column(21), inner[:, FROM_R:COLS]) + DT * high[:, EDGE:256]
    )
    dens_out[:, EDGE:FROM_R] = new[:, EDGE:FROM_R]
    dens_out[0:1, EDGE:FROM_R] = seams[2:3, EDGE:FROM_R]
    dens_out[ROWS - 1 : ROWS, EDGE:FROM_R] = seams[5:6, EDGE:FROM_R]
    row = lax.broadcasted_iota(jnp.int32, (ROWS, EDGE), 0)
    for lanes, at, n in ((slice(0, EDGE), 0, 10), (slice(FROM_R, COLS), EDGE - 1, 13)):
        block = jnp.where(row == 0, seams[2:3, lanes], new[:, lanes])
        block = jnp.where(row == ROWS - 1, seams[5:6, lanes], block)
        dens_out[:, lanes] = jnp.where(lane == at, column(n), block)


FINISH_SCRATCH = [
    pltpu.VMEM((8, TALL), F32),
    pltpu.VMEM((8, TALL), F32),
    pltpu.VMEM((128, ROWS), F32),
]


def finish_kernel(*refs):
    finish(*refs[:9], refs[9:11], *refs[11:])


def finish_prepare_kernel(*refs):
    outs = refs[13:21]
    finish(*refs[:9], refs[9:11], *refs[11:13], *outs[:2], *refs[21:])
    prepare(*outs)


def row_pairs(count, first):
    pairs = []
    for a in range(first, count, 2):
        b = (a + 1) % count
        pairs += [(a, b), (b, a)]
    return pairs


def body(density, value_field, potential, kern_rows, kern_cols):
    n_rows = lax.axis_size("rows")
    n_cols = lax.axis_size("cols")
    far_pairs = row_pairs(n_rows, 1)
    near_pairs = row_pairs(n_rows, 0)
    to_right = [(c, (c + 1) % n_cols) for c in range(n_cols)]
    to_left = [(c, (c - 1) % n_cols) for c in range(n_cols)]
    block = shape(ROWS, COLS)
    rows_table, turned_table, cols_table = tables(kern_rows, kern_cols)
    dens, value = density, value_field
    messages = call(prepare, MESSAGES, [], 2, dens, value)
    for step_index in range(STEPS):
        new, own_t, far_1, near_1, far_2, near_2 = messages
        far_1 = lax.ppermute(far_1, "rows", far_pairs)
        near_1 = lax.ppermute(near_1, "rows", near_pairs)
        far_2 = lax.ppermute(far_2, "rows", far_pairs)
        near_2 = lax.ppermute(near_2, "rows", near_pairs)
        left, right, seams, around, tall, mixed = call(
            edge_kernel,
            [shape(COL_ROWS, EDGE), shape(COL_ROWS, EDGE), shape(8, COLS), shape(8, COLS), shape(8, TALL), shape(ROWS, 2 * EDGE)],
            [pltpu.VMEM((8, COLS), F32), pltpu.VMEM((2 * KW, 2 * EDGE), F32)],
            1,
            dens, value, new, own_t, far_1, near_1, *rows_table,
        )
        right_in = lax.ppermute(left, "cols", to_left)
        left_in = lax.ppermute(right, "cols", to_right)
        cong, inner = call(
            middle_kernel,
            [block, block],
            [pltpu.VMEM((2 * KW, MID), F32), pltpu.VMEM((ROWS, MID), BF16), pltpu.VMEM((ROWS, MID), BF16)],
            3,
            new, value, potential, seams, around, far_2, near_2, *rows_table, *cols_table,
        )
        operands = (potential, new, seams, tall, left_in, right_in, mixed, cong, inner, *turned_table, *cols_table)
        if step_index < STEPS - 1:
            dens, value, *messages = call(
                finish_prepare_kernel, [block, block] + MESSAGES, FINISH_SCRATCH, 4, *operands
            )
        else:
            dens, value = call(finish_kernel, [block, block], FINISH_SCRATCH, 2, *operands)
    return dens, value


def solution(mesh):
    placed = (P("rows", "cols"), P("rows", "cols"), P("rows", "cols"), P(), P())
    return jax.shard_map(
        body,
        mesh=mesh,
        in_specs=placed,
        out_specs=(P("rows", "cols"), P("rows", "cols")),
        check_vma=False,
    )
```

```python
import functools

import jax
import jax.numpy as jnp
from jax import lax
from jax.experimental import pallas as pl
from jax.experimental.pallas import tpu as pltpu
from jax.sharding import PartitionSpec as P

STEPS = 2
EDGE_COST = 6
FIRST_MIB = 51
NU = 0.5
DT = 0.1

ROWS = 256
COLS = 1024
KW = 256
HALF = KW // 2
EDGE = 128
MID = COLS - 2 * EDGE
FROM_R = COLS - EDGE
RAW_AT = HALF
TURNED_AT = RAW_AT + 16
FIRST_ROWS = TURNED_AT + 8
TALL = 3 * ROWS
SEGMENTS = TALL // EDGE
COL_ROWS = ROWS + 4 * SEGMENTS

VMEM = pl.BlockSpec(memory_space=pltpu.VMEM)
HBM = pl.BlockSpec(memory_space=pltpu.HBM)
F32 = jnp.float32
BF16 = jnp.bfloat16


def shape(*dims, kind=F32):
    return jax.ShapeDtypeStruct(dims, kind)


def call(kernel, out_shapes, scratch, micros, *operands, hbm_in=(), hbm_out=(), aliases=None, mib=24):
    return pl.pallas_call(
        kernel,
        out_shape=out_shapes,
        in_specs=[HBM if n in hbm_in else VMEM for n in range(len(operands))],
        out_specs=[HBM if n in hbm_out else VMEM for n in range(len(out_shapes))],
        scratch_shapes=scratch,
        input_output_aliases=aliases or {},
        compiler_params=pltpu.CompilerParams(vmem_limit_bytes=mib * 1024 * 1024),
        cost_estimate=pl.CostEstimate(
            flops=int(micros * 10**9), bytes_accessed=int(micros * 3 * 10**6), transcendentals=0
        ),
    )(*operands)


def core_index():
    return lax.rem(lax.axis_index("rows"), 2)


def split(x):
    hi = x.astype(BF16)
    return hi, (x - hi.astype(F32)).astype(BF16)


def product(left, right):
    dot = functools.partial(jnp.dot, preferred_element_type=F32)
    return dot(left[0], right[0]) + (dot(left[1], right[0]) + dot(left[0], right[1]))


def put_split(refs, x):
    refs[0][...], refs[1][...] = split(x)


def band_tables(kern_rows, kern_cols, rows_hi, rows_lo, turned_hi, turned_lo, cols_hi, cols_lo):
    for kern, refs in ((kern_rows, (turned_hi, turned_lo)), (kern_cols, (cols_hi, cols_lo))):
        row = jnp.concatenate([jnp.zeros((1, 2 * KW), F32), kern[...]], axis=1)
        full = jnp.broadcast_to(row, (2 * KW, 3 * KW))
        table = pltpu.roll(full, 0, 1, stride=1, stride_axis=0)[:, :KW]
        put_split(refs, table)
        if kern is kern_rows:
            put_split((rows_hi, rows_lo), table.T)


TABLES = [shape(KW, 2 * KW, kind=BF16)] * 2 + [shape(2 * KW, KW, kind=BF16)] * 4


def flux(a, here, there):
    c = DT * NU
    a = DT * a
    return here * jnp.maximum(a + c, c) + there * jnp.minimum(a - c, -c)


def eight_rows(m, u):
    width = m.shape[1]
    flux_x = flux(u - pltpu.roll(u, 7, 0), m, pltpu.roll(m, 7, 0))
    flux_y = flux(u - pltpu.roll(u, width - 1, 1), m, pltpu.roll(m, width - 1, 1))
    return m - ((flux_x - pltpu.roll(flux_x, 1, 0)) + (flux_y - pltpu.roll(flux_y, 1, 1)))


def middle_density(dens, value, out):
    dims = (8, MID)
    sub = lax.broadcasted_iota(jnp.int32, dims, 0)
    top = sub == 0
    end = sub == 7
    own = slice(EDGE, FROM_R)

    def step(i, flux_before):
        rows = pl.ds(pl.multiple_of(8 * i, 8), 8)
        after = pl.ds(pl.multiple_of(jnp.minimum(8 * i + 8, ROWS - 8), 8), 8)
        m_all = dens[rows, :]
        u_all = value[rows, :]
        m = m_all[:, own]
        u = u_all[:, own]
        m_down = pltpu.roll(jnp.where(top, dens[after, own], m), 7, 0)
        u_down = pltpu.roll(jnp.where(top, value[after, own], u), 7, 0)
        flux_x = flux(u - u_down, m, m_down)
        flux_up = pltpu.roll(jnp.where(end, flux_before, flux_x), 1, 0)
        u_right = pltpu.roll(u_all, COLS - 1, 1)[:, 0:FROM_R]
        m_right = pltpu.roll(m_all, COLS - 1, 1)[:, 0:FROM_R]
        flux_y = flux(u_all[:, 0:FROM_R] - u_right, m_all[:, 0:FROM_R], m_right)
        flux_left = pltpu.roll(flux_y, 1, 1)[:, own]
        out[rows, :] = m - ((flux_x - flux_up) + (flux_y[:, own] - flux_left))
        return flux_x

    lax.fori_loop(0, ROWS // 8, step, jnp.zeros(dims, F32), unroll=4)


def inner_value(value, potential, out):
    dims = (8, COLS)
    sub = lax.broadcasted_iota(jnp.int32, dims, 0)
    top = sub == 0
    end = sub == 7

    def step(i, before):
        rows = pl.ds(pl.multiple_of(8 * i, 8), 8)
        after = pl.ds(pl.multiple_of(jnp.minimum(8 * i + 8, ROWS - 8), 8), 8)
        u = value[rows, :]
        down = pltpu.roll(jnp.where(top, value[after, :], u), 7, 0) - u
        up = pltpu.roll(jnp.where(end, before, down), 1, 0)
        right = pltpu.roll(u, COLS - 1, 1) - u
        left = pltpu.roll(right, 1, 1)
        out[rows, :] = value_formula(u, down, up, right, left, potential[rows, :])
        return down

    lax.fori_loop(0, ROWS // 8, step, jnp.zeros(dims, F32), unroll=4)


def end_rows(value, potential, around, out):
    sub = lax.broadcasted_iota(jnp.int32, (8, COLS), 0)
    for rows, at, halo in ((slice(0, 8), 0, 1), (slice(ROWS - 8, ROWS), 7, 6)):
        u = value[rows, :]
        there = around[halo : halo + 1, :]
        down = pltpu.roll(u, 7, 0)
        up = pltpu.roll(u, 1, 0)
        if at == 0:
            up = jnp.where(sub == 0, there, up)
        else:
            down = jnp.where(sub == 7, there, down)
        right = pltpu.roll(u, COLS - 1, 1) - u
        result = value_formula(u, down - u, u - up, right, pltpu.roll(right, 1, 1), potential[rows, :])
        out[rows.start + at : rows.start + at + 1, :] = result[at : at + 1, :]


def value_formula(u, down, up, right, left, cost):
    grad_sq = (
        jnp.square(jnp.maximum(up, 0.0))
        + jnp.square(jnp.minimum(down, 0.0))
        + jnp.square(jnp.maximum(left, 0.0))
        + jnp.square(jnp.minimum(right, 0.0))
    )
    lap = (down - up) + (right - left)
    return u + DT * (NU * lap - 0.5 * grad_sq + cost)


def side_density(dens, value, out):
    dims = (8, EDGE)
    sub = lax.broadcasted_iota(jnp.int32, dims, 0)
    lane = lax.broadcasted_iota(jnp.int32, dims, 1)
    top = sub == 0
    end = sub == 7
    blocks = [slice(at, at + EDGE) for at in (0, EDGE, FROM_R - EDGE, FROM_R)]

    def right(here, there):
        return jnp.where(lane == EDGE - 1, pltpu.roll(there, EDGE - 1, 1), pltpu.roll(here, EDGE - 1, 1))

    def left(here, there):
        return jnp.where(lane == 0, pltpu.roll(there, 1, 1), pltpu.roll(here, 1, 1))

    def step(i, carry):
        rows = pl.ds(pl.multiple_of(8 * i, 8), 8)
        after = pl.ds(pl.multiple_of(jnp.minimum(8 * i + 8, ROWS - 8), 8), 8)
        result = []
        for n, flux_before in zip((0, 3), carry):
            m = dens[rows, blocks[n]]
            u = value[rows, blocks[n]]
            m_down = pltpu.roll(jnp.where(top, dens[after, blocks[n]], m), 7, 0)
            u_down = pltpu.roll(jnp.where(top, value[after, blocks[n]], u), 7, 0)
            flux_x = flux(u - u_down, m, m_down)
            flux_up = pltpu.roll(jnp.where(end, flux_before, flux_x), 1, 0)
            if n == 0:
                flux_right = flux(u - right(u, value[rows, blocks[1]]), m, right(m, dens[rows, blocks[1]]))
                flux_left = pltpu.roll(flux_right, 1, 1)
            else:
                m_left = left(m, dens[rows, blocks[2]])
                flux_left = flux(left(u, value[rows, blocks[2]]) - u, m_left, m)
                flux_right = pltpu.roll(flux_left, EDGE - 1, 1)
            at = slice(0, EDGE) if n == 0 else slice(EDGE, 2 * EDGE)
            out[rows, at] = m - ((flux_x - flux_up) + (flux_right - flux_left))
            result.append(flux_x)
        return tuple(result)

    zeros = jnp.zeros(dims, F32)
    lax.fori_loop(0, ROWS // 8, step, (zeros, zeros), unroll=8)


def prepare_sides(dens, value, side, own_t, far, near):
    core = core_index()
    side_density(dens, value, side)
    for n, ref in enumerate((dens, value)):
        own_t[4 * n : 4 * n + 2, :] = ref[:, 0:EDGE].T[0:2, :]
        own_t[4 * n + 2 : 4 * n + 4, :] = ref[:, FROM_R:COLS].T[EDGE - 2 : EDGE, :]
    for one, bottom in ((far, core), (near, 1 - core)):
        one[0:HALF, :] = side[pl.ds(pl.multiple_of(bottom * HALF, 8), HALF), :]
        for n, ref in enumerate((dens, value)):
            eight = ref[pl.ds(pl.multiple_of(bottom * (ROWS - 8), 8), 8), :]
            pair = jnp.where(bottom == 1, eight[6:8, :], eight[0:2, :])
            for q in range(COLS // 256):
                at = RAW_AT + 4 * q + 2 * n
                one[at : at + 2, :] = pair[:, 256 * q : 256 * q + 256]
        one[TURNED_AT:FIRST_ROWS, :] = own_t[...]


def rest_kernel(dens, value, new, far, near):
    core = core_index()
    middle_density(dens, value, new)
    for two, bottom in ((far, core), (near, 1 - core)):
        two[...] = new[pl.ds(pl.multiple_of(bottom * HALF, 8), HALF), :]


FIRST = [
    shape(ROWS, 2 * EDGE),
    shape(8, ROWS),
    shape(FIRST_ROWS, 2 * EDGE),
    shape(FIRST_ROWS, 2 * EDGE),
]
SECOND = [shape(ROWS, MID), shape(HALF, MID), shape(HALF, MID)]
BLOCK = shape(ROWS, COLS)


def first_sides_kernel(dens_in, value_in, dens, value, side, own_t, far, near, semaphores):
    outer = []
    inner = []
    quarter = 2 * EDGE
    for q in (0, 3, 1, 2):
        lanes = slice(quarter * q, quarter * q + quarter)
        for source, target in ((dens_in, dens), (value_in, value)):
            copies = outer if q in (0, 3) else inner
            n = len(outer) + len(inner)
            copies.append(pltpu.make_async_copy(source.at[:, lanes], target.at[:, lanes], semaphores.at[n]))
    for copy in outer + inner:
        copy.start()
    for copy in outer + inner:
        copy.wait()
    prepare_sides(dens, value, side, own_t, far, near)


def turned_cost(potential, cost_t):
    cost_t[0:2, :] = potential[:, 0:EDGE].T[0:2, :]
    cost_t[2:4, :] = potential[:, FROM_R:COLS].T[EDGE - 2 : EDGE, :]


def first_rest_kernel(dens, value, kern_rows, kern_cols, new, far, near, *refs):
    copies = [
        pltpu.make_async_copy(source, target, refs[8].at[n])
        for n, (source, target) in enumerate(((kern_rows, refs[6]), (kern_cols, refs[7])))
    ]
    for copy in copies:
        copy.start()
    rest_kernel(dens, value, new, far, near)
    for copy in copies:
        copy.wait()
    band_tables(refs[6], refs[7], *refs[:6])


def halo_rows(ext, far, near):
    core = core_index()
    ext[pl.ds(pl.multiple_of(core * (HALF + ROWS), 8), HALF), :] = far
    ext[pl.ds(pl.multiple_of((1 - core) * (HALF + ROWS), 8), HALF), :] = near


def edge_kernel(
    dens, value, side, own_t, far, near, rows_hi, rows_lo,
    to_left, to_right, seams, around, tall, mixed, dens_8, ext,
):
    core = core_index()
    for ref, own, n in ((dens_8, dens, 0), (around, value, 1)):
        for q in range(COLS // 256):
            lanes = slice(256 * q, 256 * q + 256)
            at = RAW_AT + 4 * q + 2 * n
            f = far[at : at + 2, :]
            g = near[at : at + 2, :]
            ref[0:2, lanes] = jnp.where(core == 0, f, g)
            ref[6:8, lanes] = jnp.where(core == 0, g, f)
        ref[2:4, :] = own[0:2, :]
        ref[4:6, :] = own[ROWS - 2 : ROWS, :]
    seam = eight_rows(dens_8[...], around[...])
    seams[...] = seam
    f = far[TURNED_AT:FIRST_ROWS, :]
    g = near[TURNED_AT:FIRST_ROWS, :]
    tall[:, 0:ROWS] = jnp.where(core == 0, f, g)
    tall[:, ROWS : 2 * ROWS] = own_t[...]
    tall[:, 2 * ROWS : TALL] = jnp.where(core == 0, g, f)

    halo_rows(ext, far[0:HALF, :], near[0:HALF, :])
    ext[HALF : HALF + ROWS, :] = side[...]
    put_seams(ext, seams, ((slice(0, EDGE), slice(0, EDGE)), (slice(EDGE, 2 * EDGE), slice(FROM_R, COLS))))
    result = product((rows_hi[...], rows_lo[...]), split(ext[...]))
    mixed[...] = result
    for ref, lanes, at in ((to_left, slice(0, EDGE), 0), (to_right, slice(EDGE, 2 * EDGE), 2)):
        ref[0:ROWS, :] = result[:, lanes]
        for q in range(SEGMENTS):
            segment = slice(EDGE * q, EDGE * q + EDGE)
            ref[ROWS + 4 * q : ROWS + 4 * q + 2, :] = tall[at : at + 2, segment]
            ref[ROWS + 4 * q + 2 : ROWS + 4 * q + 4, :] = tall[at + 4 : at + 6, segment]


def put_seams(ext, seams, lane_pairs):
    for to, source in lane_pairs:
        ext[HALF - 1 : HALF, to] = seams[1:2, source]
        ext[HALF : HALF + 1, to] = seams[2:3, source]
        ext[HALF + ROWS - 1 : HALF + ROWS, to] = seams[5:6, source]
        ext[HALF + ROWS : HALF + ROWS + 1, to] = seams[6:7, source]


def middle_mix(
    new, seams, far, near, rows_hi, rows_lo, cols_hi, cols_lo, cong_s, cong_m, ext, mix_hi, mix_lo
):
    rows = (rows_hi[...], rows_lo[...])
    for b in range(MID // 256):
        lanes = slice(256 * b, 256 * b + 256)
        mix_hi[:, lanes], mix_lo[:, lanes] = split(product(rows, split(ext[:, lanes])))
    before = (cols_hi[0:KW, :], cols_lo[0:KW, :])
    after = (cols_hi[KW : 2 * KW, :], cols_lo[KW : 2 * KW, :])
    for b in range(COLS // 256):
        total = None
        for block, table in ((b - 1, before), (b, after)):
            if 0 <= block < MID // 256:
                lanes = slice(256 * block, 256 * block + 256)
                part = product((mix_hi[:, lanes], mix_lo[:, lanes]), table)
                total = part if total is None else total + part
        if b == 0:
            cong_s[:, 0:256] = total
        elif b == COLS // 256 - 1:
            cong_s[:, 256:512] = total
        else:
            cong_m[:, 256 * (b - 1) : 256 * b] = total


INSIDE = slice(2 * EDGE, COLS - 2 * EDGE)
INSIDE_N = COLS - 4 * EDGE


def middle_ext(new, seams, far, near, ext):
    halo_rows(ext, far[...], near[...])
    ext[HALF : HALF + ROWS, :] = new[...]
    put_seams(ext, seams, ((slice(0, MID), slice(EDGE, FROM_R)),))


def middle_kernel(*refs):
    new, seams, far, near = refs[:4]
    value, potential, around = refs[8:11]
    cong_s, inner, cost_t, dens_out, value_out, ext, mix_hi, mix_lo, cong_m = refs[11:]
    middle_ext(new, seams, far, near, ext)
    middle_mix(*refs[:8], cong_s, cong_m, ext, mix_hi, mix_lo)
    turned_cost(potential, cost_t)
    inner_value(value, potential, inner)
    end_rows(value, potential, around, inner)
    dens_out[:, EDGE:FROM_R] = ext[HALF : HALF + ROWS, :]
    value_out[:, INSIDE] = inner[:, INSIDE] + DT * cong_m[...]


def last_middle_kernel(*refs):
    new, seams, far, near = refs[:4]
    value, potential, around = refs[8:11]
    cong_s, inner, cost_t, dens_out, value_out, ext, mix_hi, mix_lo, cong_m, value_mid, semaphores = refs[11:]
    middle_ext(new, seams, far, near, ext)
    dens_copy = pltpu.make_async_copy(
        ext.at[HALF : HALF + ROWS, :], dens_out.at[:, EDGE:FROM_R], semaphores.at[0]
    )
    dens_copy.start()
    middle_mix(*refs[:8], cong_s, cong_m, ext, mix_hi, mix_lo)
    turned_cost(potential, cost_t)
    inner_value(value, potential, inner)
    end_rows(value, potential, around, inner)
    value_mid[...] = inner[:, INSIDE] + DT * cong_m[...]
    value_copy = pltpu.make_async_copy(value_mid, value_out.at[:, INSIDE], semaphores.at[1])
    value_copy.start()
    dens_copy.wait()
    value_copy.wait()


def finish(
    cost_t, side, seams, tall, left, right, mixed, cong, inner, turned_hi, turned_lo, cols_hi, cols_lo,
    put_dens, put_value, dens_t, value_t, turn,
):
    for ref, n in ((dens_t, 0), (value_t, 1)):
        for q in range(SEGMENTS):
            lanes = slice(EDGE * q, EDGE * q + EDGE)
            at = ROWS + 4 * q + 2 * n
            ref[0:2, lanes] = left[at : at + 2, :]
            ref[6:8, lanes] = right[at : at + 2, :]
        ref[2:6, :] = tall[4 * n : 4 * n + 4, :]
    u = value_t[...]
    new_t = eight_rows(dens_t[...], u)
    window = new_t[:, HALF : HALF + 2 * KW]
    window = jnp.concatenate([window, window], axis=0)
    turn[0:8, :] = product(split(window), (turned_hi[...], turned_lo[...]))[0:8, :]
    own = slice(ROWS, 2 * ROWS)
    turn[8:16, :] = new_t[:, own]
    right_t = pltpu.roll(u, 7, 0) - u
    left_t = u - pltpu.roll(u, 1, 0)
    down_t = pltpu.roll(u, TALL - 1, 1) - u
    up_t = u - pltpu.roll(u, 1, 1)
    cost = jnp.concatenate([cost_t[0:2, :], cost_t[0:4, :], cost_t[2:4, :]], axis=0)
    turn[16:24, :] = value_formula(
        u[:, own], down_t[:, own], up_t[:, own], right_t[:, own], left_t[:, own], cost
    )
    columns = turn[...].T

    def column(n):
        return columns[:, n : n + 1]

    lane = lax.broadcasted_iota(jnp.int32, (ROWS, 2 * EDGE), 1)
    before = (cols_hi[0:KW, :], cols_lo[0:KW, :])
    after = (cols_hi[KW : 2 * KW, :], cols_lo[KW : 2 * KW, :])
    low = jnp.concatenate([left[0:ROWS, :], mixed[:, 0:EDGE]], axis=1)
    low = jnp.where(lane == EDGE - 1, column(1), jnp.where(lane == EDGE, column(2), low))
    low = cong[:, 0:256] + product(split(low), before)
    high = jnp.concatenate([mixed[:, EDGE : 2 * EDGE], right[0:ROWS, :]], axis=1)
    high = jnp.where(lane == EDGE - 1, column(5), jnp.where(lane == EDGE, column(6), high))
    high = cong[:, 256:512] + product(split(high), after)

    lane = lax.broadcasted_iota(jnp.int32, (ROWS, EDGE), 1)
    row = lax.broadcasted_iota(jnp.int32, (ROWS, EDGE), 0)
    put_value(1, inner[:, EDGE : 2 * EDGE] + DT * low[:, EDGE : 2 * EDGE])
    put_value(2, inner[:, FROM_R - EDGE : FROM_R] + DT * high[:, 0:EDGE])
    put_value(0, jnp.where(lane == 0, column(18), inner[:, 0:EDGE]) + DT * low[:, 0:EDGE])
    put_value(
        3, jnp.where(lane == EDGE - 1, column(21), inner[:, FROM_R:COLS]) + DT * high[:, EDGE : 2 * EDGE]
    )
    for block, lanes, from_side, at, n in (
        (0, slice(0, EDGE), slice(0, EDGE), 0, 10),
        (3, slice(FROM_R, COLS), slice(EDGE, 2 * EDGE), EDGE - 1, 13),
    ):
        x = jnp.where(row == 0, seams[2:3, lanes], side[:, from_side])
        x = jnp.where(row == ROWS - 1, seams[5:6, lanes], x)
        put_dens(block, jnp.where(lane == at, column(n), x))


FINISH_SCRATCH = [
    pltpu.VMEM((8, TALL), F32),
    pltpu.VMEM((8, TALL), F32),
    pltpu.VMEM((128, ROWS), F32),
]


def next_sides_kernel(*refs):
    dens, value = refs[15:17]
    starts = (0, EDGE, FROM_R - EDGE, FROM_R)

    def put(ref):
        def store(block, x):
            ref[:, starts[block] : starts[block] + EDGE] = x

        return store

    finish(*refs[:13], put(dens), put(value), *refs[21:])
    prepare_sides(dens, value, *refs[17:21])


def last_sides_kernel(*refs):
    dens_out, value_out = refs[15:17]
    dens_s, value_s, dens_t, value_t, turn, semaphores = refs[17:]
    starts = (0, EDGE, FROM_R - EDGE, FROM_R)
    copies = []

    def put(sides, out):
        def store(block, x):
            lanes = slice(EDGE * block, EDGE * block + EDGE)
            sides[:, lanes] = x
            target = out.at[:, starts[block] : starts[block] + EDGE]
            copy = pltpu.make_async_copy(sides.at[:, lanes], target, semaphores.at[len(copies)])
            copy.start()
            copies.append(copy)

        return store

    finish(*refs[:13], put(dens_s, dens_out), put(value_s, value_out), dens_t, value_t, turn)
    for copy in copies:
        copy.wait()


def row_pairs(count, first):
    pairs = []
    for a in range(first, count, 2):
        b = (a + 1) % count
        pairs += [(a, b), (b, a)]
    return pairs


def body(density, value_field, potential, kern_rows, kern_cols):
    n_rows = lax.axis_size("rows")
    n_cols = lax.axis_size("cols")
    far_pairs = row_pairs(n_rows, 1)
    near_pairs = row_pairs(n_rows, 0)
    to_right = [(c, (c + 1) % n_cols) for c in range(n_cols)]
    to_left = [(c, (c - 1) % n_cols) for c in range(n_cols)]
    dens, value, side, own_t, far_1, near_1 = call(
        first_sides_kernel,
        [BLOCK, BLOCK] + FIRST,
        [pltpu.SemaphoreType.DMA((8,))],
        1,
        density, value_field,
        hbm_in=(0, 1),
        mib=FIRST_MIB,
    )
    for step_index in range(STEPS):
        last = step_index == STEPS - 1
        if step_index == 0:
            new, far_2, near_2, *table = call(
                first_rest_kernel,
                SECOND + TABLES,
                [pltpu.VMEM((1, KW), F32), pltpu.VMEM((1, KW), F32), pltpu.SemaphoreType.DMA((2,))],
                1,
                dens, value, kern_rows[None], kern_cols[None],
                hbm_in=(2, 3),
            )
            rows_table, turned_table, cols_table = table[0:2], table[2:4], table[4:6]
        else:
            new, far_2, near_2 = call(rest_kernel, SECOND, [], 1, dens, value)
        far_1 = lax.ppermute(far_1, "rows", far_pairs)
        near_1 = lax.ppermute(near_1, "rows", near_pairs)
        far_2 = lax.ppermute(far_2, "rows", far_pairs)
        near_2 = lax.ppermute(near_2, "rows", near_pairs)
        left, right, seams, around, tall, mixed = call(
            edge_kernel,
            [shape(COL_ROWS, EDGE), shape(COL_ROWS, EDGE), shape(8, COLS), shape(8, COLS), shape(8, TALL), shape(ROWS, 2 * EDGE)],
            [pltpu.VMEM((8, COLS), F32), pltpu.VMEM((2 * KW, 2 * EDGE), F32)],
            EDGE_COST,
            dens, value, side, own_t, far_1, near_1, *rows_table,
        )
        right_in = lax.ppermute(left, "cols", to_left)
        left_in = lax.ppermute(right, "cols", to_right)
        scratch = [
            pltpu.VMEM((2 * KW, MID), F32),
            pltpu.VMEM((ROWS, MID), BF16),
            pltpu.VMEM((ROWS, MID), BF16),
            pltpu.VMEM((ROWS, INSIDE_N), F32),
        ]
        if last:
            scratch += [pltpu.VMEM((ROWS, INSIDE_N), F32), pltpu.SemaphoreType.DMA((2,))]
        cong, inner, cost_t, *results = call(
            last_middle_kernel if last else middle_kernel,
            [shape(ROWS, 4 * EDGE), BLOCK, shape(8, ROWS), BLOCK, BLOCK],
            scratch,
            3,
            new, seams, far_2, near_2, *rows_table, *cols_table, value, potential, around,
            hbm_out=(3, 4) if last else (),
        )
        operands = (cost_t, side, seams, tall, left_in, right_in, mixed, cong, inner, *turned_table, *cols_table, *results)
        if last:
            scratch = [pltpu.VMEM((ROWS, 4 * EDGE), F32), pltpu.VMEM((ROWS, 4 * EDGE), F32)]
            return tuple(
                call(
                    last_sides_kernel,
                    [BLOCK, BLOCK],
                    scratch + FINISH_SCRATCH + [pltpu.SemaphoreType.DMA((6,))],
                    1,
                    *operands,
                    hbm_in=(13, 14),
                    hbm_out=(0, 1),
                    aliases={13: 0, 14: 1},
                )
            )
        dens, value, side, own_t, far_1, near_1 = call(
            next_sides_kernel, [BLOCK, BLOCK] + FIRST, FINISH_SCRATCH, 1, *operands, aliases={13: 0, 14: 1}
        )


def solution(mesh):
    placed = (P("rows", "cols"), P("rows", "cols"), P("rows", "cols"), P(), P())
    return jax.shard_map(
        body,
        mesh=mesh,
        in_specs=placed,
        out_specs=(P("rows", "cols"), P("rows", "cols")),
        check_vma=False,
    )
```

```python
import functools

import jax
import jax.numpy as jnp
from jax import lax
from jax.experimental import pallas as pl
from jax.experimental.pallas import tpu as pltpu
from jax.sharding import PartitionSpec as P

STEPS = 2
EDGE_COST = 6
FIRST_MIB = 51
NU = 0.5
DT = 0.1

ROWS = 256
COLS = 1024
KW = 256
HALF = KW // 2
EDGE = 128
MID = COLS - 2 * EDGE
FROM_R = COLS - EDGE
RAW_AT = HALF
TURNED_AT = RAW_AT + 16
FIRST_ROWS = TURNED_AT + 8
TALL = 3 * ROWS
SEGMENTS = TALL // EDGE
COL_ROWS = ROWS + 4 * SEGMENTS

VMEM = pl.BlockSpec(memory_space=pltpu.VMEM)
HBM = pl.BlockSpec(memory_space=pltpu.HBM)
F32 = jnp.float32
BF16 = jnp.bfloat16


def shape(*dims, kind=F32):
    return jax.ShapeDtypeStruct(dims, kind)


def call(kernel, out_shapes, scratch, micros, *operands, hbm_in=(), hbm_out=(), aliases=None, mib=24):
    return pl.pallas_call(
        kernel,
        out_shape=out_shapes,
        in_specs=[HBM if n in hbm_in else VMEM for n in range(len(operands))],
        out_specs=[HBM if n in hbm_out else VMEM for n in range(len(out_shapes))],
        scratch_shapes=scratch,
        input_output_aliases=aliases or {},
        compiler_params=pltpu.CompilerParams(vmem_limit_bytes=mib * 1024 * 1024),
        cost_estimate=pl.CostEstimate(
            flops=int(micros * 10**9), bytes_accessed=int(micros * 3 * 10**6), transcendentals=0
        ),
    )(*operands)


def core_index():
    return lax.rem(lax.axis_index("rows"), 2)


def split(x):
    hi = x.astype(BF16)
    return hi, (x - hi.astype(F32)).astype(BF16)


def product(left, right):
    dot = functools.partial(jnp.dot, preferred_element_type=F32)
    return dot(left[0], right[0]) + (dot(left[1], right[0]) + dot(left[0], right[1]))


def put_split(refs, x):
    refs[0][...], refs[1][...] = split(x)


def band_tables(kern_rows, kern_cols, rows_hi, rows_lo, turned_hi, turned_lo, cols_hi, cols_lo):
    for kern, refs in ((kern_rows, (turned_hi, turned_lo)), (kern_cols, (cols_hi, cols_lo))):
        row = jnp.concatenate([jnp.zeros((1, 2 * KW), F32), kern[...]], axis=1)
        full = jnp.broadcast_to(row, (2 * KW, 3 * KW))
        table = pltpu.roll(full, 0, 1, stride=1, stride_axis=0)[:, :KW]
        put_split(refs, table)
        if kern is kern_rows:
            put_split((rows_hi, rows_lo), table.T)


TABLES = [shape(KW, 2 * KW, kind=BF16)] * 2 + [shape(2 * KW, KW, kind=BF16)] * 4


def flux(a, here, there):
    c = DT * NU
    a = DT * a
    return here * jnp.maximum(a + c, c) + there * jnp.minimum(a - c, -c)


def eight_rows(m, u):
    width = m.shape[1]
    flux_x = flux(u - pltpu.roll(u, 7, 0), m, pltpu.roll(m, 7, 0))
    flux_y = flux(u - pltpu.roll(u, width - 1, 1), m, pltpu.roll(m, width - 1, 1))
    return m - ((flux_x - pltpu.roll(flux_x, 1, 0)) + (flux_y - pltpu.roll(flux_y, 1, 1)))


def middle_density(dens, value, out):
    own = slice(EDGE, FROM_R)
    tall = 64

    def step(i, flux_before):
        rows = pl.ds(pl.multiple_of(tall * i, tall), tall)
        after = pl.ds(pl.multiple_of(jnp.minimum(tall * i + tall, ROWS - 8), 8), 8)
        m_all = dens[rows, :]
        u_all = value[rows, :]
        m = m_all[:, own]
        u = u_all[:, own]
        m_down = jnp.concatenate([m[1:], dens[after, own][0:1]], axis=0)
        u_down = jnp.concatenate([u[1:], value[after, own][0:1]], axis=0)
        flux_x = flux(u - u_down, m, m_down)
        flux_up = jnp.concatenate([flux_before, flux_x[:-1]], axis=0)
        u_right = pltpu.roll(u_all, COLS - 1, 1)[:, 0:FROM_R]
        m_right = pltpu.roll(m_all, COLS - 1, 1)[:, 0:FROM_R]
        flux_y = flux(u_all[:, 0:FROM_R] - u_right, m_all[:, 0:FROM_R], m_right)
        flux_left = pltpu.roll(flux_y, 1, 1)[:, own]
        out[rows, :] = m - ((flux_x - flux_up) + (flux_y[:, own] - flux_left))
        return flux_x[-1:]

    lax.fori_loop(0, ROWS // tall, step, jnp.zeros((1, MID), F32))


def inner_value(value, potential, out):
    tall = 32

    def step(i, before):
        rows = pl.ds(pl.multiple_of(tall * i, tall), tall)
        after = pl.ds(pl.multiple_of(jnp.minimum(tall * i + tall, ROWS - 8), 8), 8)
        u = value[rows, :]
        down = jnp.concatenate([u[1:], value[after, :][0:1]], axis=0) - u
        up = jnp.concatenate([before, down[:-1]], axis=0)
        right = pltpu.roll(u, COLS - 1, 1) - u
        left = pltpu.roll(right, 1, 1)
        out[rows, :] = value_formula(u, down, up, right, left, potential[rows, :])
        return down[-1:]

    lax.fori_loop(0, ROWS // tall, step, jnp.zeros((1, COLS), F32), unroll=4)


def end_rows(value, potential, around, out):
    sub = lax.broadcasted_iota(jnp.int32, (8, COLS), 0)
    for rows, at, halo in ((slice(0, 8), 0, 1), (slice(ROWS - 8, ROWS), 7, 6)):
        u = value[rows, :]
        there = around[halo : halo + 1, :]
        down = pltpu.roll(u, 7, 0)
        up = pltpu.roll(u, 1, 0)
        if at == 0:
            up = jnp.where(sub == 0, there, up)
        else:
            down = jnp.where(sub == 7, there, down)
        right = pltpu.roll(u, COLS - 1, 1) - u
        result = value_formula(u, down - u, u - up, right, pltpu.roll(right, 1, 1), potential[rows, :])
        out[rows.start + at : rows.start + at + 1, :] = result[at : at + 1, :]


def value_formula(u, down, up, right, left, cost):
    grad_sq = (
        jnp.square(jnp.maximum(up, 0.0))
        + jnp.square(jnp.minimum(down, 0.0))
        + jnp.square(jnp.maximum(left, 0.0))
        + jnp.square(jnp.minimum(right, 0.0))
    )
    lap = (down - up) + (right - left)
    return u + DT * (NU * lap - 0.5 * grad_sq + cost)


def side_density(dens, value, out):
    lane = lax.broadcasted_iota(jnp.int32, (ROWS, EDGE), 1)
    blocks = [slice(at, at + EDGE) for at in (0, EDGE, FROM_R - EDGE, FROM_R)]

    def right(ref, here):
        there = pltpu.roll(ref[:, blocks[1]], EDGE - 1, 1)
        return jnp.where(lane == EDGE - 1, there, pltpu.roll(here, EDGE - 1, 1))

    def left(ref, here):
        there = pltpu.roll(ref[:, blocks[2]], 1, 1)
        return jnp.where(lane == 0, there, pltpu.roll(here, 1, 1))

    for n in (0, 3):
        m = dens[:, blocks[n]]
        u = value[:, blocks[n]]
        flux_x = flux(u - pltpu.roll(u, ROWS - 1, 0), m, pltpu.roll(m, ROWS - 1, 0))
        flux_up = pltpu.roll(flux_x, 1, 0)
        if n == 0:
            flux_right = flux(u - right(value, u), m, right(dens, m))
            flux_left = pltpu.roll(flux_right, 1, 1)
        else:
            flux_left = flux(left(value, u) - u, left(dens, m), m)
            flux_right = pltpu.roll(flux_left, EDGE - 1, 1)
        at = slice(0, EDGE) if n == 0 else slice(EDGE, 2 * EDGE)
        out[:, at] = m - ((flux_x - flux_up) + (flux_right - flux_left))


def prepare_sides(dens, value, side, own_t, far, near, wait_middle=None):
    core = core_index()
    side_density(dens, value, side)
    if wait_middle is not None:
        wait_middle()
    for n, ref in enumerate((dens, value)):
        own_t[4 * n : 4 * n + 2, :] = ref[:, 0:EDGE].T[0:2, :]
        own_t[4 * n + 2 : 4 * n + 4, :] = ref[:, FROM_R:COLS].T[EDGE - 2 : EDGE, :]
    for one, bottom in ((far, core), (near, 1 - core)):
        one[0:HALF, :] = side[pl.ds(pl.multiple_of(bottom * HALF, 8), HALF), :]
        for n, ref in enumerate((dens, value)):
            eight = ref[pl.ds(pl.multiple_of(bottom * (ROWS - 8), 8), 8), :]
            pair = jnp.where(bottom == 1, eight[6:8, :], eight[0:2, :])
            for q in range(COLS // 256):
                at = RAW_AT + 4 * q + 2 * n
                one[at : at + 2, :] = pair[:, 256 * q : 256 * q + 256]
        one[TURNED_AT:FIRST_ROWS, :] = own_t[...]


def rest_kernel(dens, value, new, far, near):
    core = core_index()
    middle_density(dens, value, new)
    for two, bottom in ((far, core), (near, 1 - core)):
        two[...] = new[pl.ds(pl.multiple_of(bottom * HALF, 8), HALF), :]


FIRST = [
    shape(ROWS, 2 * EDGE),
    shape(8, ROWS),
    shape(FIRST_ROWS, 2 * EDGE),
    shape(FIRST_ROWS, 2 * EDGE),
]
SECOND = [shape(ROWS, MID), shape(HALF, MID), shape(HALF, MID)]
BLOCK = shape(ROWS, COLS)


def first_sides_kernel(dens_in, value_in, dens, value, side, own_t, far, near, semaphores):
    outer = []
    inner = []
    quarter = 2 * EDGE
    for q in (0, 3, 1, 2):
        lanes = slice(quarter * q, quarter * q + quarter)
        for source, target in ((dens_in, dens), (value_in, value)):
            copies = outer if q in (0, 3) else inner
            n = len(outer) + len(inner)
            copies.append(pltpu.make_async_copy(source.at[:, lanes], target.at[:, lanes], semaphores.at[n]))
    for copy in outer + inner:
        copy.start()
    for copy in outer:
        copy.wait()

    def wait_middle():
        for copy in inner:
            copy.wait()

    prepare_sides(dens, value, side, own_t, far, near, wait_middle)


def turned_cost(potential, cost_t):
    cost_t[0:2, :] = potential[:, 0:EDGE].T[0:2, :]
    cost_t[2:4, :] = potential[:, FROM_R:COLS].T[EDGE - 2 : EDGE, :]


def first_rest_kernel(dens, value, kern_rows, kern_cols, new, far, near, *refs):
    copies = [
        pltpu.make_async_copy(source, target, refs[8].at[n])
        for n, (source, target) in enumerate(((kern_rows, refs[6]), (kern_cols, refs[7])))
    ]
    for copy in copies:
        copy.start()
    rest_kernel(dens, value, new, far, near)
    for copy in copies:
        copy.wait()
    band_tables(refs[6], refs[7], *refs[:6])


def halo_rows(ext, far, near):
    core = core_index()
    ext[pl.ds(pl.multiple_of(core * (HALF + ROWS), 8), HALF), :] = far
    ext[pl.ds(pl.multiple_of((1 - core) * (HALF + ROWS), 8), HALF), :] = near


def edge_kernel(
    dens, value, side, own_t, far, near, rows_hi, rows_lo,
    to_left, to_right, seams, around, tall, mixed, dens_8, ext,
):
    core = core_index()
    for ref, own, n in ((dens_8, dens, 0), (around, value, 1)):
        for q in range(COLS // 256):
            lanes = slice(256 * q, 256 * q + 256)
            at = RAW_AT + 4 * q + 2 * n
            f = far[at : at + 2, :]
            g = near[at : at + 2, :]
            ref[0:2, lanes] = jnp.where(core == 0, f, g)
            ref[6:8, lanes] = jnp.where(core == 0, g, f)
        ref[2:4, :] = own[0:2, :]
        ref[4:6, :] = own[ROWS - 2 : ROWS, :]
    seam = eight_rows(dens_8[...], around[...])
    seams[...] = seam
    f = far[TURNED_AT:FIRST_ROWS, :]
    g = near[TURNED_AT:FIRST_ROWS, :]
    tall[:, 0:ROWS] = jnp.where(core == 0, f, g)
    tall[:, ROWS : 2 * ROWS] = own_t[...]
    tall[:, 2 * ROWS : TALL] = jnp.where(core == 0, g, f)

    halo_rows(ext, far[0:HALF, :], near[0:HALF, :])
    ext[HALF : HALF + ROWS, :] = side[...]
    put_seams(ext, seams, ((slice(0, EDGE), slice(0, EDGE)), (slice(EDGE, 2 * EDGE), slice(FROM_R, COLS))))
    result = product((rows_hi[...], rows_lo[...]), split(ext[...]))
    mixed[...] = result
    for ref, lanes, at in ((to_left, slice(0, EDGE), 0), (to_right, slice(EDGE, 2 * EDGE), 2)):
        ref[0:ROWS, :] = result[:, lanes]
        for q in range(SEGMENTS):
            segment = slice(EDGE * q, EDGE * q + EDGE)
            ref[ROWS + 4 * q : ROWS + 4 * q + 2, :] = tall[at : at + 2, segment]
            ref[ROWS + 4 * q + 2 : ROWS + 4 * q + 4, :] = tall[at + 4 : at + 6, segment]


def put_seams(ext, seams, lane_pairs):
    for to, source in lane_pairs:
        ext[HALF - 1 : HALF, to] = seams[1:2, source]
        ext[HALF : HALF + 1, to] = seams[2:3, source]
        ext[HALF + ROWS - 1 : HALF + ROWS, to] = seams[5:6, source]
        ext[HALF + ROWS : HALF + ROWS + 1, to] = seams[6:7, source]


def middle_mix(
    new, seams, far, near, rows_hi, rows_lo, cols_hi, cols_lo, cong_s, cong_m, ext, mix_hi, mix_lo
):
    rows = (rows_hi[...], rows_lo[...])
    for b in range(MID // 256):
        lanes = slice(256 * b, 256 * b + 256)
        mix_hi[:, lanes], mix_lo[:, lanes] = split(product(rows, split(ext[:, lanes])))
    before = (cols_hi[0:KW, :], cols_lo[0:KW, :])
    after = (cols_hi[KW : 2 * KW, :], cols_lo[KW : 2 * KW, :])
    for b in range(COLS // 256):
        total = None
        for block, table in ((b - 1, before), (b, after)):
            if 0 <= block < MID // 256:
                lanes = slice(256 * block, 256 * block + 256)
                part = product((mix_hi[:, lanes], mix_lo[:, lanes]), table)
                total = part if total is None else total + part
        if b == 0:
            cong_s[:, 0:256] = total
        elif b == COLS // 256 - 1:
            cong_s[:, 256:512] = total
        else:
            cong_m[:, 256 * (b - 1) : 256 * b] = total


INSIDE = slice(2 * EDGE, COLS - 2 * EDGE)
INSIDE_N = COLS - 4 * EDGE


def middle_ext(new, seams, far, near, ext):
    halo_rows(ext, far[...], near[...])
    ext[HALF : HALF + ROWS, :] = new[...]
    put_seams(ext, seams, ((slice(0, MID), slice(EDGE, FROM_R)),))


def middle_kernel(*refs):
    new, seams, far, near = refs[:4]
    value, potential, around = refs[8:11]
    cong_s, inner, cost_t, dens_out, value_out, ext, mix_hi, mix_lo, cong_m = refs[11:]
    middle_ext(new, seams, far, near, ext)
    middle_mix(*refs[:8], cong_s, cong_m, ext, mix_hi, mix_lo)
    turned_cost(potential, cost_t)
    inner_value(value, potential, inner)
    end_rows(value, potential, around, inner)
    dens_out[:, EDGE:FROM_R] = ext[HALF : HALF + ROWS, :]
    value_out[:, INSIDE] = inner[:, INSIDE] + DT * cong_m[...]


def last_middle_kernel(*refs):
    new, seams, far, near = refs[:4]
    value, potential, around = refs[8:11]
    cong_s, inner, cost_t, dens_out, value_out, ext, mix_hi, mix_lo, cong_m, value_mid, semaphores = refs[11:]
    middle_ext(new, seams, far, near, ext)
    dens_copy = pltpu.make_async_copy(
        ext.at[HALF : HALF + ROWS, :], dens_out.at[:, EDGE:FROM_R], semaphores.at[0]
    )
    dens_copy.start()
    middle_mix(*refs[:8], cong_s, cong_m, ext, mix_hi, mix_lo)
    turned_cost(potential, cost_t)
    inner_value(value, potential, inner)
    end_rows(value, potential, around, inner)
    value_mid[...] = inner[:, INSIDE] + DT * cong_m[...]
    value_copy = pltpu.make_async_copy(value_mid, value_out.at[:, INSIDE], semaphores.at[1])
    value_copy.start()
    dens_copy.wait()
    value_copy.wait()


def finish(
    cost_t, side, seams, tall, left, right, mixed, cong, inner, turned_hi, turned_lo, cols_hi, cols_lo,
    put_dens, put_value, dens_t, value_t, turn,
):
    for ref, n in ((dens_t, 0), (value_t, 1)):
        for q in range(SEGMENTS):
            lanes = slice(EDGE * q, EDGE * q + EDGE)
            at = ROWS + 4 * q + 2 * n
            ref[0:2, lanes] = left[at : at + 2, :]
            ref[6:8, lanes] = right[at : at + 2, :]
        ref[2:6, :] = tall[4 * n : 4 * n + 4, :]
    u = value_t[...]
    new_t = eight_rows(dens_t[...], u)
    window = new_t[:, HALF : HALF + 2 * KW]
    window = jnp.concatenate([window, window], axis=0)
    turn[0:8, :] = product(split(window), (turned_hi[...], turned_lo[...]))[0:8, :]
    own = slice(ROWS, 2 * ROWS)
    turn[8:16, :] = new_t[:, own]
    right_t = pltpu.roll(u, 7, 0) - u
    left_t = u - pltpu.roll(u, 1, 0)
    down_t = pltpu.roll(u, TALL - 1, 1) - u
    up_t = u - pltpu.roll(u, 1, 1)
    cost = jnp.concatenate([cost_t[0:2, :], cost_t[0:4, :], cost_t[2:4, :]], axis=0)
    turn[16:24, :] = value_formula(
        u[:, own], down_t[:, own], up_t[:, own], right_t[:, own], left_t[:, own], cost
    )
    columns = turn[...].T

    def column(n):
        return columns[:, n : n + 1]

    lane = lax.broadcasted_iota(jnp.int32, (ROWS, 2 * EDGE), 1)
    before = (cols_hi[0:KW, :], cols_lo[0:KW, :])
    after = (cols_hi[KW : 2 * KW, :], cols_lo[KW : 2 * KW, :])
    low = jnp.concatenate([left[0:ROWS, :], mixed[:, 0:EDGE]], axis=1)
    low = jnp.where(lane == EDGE - 1, column(1), jnp.where(lane == EDGE, column(2), low))
    low = cong[:, 0:256] + product(split(low), before)
    high = jnp.concatenate([mixed[:, EDGE : 2 * EDGE], right[0:ROWS, :]], axis=1)
    high = jnp.where(lane == EDGE - 1, column(5), jnp.where(lane == EDGE, column(6), high))
    high = cong[:, 256:512] + product(split(high), after)

    lane = lax.broadcasted_iota(jnp.int32, (ROWS, EDGE), 1)
    row = lax.broadcasted_iota(jnp.int32, (ROWS, EDGE), 0)
    put_value(1, inner[:, EDGE : 2 * EDGE] + DT * low[:, EDGE : 2 * EDGE])
    put_value(2, inner[:, FROM_R - EDGE : FROM_R] + DT * high[:, 0:EDGE])
    put_value(0, jnp.where(lane == 0, column(18), inner[:, 0:EDGE]) + DT * low[:, 0:EDGE])
    put_value(
        3, jnp.where(lane == EDGE - 1, column(21), inner[:, FROM_R:COLS]) + DT * high[:, EDGE : 2 * EDGE]
    )
    for block, lanes, from_side, at, n in (
        (0, slice(0, EDGE), slice(0, EDGE), 0, 10),
        (3, slice(FROM_R, COLS), slice(EDGE, 2 * EDGE), EDGE - 1, 13),
    ):
        x = jnp.where(row == 0, seams[2:3, lanes], side[:, from_side])
        x = jnp.where(row == ROWS - 1, seams[5:6, lanes], x)
        put_dens(block, jnp.where(lane == at, column(n), x))


FINISH_SCRATCH = [
    pltpu.VMEM((8, TALL), F32),
    pltpu.VMEM((8, TALL), F32),
    pltpu.VMEM((128, ROWS), F32),
]


def next_sides_kernel(*refs):
    dens, value = refs[15:17]
    starts = (0, EDGE, FROM_R - EDGE, FROM_R)

    def put(ref):
        def store(block, x):
            ref[:, starts[block] : starts[block] + EDGE] = x

        return store

    finish(*refs[:13], put(dens), put(value), *refs[21:])
    prepare_sides(dens, value, *refs[17:21])


def last_sides_kernel(*refs):
    dens_out, value_out = refs[15:17]
    dens_s, value_s, dens_t, value_t, turn, semaphores = refs[17:]
    starts = (0, EDGE, FROM_R - EDGE, FROM_R)
    copies = []

    def put(sides, out):
        def store(block, x):
            lanes = slice(EDGE * block, EDGE * block + EDGE)
            sides[:, lanes] = x
            target = out.at[:, starts[block] : starts[block] + EDGE]
            copy = pltpu.make_async_copy(sides.at[:, lanes], target, semaphores.at[len(copies)])
            copy.start()
            copies.append(copy)

        return store

    finish(*refs[:13], put(dens_s, dens_out), put(value_s, value_out), dens_t, value_t, turn)
    for copy in copies:
        copy.wait()


def row_pairs(count, first):
    pairs = []
    for a in range(first, count, 2):
        b = (a + 1) % count
        pairs += [(a, b), (b, a)]
    return pairs


def body(density, value_field, potential, kern_rows, kern_cols):
    n_rows = lax.axis_size("rows")
    n_cols = lax.axis_size("cols")
    far_pairs = row_pairs(n_rows, 1)
    near_pairs = row_pairs(n_rows, 0)
    to_right = [(c, (c + 1) % n_cols) for c in range(n_cols)]
    to_left = [(c, (c - 1) % n_cols) for c in range(n_cols)]
    dens, value, side, own_t, far_1, near_1 = call(
        first_sides_kernel,
        [BLOCK, BLOCK] + FIRST,
        [pltpu.SemaphoreType.DMA((8,))],
        1,
        density, value_field,
        hbm_in=(0, 1),
        mib=FIRST_MIB,
    )
    for step_index in range(STEPS):
        last = step_index == STEPS - 1
        if step_index == 0:
            new, far_2, near_2, *table = call(
                first_rest_kernel,
                SECOND + TABLES,
                [pltpu.VMEM((1, KW), F32), pltpu.VMEM((1, KW), F32), pltpu.SemaphoreType.DMA((2,))],
                1,
                dens, value, kern_rows[None], kern_cols[None],
                hbm_in=(2, 3),
            )
            rows_table, turned_table, cols_table = table[0:2], table[2:4], table[4:6]
        else:
            new, far_2, near_2 = call(rest_kernel, SECOND, [], 1, dens, value)
        far_1 = lax.ppermute(far_1, "rows", far_pairs)
        near_1 = lax.ppermute(near_1, "rows", near_pairs)
        far_2 = lax.ppermute(far_2, "rows", far_pairs)
        near_2 = lax.ppermute(near_2, "rows", near_pairs)
        left, right, seams, around, tall, mixed = call(
            edge_kernel,
            [shape(COL_ROWS, EDGE), shape(COL_ROWS, EDGE), shape(8, COLS), shape(8, COLS), shape(8, TALL), shape(ROWS, 2 * EDGE)],
            [pltpu.VMEM((8, COLS), F32), pltpu.VMEM((2 * KW, 2 * EDGE), F32)],
            EDGE_COST,
            dens, value, side, own_t, far_1, near_1, *rows_table,
        )
        right_in = lax.ppermute(left, "cols", to_left)
        left_in = lax.ppermute(right, "cols", to_right)
        scratch = [
            pltpu.VMEM((2 * KW, MID), F32),
            pltpu.VMEM((ROWS, MID), BF16),
            pltpu.VMEM((ROWS, MID), BF16),
            pltpu.VMEM((ROWS, INSIDE_N), F32),
        ]
        if last:
            scratch += [pltpu.VMEM((ROWS, INSIDE_N), F32), pltpu.SemaphoreType.DMA((2,))]
        cong, inner, cost_t, *results = call(
            last_middle_kernel if last else middle_kernel,
            [shape(ROWS, 4 * EDGE), BLOCK, shape(8, ROWS), BLOCK, BLOCK],
            scratch,
            3,
            new, seams, far_2, near_2, *rows_table, *cols_table, value, potential, around,
            hbm_out=(3, 4) if last else (),
        )
        operands = (cost_t, side, seams, tall, left_in, right_in, mixed, cong, inner, *turned_table, *cols_table, *results)
        if last:
            scratch = [pltpu.VMEM((ROWS, 4 * EDGE), F32), pltpu.VMEM((ROWS, 4 * EDGE), F32)]
            return tuple(
                call(
                    last_sides_kernel,
                    [BLOCK, BLOCK],
                    scratch + FINISH_SCRATCH + [pltpu.SemaphoreType.DMA((6,))],
                    1,
                    *operands,
                    hbm_in=(13, 14),
                    hbm_out=(0, 1),
                    aliases={13: 0, 14: 1},
                )
            )
        dens, value, side, own_t, far_1, near_1 = call(
            next_sides_kernel, [BLOCK, BLOCK] + FIRST, FINISH_SCRATCH, 1, *operands, aliases={13: 0, 14: 1}
        )


def solution(mesh):
    placed = (P("rows", "cols"), P("rows", "cols"), P("rows", "cols"), P(), P())
    return jax.shard_map(
        body,
        mesh=mesh,
        in_specs=placed,
        out_specs=(P("rows", "cols"), P("rows", "cols")),
        check_vma=False,
    )
```

```python
import functools

import jax
import jax.numpy as jnp
from jax import lax
from jax.experimental import pallas as pl
from jax.experimental.pallas import tpu as pltpu
from jax.sharding import PartitionSpec as P

STEPS = 2
EDGE_COST = 6
FIRST_MIB = 51
NU = 0.5
DT = 0.1

ROWS = 256
COLS = 1024
KW = 256
HALF = KW // 2
EDGE = 128
MID = COLS - 2 * EDGE
FROM_R = COLS - EDGE
RAW_AT = HALF
TURNED_AT = RAW_AT + 16
FIRST_ROWS = TURNED_AT + 8
TALL = 3 * ROWS
SEGMENTS = TALL // EDGE
COL_ROWS = ROWS + 4 * SEGMENTS

VMEM = pl.BlockSpec(memory_space=pltpu.VMEM)
HBM = pl.BlockSpec(memory_space=pltpu.HBM)
F32 = jnp.float32
BF16 = jnp.bfloat16


def shape(*dims, kind=F32):
    return jax.ShapeDtypeStruct(dims, kind)


def call(kernel, out_shapes, scratch, micros, *operands, hbm_in=(), hbm_out=(), aliases=None, mib=24):
    return pl.pallas_call(
        kernel,
        out_shape=out_shapes,
        in_specs=[HBM if n in hbm_in else VMEM for n in range(len(operands))],
        out_specs=[HBM if n in hbm_out else VMEM for n in range(len(out_shapes))],
        scratch_shapes=scratch,
        input_output_aliases=aliases or {},
        compiler_params=pltpu.CompilerParams(vmem_limit_bytes=mib * 1024 * 1024),
        cost_estimate=pl.CostEstimate(
            flops=int(micros * 10**9), bytes_accessed=int(micros * 3 * 10**6), transcendentals=0
        ),
    )(*operands)


def core_index():
    return lax.rem(lax.axis_index("rows"), 2)


def split(x):
    hi = x.astype(BF16)
    return hi, (x - hi.astype(F32)).astype(BF16)


def product(left, right):
    dot = functools.partial(jnp.dot, preferred_element_type=F32)
    return dot(left[0], right[0]) + (dot(left[1], right[0]) + dot(left[0], right[1]))


def put_split(refs, x):
    refs[0][...], refs[1][...] = split(x)


def band(kern, turned, rows=None):
    row = jnp.concatenate([jnp.zeros((1, 2 * KW), F32), kern[...]], axis=1)
    full = jnp.broadcast_to(row, (2 * KW, 3 * KW))
    table = pltpu.roll(full, 0, 1, stride=1, stride_axis=0)[:, :KW]
    put_split(turned, table)
    if rows is not None:
        put_split(rows, table.T)


ROWS_TABLE = [shape(KW, 2 * KW, kind=BF16)] * 2
TURNED_TABLE = [shape(2 * KW, KW, kind=BF16)] * 2


def flux(a, here, there):
    c = DT * NU
    a = DT * a
    return here * jnp.maximum(a + c, c) + there * jnp.minimum(a - c, -c)


def eight_rows(m, u):
    width = m.shape[1]
    flux_x = flux(u - pltpu.roll(u, 7, 0), m, pltpu.roll(m, 7, 0))
    flux_y = flux(u - pltpu.roll(u, width - 1, 1), m, pltpu.roll(m, width - 1, 1))
    return m - ((flux_x - pltpu.roll(flux_x, 1, 0)) + (flux_y - pltpu.roll(flux_y, 1, 1)))


def middle_density(dens, value, out):
    own = slice(EDGE, FROM_R)
    tall = 64

    def step(i, flux_before):
        rows = pl.ds(pl.multiple_of(tall * i, tall), tall)
        after = pl.ds(pl.multiple_of(jnp.minimum(tall * i + tall, ROWS - 8), 8), 8)
        m_all = dens[rows, :]
        u_all = value[rows, :]
        m = m_all[:, own]
        u = u_all[:, own]
        m_down = jnp.concatenate([m[1:], dens[after, own][0:1]], axis=0)
        u_down = jnp.concatenate([u[1:], value[after, own][0:1]], axis=0)
        flux_x = flux(u - u_down, m, m_down)
        flux_up = jnp.concatenate([flux_before, flux_x[:-1]], axis=0)
        u_right = pltpu.roll(u_all, COLS - 1, 1)[:, 0:FROM_R]
        m_right = pltpu.roll(m_all, COLS - 1, 1)[:, 0:FROM_R]
        flux_y = flux(u_all[:, 0:FROM_R] - u_right, m_all[:, 0:FROM_R], m_right)
        flux_left = pltpu.roll(flux_y, 1, 1)[:, own]
        out[rows, :] = m - ((flux_x - flux_up) + (flux_y[:, own] - flux_left))
        return flux_x[-1:]

    lax.fori_loop(0, ROWS // tall, step, jnp.zeros((1, MID), F32))


def inner_value(value, potential, out):
    tall = 32

    def step(i, before):
        rows = pl.ds(pl.multiple_of(tall * i, tall), tall)
        after = pl.ds(pl.multiple_of(jnp.minimum(tall * i + tall, ROWS - 8), 8), 8)
        u = value[rows, :]
        down = jnp.concatenate([u[1:], value[after, :][0:1]], axis=0) - u
        up = jnp.concatenate([before, down[:-1]], axis=0)
        right = pltpu.roll(u, COLS - 1, 1) - u
        left = pltpu.roll(right, 1, 1)
        out[rows, :] = value_formula(u, down, up, right, left, potential[rows, :])
        return down[-1:]

    lax.fori_loop(0, ROWS // tall, step, jnp.zeros((1, COLS), F32), unroll=4)


def end_rows(value, potential, around, out):
    sub = lax.broadcasted_iota(jnp.int32, (8, COLS), 0)
    for rows, at, halo in ((slice(0, 8), 0, 1), (slice(ROWS - 8, ROWS), 7, 6)):
        u = value[rows, :]
        there = around[halo : halo + 1, :]
        down = pltpu.roll(u, 7, 0)
        up = pltpu.roll(u, 1, 0)
        if at == 0:
            up = jnp.where(sub == 0, there, up)
        else:
            down = jnp.where(sub == 7, there, down)
        right = pltpu.roll(u, COLS - 1, 1) - u
        result = value_formula(u, down - u, u - up, right, pltpu.roll(right, 1, 1), potential[rows, :])
        out[rows.start + at : rows.start + at + 1, :] = result[at : at + 1, :]


def value_formula(u, down, up, right, left, cost):
    grad_sq = (
        jnp.square(jnp.maximum(up, 0.0))
        + jnp.square(jnp.minimum(down, 0.0))
        + jnp.square(jnp.maximum(left, 0.0))
        + jnp.square(jnp.minimum(right, 0.0))
    )
    lap = (down - up) + (right - left)
    return u + DT * (NU * lap - 0.5 * grad_sq + cost)


def side_density(dens, value, out):
    lane = lax.broadcasted_iota(jnp.int32, (ROWS, EDGE), 1)
    blocks = [slice(at, at + EDGE) for at in (0, EDGE, FROM_R - EDGE, FROM_R)]

    def right(ref, here):
        there = pltpu.roll(ref[:, blocks[1]], EDGE - 1, 1)
        return jnp.where(lane == EDGE - 1, there, pltpu.roll(here, EDGE - 1, 1))

    def left(ref, here):
        there = pltpu.roll(ref[:, blocks[2]], 1, 1)
        return jnp.where(lane == 0, there, pltpu.roll(here, 1, 1))

    for n in (0, 3):
        m = dens[:, blocks[n]]
        u = value[:, blocks[n]]
        flux_x = flux(u - pltpu.roll(u, ROWS - 1, 0), m, pltpu.roll(m, ROWS - 1, 0))
        flux_up = pltpu.roll(flux_x, 1, 0)
        if n == 0:
            flux_right = flux(u - right(value, u), m, right(dens, m))
            flux_left = pltpu.roll(flux_right, 1, 1)
        else:
            flux_left = flux(left(value, u) - u, left(dens, m), m)
            flux_right = pltpu.roll(flux_left, EDGE - 1, 1)
        at = slice(0, EDGE) if n == 0 else slice(EDGE, 2 * EDGE)
        out[:, at] = m - ((flux_x - flux_up) + (flux_right - flux_left))


def prepare_sides(dens, value, side, own_t, far, near, wait_middle=None):
    core = core_index()
    side_density(dens, value, side)
    if wait_middle is not None:
        wait_middle()
    for n, ref in enumerate((dens, value)):
        own_t[4 * n : 4 * n + 2, :] = ref[:, 0:EDGE].T[0:2, :]
        own_t[4 * n + 2 : 4 * n + 4, :] = ref[:, FROM_R:COLS].T[EDGE - 2 : EDGE, :]
    for one, bottom in ((far, core), (near, 1 - core)):
        one[0:HALF, :] = side[pl.ds(pl.multiple_of(bottom * HALF, 8), HALF), :]
        for n, ref in enumerate((dens, value)):
            eight = ref[pl.ds(pl.multiple_of(bottom * (ROWS - 8), 8), 8), :]
            pair = jnp.where(bottom == 1, eight[6:8, :], eight[0:2, :])
            for q in range(COLS // 256):
                at = RAW_AT + 4 * q + 2 * n
                one[at : at + 2, :] = pair[:, 256 * q : 256 * q + 256]
        one[TURNED_AT:FIRST_ROWS, :] = own_t[...]


def rest_kernel(dens, value, new, far, near):
    core = core_index()
    middle_density(dens, value, new)
    for two, bottom in ((far, core), (near, 1 - core)):
        two[...] = new[pl.ds(pl.multiple_of(bottom * HALF, 8), HALF), :]


FIRST = [
    shape(ROWS, 2 * EDGE),
    shape(8, ROWS),
    shape(FIRST_ROWS, 2 * EDGE),
    shape(FIRST_ROWS, 2 * EDGE),
]
SECOND = [shape(ROWS, MID), shape(HALF, MID), shape(HALF, MID)]
BLOCK = shape(ROWS, COLS)


def first_sides_kernel(dens_in, value_in, dens, value, side, own_t, far, near, semaphores):
    outer = []
    inner = []
    quarter = 2 * EDGE
    for q in (0, 3, 1, 2):
        lanes = slice(quarter * q, quarter * q + quarter)
        for source, target in ((dens_in, dens), (value_in, value)):
            copies = outer if q in (0, 3) else inner
            n = len(outer) + len(inner)
            copies.append(pltpu.make_async_copy(source.at[:, lanes], target.at[:, lanes], semaphores.at[n]))
    for copy in outer + inner:
        copy.start()
    for copy in outer:
        copy.wait()

    def wait_middle():
        for copy in inner:
            copy.wait()

    prepare_sides(dens, value, side, own_t, far, near, wait_middle)


def turned_cost(potential, cost_t):
    cost_t[0:2, :] = potential[:, 0:EDGE].T[0:2, :]
    cost_t[2:4, :] = potential[:, FROM_R:COLS].T[EDGE - 2 : EDGE, :]


def first_rest_kernel(dens, value, kern_rows, new, far, near, *table):
    rest_kernel(dens, value, new, far, near)
    band(kern_rows, table[2:4], table[0:2])


def halo_rows(ext, far, near):
    core = core_index()
    ext[pl.ds(pl.multiple_of(core * (HALF + ROWS), 8), HALF), :] = far
    ext[pl.ds(pl.multiple_of((1 - core) * (HALF + ROWS), 8), HALF), :] = near


def edge_kernel(
    dens, value, side, own_t, far, near, rows_hi, rows_lo,
    to_left, to_right, seams, around, tall, mixed, dens_8, ext,
):
    core = core_index()
    for ref, own, n in ((dens_8, dens, 0), (around, value, 1)):
        for q in range(COLS // 256):
            lanes = slice(256 * q, 256 * q + 256)
            at = RAW_AT + 4 * q + 2 * n
            f = far[at : at + 2, :]
            g = near[at : at + 2, :]
            ref[0:2, lanes] = jnp.where(core == 0, f, g)
            ref[6:8, lanes] = jnp.where(core == 0, g, f)
        ref[2:4, :] = own[0:2, :]
        ref[4:6, :] = own[ROWS - 2 : ROWS, :]
    seam = eight_rows(dens_8[...], around[...])
    seams[...] = seam
    f = far[TURNED_AT:FIRST_ROWS, :]
    g = near[TURNED_AT:FIRST_ROWS, :]
    tall[:, 0:ROWS] = jnp.where(core == 0, f, g)
    tall[:, ROWS : 2 * ROWS] = own_t[...]
    tall[:, 2 * ROWS : TALL] = jnp.where(core == 0, g, f)

    halo_rows(ext, far[0:HALF, :], near[0:HALF, :])
    ext[HALF : HALF + ROWS, :] = side[...]
    put_seams(ext, seams, ((slice(0, EDGE), slice(0, EDGE)), (slice(EDGE, 2 * EDGE), slice(FROM_R, COLS))))
    result = product((rows_hi[...], rows_lo[...]), split(ext[...]))
    mixed[...] = result
    for ref, lanes, at in ((to_left, slice(0, EDGE), 0), (to_right, slice(EDGE, 2 * EDGE), 2)):
        ref[0:ROWS, :] = result[:, lanes]
        for q in range(SEGMENTS):
            segment = slice(EDGE * q, EDGE * q + EDGE)
            ref[ROWS + 4 * q : ROWS + 4 * q + 2, :] = tall[at : at + 2, segment]
            ref[ROWS + 4 * q + 2 : ROWS + 4 * q + 4, :] = tall[at + 4 : at + 6, segment]


def put_seams(ext, seams, lane_pairs):
    for to, source in lane_pairs:
        ext[HALF - 1 : HALF, to] = seams[1:2, source]
        ext[HALF : HALF + 1, to] = seams[2:3, source]
        ext[HALF + ROWS - 1 : HALF + ROWS, to] = seams[5:6, source]
        ext[HALF + ROWS : HALF + ROWS + 1, to] = seams[6:7, source]


def middle_mix(
    new, seams, far, near, rows_hi, rows_lo, cols_hi, cols_lo, cong_s, cong_m, ext, mix_hi, mix_lo
):
    rows = (rows_hi[...], rows_lo[...])
    for b in range(MID // 256):
        lanes = slice(256 * b, 256 * b + 256)
        mix_hi[:, lanes], mix_lo[:, lanes] = split(product(rows, split(ext[:, lanes])))
    before = (cols_hi[0:KW, :], cols_lo[0:KW, :])
    after = (cols_hi[KW : 2 * KW, :], cols_lo[KW : 2 * KW, :])
    for b in range(COLS // 256):
        total = None
        for block, table in ((b - 1, before), (b, after)):
            if 0 <= block < MID // 256:
                lanes = slice(256 * block, 256 * block + 256)
                part = product((mix_hi[:, lanes], mix_lo[:, lanes]), table)
                total = part if total is None else total + part
        if b == 0:
            cong_s[:, 0:256] = total
        elif b == COLS // 256 - 1:
            cong_s[:, 256:512] = total
        else:
            cong_m[:, 256 * (b - 1) : 256 * b] = total


INSIDE = slice(2 * EDGE, COLS - 2 * EDGE)
INSIDE_N = COLS - 4 * EDGE


def middle_ext(new, seams, far, near, ext):
    halo_rows(ext, far[...], near[...])
    ext[HALF : HALF + ROWS, :] = new[...]
    put_seams(ext, seams, ((slice(0, MID), slice(EDGE, FROM_R)),))


def first_middle_kernel(*refs):
    new, seams, far, near, rows_hi, rows_lo, kern_cols, value, potential, around = refs[:10]
    cong_s, inner, cost_t, dens_out, value_out, cols_hi, cols_lo, ext, mix_hi, mix_lo, cong_m = refs[10:]
    band(kern_cols, (cols_hi, cols_lo))
    table = (rows_hi, rows_lo, cols_hi, cols_lo)
    middle_ext(new, seams, far, near, ext)
    middle_mix(new, seams, far, near, *table, cong_s, cong_m, ext, mix_hi, mix_lo)
    turned_cost(potential, cost_t)
    inner_value(value, potential, inner)
    end_rows(value, potential, around, inner)
    dens_out[:, EDGE:FROM_R] = ext[HALF : HALF + ROWS, :]
    value_out[:, INSIDE] = inner[:, INSIDE] + DT * cong_m[...]


def last_middle_kernel(*refs):
    new, seams, far, near = refs[:4]
    value, potential, around = refs[8:11]
    cong_s, inner, cost_t, dens_out, value_out, ext, mix_hi, mix_lo, cong_m, value_mid, semaphores = refs[11:]
    middle_ext(new, seams, far, near, ext)
    dens_copy = pltpu.make_async_copy(
        ext.at[HALF : HALF + ROWS, :], dens_out.at[:, EDGE:FROM_R], semaphores.at[0]
    )
    dens_copy.start()
    middle_mix(*refs[:8], cong_s, cong_m, ext, mix_hi, mix_lo)
    turned_cost(potential, cost_t)
    inner_value(value, potential, inner)
    end_rows(value, potential, around, inner)
    value_mid[...] = inner[:, INSIDE] + DT * cong_m[...]
    value_copy = pltpu.make_async_copy(value_mid, value_out.at[:, INSIDE], semaphores.at[1])
    value_copy.start()
    dens_copy.wait()
    value_copy.wait()


def finish(
    cost_t, side, seams, tall, left, right, mixed, cong, inner, turned_hi, turned_lo, cols_hi, cols_lo,
    put_dens, put_value, dens_t, value_t, turn,
):
    for ref, n in ((dens_t, 0), (value_t, 1)):
        for q in range(SEGMENTS):
            lanes = slice(EDGE * q, EDGE * q + EDGE)
            at = ROWS + 4 * q + 2 * n
            ref[0:2, lanes] = left[at : at + 2, :]
            ref[6:8, lanes] = right[at : at + 2, :]
        ref[2:6, :] = tall[4 * n : 4 * n + 4, :]
    u = value_t[...]
    new_t = eight_rows(dens_t[...], u)
    window = new_t[:, HALF : HALF + 2 * KW]
    window = jnp.concatenate([window, window], axis=0)
    turn[0:8, :] = product(split(window), (turned_hi[...], turned_lo[...]))[0:8, :]
    own = slice(ROWS, 2 * ROWS)
    turn[8:16, :] = new_t[:, own]
    right_t = pltpu.roll(u, 7, 0) - u
    left_t = u - pltpu.roll(u, 1, 0)
    down_t = pltpu.roll(u, TALL - 1, 1) - u
    up_t = u - pltpu.roll(u, 1, 1)
    cost = jnp.concatenate([cost_t[0:2, :], cost_t[0:4, :], cost_t[2:4, :]], axis=0)
    turn[16:24, :] = value_formula(
        u[:, own], down_t[:, own], up_t[:, own], right_t[:, own], left_t[:, own], cost
    )
    columns = turn[...].T

    def column(n):
        return columns[:, n : n + 1]

    lane = lax.broadcasted_iota(jnp.int32, (ROWS, EDGE), 1)
    row = lax.broadcasted_iota(jnp.int32, (ROWS, EDGE), 0)
    for block, lanes, from_side, at, n in (
        (0, slice(0, EDGE), slice(0, EDGE), 0, 10),
        (3, slice(FROM_R, COLS), slice(EDGE, 2 * EDGE), EDGE - 1, 13),
    ):
        x = jnp.where(row == 0, seams[2:3, lanes], side[:, from_side])
        x = jnp.where(row == ROWS - 1, seams[5:6, lanes], x)
        put_dens(block, jnp.where(lane == at, column(n), x))
    lane = lax.broadcasted_iota(jnp.int32, (ROWS, 2 * EDGE), 1)
    known = jnp.logical_and(lane != EDGE - 1, lane != EDGE)
    before = (cols_hi[0:KW, :], cols_lo[0:KW, :])
    after = (cols_hi[KW : 2 * KW, :], cols_lo[KW : 2 * KW, :])

    def table_row(n):
        base = n // 16 * 16
        rows = cols_hi[base : base + 16, :].astype(F32) + cols_lo[base : base + 16, :].astype(F32)
        return rows[n - base : n - base + 1, :]

    low = jnp.where(known, jnp.concatenate([left[0:ROWS, :], mixed[:, 0:EDGE]], axis=1), 0.0)
    low = cong[:, 0:256] + product(split(low), before)
    low = low + (column(1) * table_row(EDGE - 1) + column(2) * table_row(EDGE))
    half = lax.broadcasted_iota(jnp.int32, (ROWS, EDGE), 1)
    put_value(1, inner[:, EDGE : 2 * EDGE] + DT * low[:, EDGE : 2 * EDGE])
    put_value(0, jnp.where(half == 0, column(18), inner[:, 0:EDGE]) + DT * low[:, 0:EDGE])
    high = jnp.where(known, jnp.concatenate([mixed[:, EDGE : 2 * EDGE], right[0:ROWS, :]], axis=1), 0.0)
    high = cong[:, 256:512] + product(split(high), after)
    high = high + (column(5) * table_row(KW + EDGE - 1) + column(6) * table_row(KW + EDGE))
    put_value(2, inner[:, FROM_R - EDGE : FROM_R] + DT * high[:, 0:EDGE])
    put_value(
        3, jnp.where(half == EDGE - 1, column(21), inner[:, FROM_R:COLS]) + DT * high[:, EDGE : 2 * EDGE]
    )


FINISH_SCRATCH = [
    pltpu.VMEM((8, TALL), F32),
    pltpu.VMEM((8, TALL), F32),
    pltpu.VMEM((128, ROWS), F32),
]


def next_sides_kernel(*refs):
    dens, value = refs[15:17]
    starts = (0, EDGE, FROM_R - EDGE, FROM_R)

    def put(ref):
        def store(block, x):
            ref[:, starts[block] : starts[block] + EDGE] = x

        return store

    finish(*refs[:13], put(dens), put(value), *refs[21:])
    prepare_sides(dens, value, *refs[17:21])


def last_sides_kernel(*refs):
    dens_out, value_out = refs[15:17]
    dens_s, value_s, dens_t, value_t, turn, semaphores = refs[17:]
    starts = (0, EDGE, FROM_R - EDGE, FROM_R)
    copies = []

    def put(sides, out):
        def store(block, x):
            lanes = slice(EDGE * block, EDGE * block + EDGE)
            sides[:, lanes] = x
            target = out.at[:, starts[block] : starts[block] + EDGE]
            copy = pltpu.make_async_copy(sides.at[:, lanes], target, semaphores.at[len(copies)])
            copy.start()
            copies.append(copy)

        return store

    finish(*refs[:13], put(dens_s, dens_out), put(value_s, value_out), dens_t, value_t, turn)
    for copy in copies:
        copy.wait()


def row_pairs(count, first):
    pairs = []
    for a in range(first, count, 2):
        b = (a + 1) % count
        pairs += [(a, b), (b, a)]
    return pairs


def body(density, value_field, potential, kern_rows, kern_cols):
    n_rows = lax.axis_size("rows")
    n_cols = lax.axis_size("cols")
    far_pairs = row_pairs(n_rows, 1)
    near_pairs = row_pairs(n_rows, 0)
    to_right = [(c, (c + 1) % n_cols) for c in range(n_cols)]
    to_left = [(c, (c - 1) % n_cols) for c in range(n_cols)]
    dens, value, side, own_t, far_1, near_1 = call(
        first_sides_kernel,
        [BLOCK, BLOCK] + FIRST,
        [pltpu.SemaphoreType.DMA((8,))],
        1,
        density, value_field,
        hbm_in=(0, 1),
        mib=FIRST_MIB,
    )
    for step_index in range(STEPS):
        last = step_index == STEPS - 1
        if step_index == 0:
            new, far_2, near_2, *table = call(
                first_rest_kernel, SECOND + ROWS_TABLE + TURNED_TABLE, [], 1, dens, value, kern_rows[None]
            )
            rows_table, turned_table = table[0:2], table[2:4]
        else:
            new, far_2, near_2 = call(rest_kernel, SECOND, [], 1, dens, value)
        far_1 = lax.ppermute(far_1, "rows", far_pairs)
        near_1 = lax.ppermute(near_1, "rows", near_pairs)
        far_2 = lax.ppermute(far_2, "rows", far_pairs)
        near_2 = lax.ppermute(near_2, "rows", near_pairs)
        left, right, seams, around, tall, mixed = call(
            edge_kernel,
            [shape(COL_ROWS, EDGE), shape(COL_ROWS, EDGE), shape(8, COLS), shape(8, COLS), shape(8, TALL), shape(ROWS, 2 * EDGE)],
            [pltpu.VMEM((8, COLS), F32), pltpu.VMEM((2 * KW, 2 * EDGE), F32)],
            EDGE_COST,
            dens, value, side, own_t, far_1, near_1, *rows_table,
        )
        right_in = lax.ppermute(left, "cols", to_left)
        left_in = lax.ppermute(right, "cols", to_right)
        scratch = [
            pltpu.VMEM((2 * KW, MID), F32),
            pltpu.VMEM((ROWS, MID), BF16),
            pltpu.VMEM((ROWS, MID), BF16),
            pltpu.VMEM((ROWS, INSIDE_N), F32),
        ]
        if last:
            scratch += [pltpu.VMEM((ROWS, INSIDE_N), F32), pltpu.SemaphoreType.DMA((2,))]
        if last:
            cong, inner, cost_t, *results = call(
                last_middle_kernel,
                [shape(ROWS, 4 * EDGE), BLOCK, shape(8, ROWS), BLOCK, BLOCK],
                scratch,
                3,
                new, seams, far_2, near_2, *rows_table, *cols_table, value, potential, around,
                hbm_out=(3, 4),
            )
        else:
            cong, inner, cost_t, dens_out, value_out, *cols_table = call(
                first_middle_kernel,
                [shape(ROWS, 4 * EDGE), BLOCK, shape(8, ROWS), BLOCK, BLOCK] + TURNED_TABLE,
                scratch,
                3,
                new, seams, far_2, near_2, *rows_table, kern_cols[None], value, potential, around,
            )
            results = [dens_out, value_out]
        operands = (cost_t, side, seams, tall, left_in, right_in, mixed, cong, inner, *turned_table, *cols_table, *results)
        if last:
            scratch = [pltpu.VMEM((ROWS, 4 * EDGE), F32), pltpu.VMEM((ROWS, 4 * EDGE), F32)]
            return tuple(
                call(
                    last_sides_kernel,
                    [BLOCK, BLOCK],
                    scratch + FINISH_SCRATCH + [pltpu.SemaphoreType.DMA((6,))],
                    1,
                    *operands,
                    hbm_in=(13, 14),
                    hbm_out=(0, 1),
                    aliases={13: 0, 14: 1},
                )
            )
        dens, value, side, own_t, far_1, near_1 = call(
            next_sides_kernel, [BLOCK, BLOCK] + FIRST, FINISH_SCRATCH, 1, *operands, aliases={13: 0, 14: 1}
        )


def solution(mesh):
    placed = (P("rows", "cols"), P("rows", "cols"), P("rows", "cols"), P(), P())
    return jax.shard_map(
        body,
        mesh=mesh,
        in_specs=placed,
        out_specs=(P("rows", "cols"), P("rows", "cols")),
        check_vma=False,
    )
```

```python
import functools

import jax
import jax.numpy as jnp
from jax import lax
from jax.experimental import pallas as pl
from jax.experimental.pallas import tpu as pltpu
from jax.sharding import PartitionSpec as P

STEPS = 2
EDGE_COST = 6
TABLE_COST = 0.3
FIRST_MIB = 51
NU = 0.5
DT = 0.1

ROWS = 256
COLS = 1024
KW = 256
HALF = KW // 2
EDGE = 128
MID = COLS - 2 * EDGE
FROM_R = COLS - EDGE
RAW_AT = HALF
TURNED_AT = RAW_AT + 16
FIRST_ROWS = TURNED_AT + 8
TALL = 3 * ROWS
SEGMENTS = TALL // EDGE
COL_ROWS = ROWS + 4 * SEGMENTS

VMEM = pl.BlockSpec(memory_space=pltpu.VMEM)
HBM = pl.BlockSpec(memory_space=pltpu.HBM)
F32 = jnp.float32
BF16 = jnp.bfloat16


def shape(*dims, kind=F32):
    return jax.ShapeDtypeStruct(dims, kind)


def call(kernel, out_shapes, scratch, micros, *operands, hbm_in=(), hbm_out=(), aliases=None, mib=24):
    return pl.pallas_call(
        kernel,
        out_shape=out_shapes,
        in_specs=[HBM if n in hbm_in else VMEM for n in range(len(operands))],
        out_specs=[HBM if n in hbm_out else VMEM for n in range(len(out_shapes))],
        scratch_shapes=scratch,
        input_output_aliases=aliases or {},
        compiler_params=pltpu.CompilerParams(vmem_limit_bytes=mib * 1024 * 1024),
        cost_estimate=pl.CostEstimate(
            flops=int(micros * 10**9), bytes_accessed=int(micros * 3 * 10**6), transcendentals=0
        ),
    )(*operands)


def core_index():
    return lax.rem(lax.axis_index("rows"), 2)


def split(x):
    hi = x.astype(BF16)
    return hi, (x - hi.astype(F32)).astype(BF16)


def product(left, right):
    dot = functools.partial(jnp.dot, preferred_element_type=F32)
    return dot(left[0], right[0]) + (dot(left[1], right[0]) + dot(left[0], right[1]))


def put_split(refs, x):
    refs[0][...], refs[1][...] = split(x)


def band(kern, turned, rows=None):
    row = jnp.concatenate([jnp.zeros((1, 2 * KW), F32), kern[...]], axis=1)
    full = jnp.broadcast_to(row, (2 * KW, 3 * KW))
    table = pltpu.roll(full, 0, 1, stride=1, stride_axis=0)[:, :KW]
    put_split(turned, table)
    if rows is not None:
        put_split(rows, table.T)


ROWS_TABLE = [shape(KW, 2 * KW, kind=BF16)] * 2
TURNED_TABLE = [shape(2 * KW, KW, kind=BF16)] * 2


def flux(a, here, there):
    c = DT * NU
    a = DT * a
    return here * jnp.maximum(a + c, c) + there * jnp.minimum(a - c, -c)


def eight_rows(m, u):
    width = m.shape[1]
    flux_x = flux(u - pltpu.roll(u, 7, 0), m, pltpu.roll(m, 7, 0))
    flux_y = flux(u - pltpu.roll(u, width - 1, 1), m, pltpu.roll(m, width - 1, 1))
    return m - ((flux_x - pltpu.roll(flux_x, 1, 0)) + (flux_y - pltpu.roll(flux_y, 1, 1)))


def middle_density(dens, value, out):
    own = slice(EDGE, FROM_R)
    tall = 64

    def step(i, flux_before):
        rows = pl.ds(pl.multiple_of(tall * i, tall), tall)
        after = pl.ds(pl.multiple_of(jnp.minimum(tall * i + tall, ROWS - 8), 8), 8)
        m_all = dens[rows, :]
        u_all = value[rows, :]
        m = m_all[:, own]
        u = u_all[:, own]
        m_down = jnp.concatenate([m[1:], dens[after, own][0:1]], axis=0)
        u_down = jnp.concatenate([u[1:], value[after, own][0:1]], axis=0)
        flux_x = flux(u - u_down, m, m_down)
        flux_up = jnp.concatenate([flux_before, flux_x[:-1]], axis=0)
        u_right = pltpu.roll(u_all, COLS - 1, 1)[:, 0:FROM_R]
        m_right = pltpu.roll(m_all, COLS - 1, 1)[:, 0:FROM_R]
        flux_y = flux(u_all[:, 0:FROM_R] - u_right, m_all[:, 0:FROM_R], m_right)
        flux_left = pltpu.roll(flux_y, 1, 1)[:, own]
        out[rows, :] = m - ((flux_x - flux_up) + (flux_y[:, own] - flux_left))
        return flux_x[-1:]

    lax.fori_loop(0, ROWS // tall, step, jnp.zeros((1, MID), F32))


def inner_value(value, potential, out):
    tall = 32

    def step(i, before):
        rows = pl.ds(pl.multiple_of(tall * i, tall), tall)
        after = pl.ds(pl.multiple_of(jnp.minimum(tall * i + tall, ROWS - 8), 8), 8)
        u = value[rows, :]
        down = jnp.concatenate([u[1:], value[after, :][0:1]], axis=0) - u
        up = jnp.concatenate([before, down[:-1]], axis=0)
        right = pltpu.roll(u, COLS - 1, 1) - u
        left = pltpu.roll(right, 1, 1)
        out[rows, :] = value_formula(u, down, up, right, left, potential[rows, :])
        return down[-1:]

    lax.fori_loop(0, ROWS // tall, step, jnp.zeros((1, COLS), F32), unroll=4)


def end_rows(value, potential, around, out):
    sub = lax.broadcasted_iota(jnp.int32, (8, COLS), 0)
    for rows, at, halo in ((slice(0, 8), 0, 1), (slice(ROWS - 8, ROWS), 7, 6)):
        u = value[rows, :]
        there = around[halo : halo + 1, :]
        down = pltpu.roll(u, 7, 0)
        up = pltpu.roll(u, 1, 0)
        if at == 0:
            up = jnp.where(sub == 0, there, up)
        else:
            down = jnp.where(sub == 7, there, down)
        right = pltpu.roll(u, COLS - 1, 1) - u
        result = value_formula(u, down - u, u - up, right, pltpu.roll(right, 1, 1), potential[rows, :])
        out[rows.start + at : rows.start + at + 1, :] = result[at : at + 1, :]


def value_formula(u, down, up, right, left, cost):
    grad_sq = (
        jnp.square(jnp.maximum(up, 0.0))
        + jnp.square(jnp.minimum(down, 0.0))
        + jnp.square(jnp.maximum(left, 0.0))
        + jnp.square(jnp.minimum(right, 0.0))
    )
    lap = (down - up) + (right - left)
    return u + DT * (NU * lap - 0.5 * grad_sq + cost)


def side_density(dens, value, out):
    lane = lax.broadcasted_iota(jnp.int32, (ROWS, EDGE), 1)
    blocks = [slice(at, at + EDGE) for at in (0, EDGE, FROM_R - EDGE, FROM_R)]

    def right(ref, here):
        there = pltpu.roll(ref[:, blocks[1]], EDGE - 1, 1)
        return jnp.where(lane == EDGE - 1, there, pltpu.roll(here, EDGE - 1, 1))

    def left(ref, here):
        there = pltpu.roll(ref[:, blocks[2]], 1, 1)
        return jnp.where(lane == 0, there, pltpu.roll(here, 1, 1))

    for n in (0, 3):
        m = dens[:, blocks[n]]
        u = value[:, blocks[n]]
        flux_x = flux(u - pltpu.roll(u, ROWS - 1, 0), m, pltpu.roll(m, ROWS - 1, 0))
        flux_up = pltpu.roll(flux_x, 1, 0)
        if n == 0:
            flux_right = flux(u - right(value, u), m, right(dens, m))
            flux_left = pltpu.roll(flux_right, 1, 1)
        else:
            flux_left = flux(left(value, u) - u, left(dens, m), m)
            flux_right = pltpu.roll(flux_left, EDGE - 1, 1)
        at = slice(0, EDGE) if n == 0 else slice(EDGE, 2 * EDGE)
        out[:, at] = m - ((flux_x - flux_up) + (flux_right - flux_left))


def prepare_sides(dens, value, side, own_t, far, near, wait_middle=None):
    core = core_index()
    side_density(dens, value, side)
    if wait_middle is not None:
        wait_middle()
    for n, ref in enumerate((dens, value)):
        own_t[4 * n : 4 * n + 2, :] = ref[:, 0:EDGE].T[0:2, :]
        own_t[4 * n + 2 : 4 * n + 4, :] = ref[:, FROM_R:COLS].T[EDGE - 2 : EDGE, :]
    for one, bottom in ((far, core), (near, 1 - core)):
        one[0:HALF, :] = side[pl.ds(pl.multiple_of(bottom * HALF, 8), HALF), :]
        for n, ref in enumerate((dens, value)):
            eight = ref[pl.ds(pl.multiple_of(bottom * (ROWS - 8), 8), 8), :]
            pair = jnp.where(bottom == 1, eight[6:8, :], eight[0:2, :])
            for q in range(COLS // 256):
                at = RAW_AT + 4 * q + 2 * n
                one[at : at + 2, :] = pair[:, 256 * q : 256 * q + 256]
        one[TURNED_AT:FIRST_ROWS, :] = own_t[...]


def rest_kernel(dens, value, new, far, near):
    core = core_index()
    middle_density(dens, value, new)
    for two, bottom in ((far, core), (near, 1 - core)):
        two[...] = new[pl.ds(pl.multiple_of(bottom * HALF, 8), HALF), :]


FIRST = [
    shape(ROWS, 2 * EDGE),
    shape(8, ROWS),
    shape(FIRST_ROWS, 2 * EDGE),
    shape(FIRST_ROWS, 2 * EDGE),
]
SECOND = [shape(ROWS, MID), shape(HALF, MID), shape(HALF, MID)]
BLOCK = shape(ROWS, COLS)


def first_sides_kernel(dens_in, value_in, dens, value, side, own_t, far, near, semaphores):
    outer = []
    inner = []
    quarter = 2 * EDGE
    for q in (0, 3, 1, 2):
        lanes = slice(quarter * q, quarter * q + quarter)
        for source, target in ((dens_in, dens), (value_in, value)):
            copies = outer if q in (0, 3) else inner
            n = len(outer) + len(inner)
            copies.append(pltpu.make_async_copy(source.at[:, lanes], target.at[:, lanes], semaphores.at[n]))
    for copy in outer + inner:
        copy.start()
    for copy in outer:
        copy.wait()

    def wait_middle():
        for copy in inner:
            copy.wait()

    prepare_sides(dens, value, side, own_t, far, near, wait_middle)


def turned_cost(potential, cost_t):
    cost_t[0:2, :] = potential[:, 0:EDGE].T[0:2, :]
    cost_t[2:4, :] = potential[:, FROM_R:COLS].T[EDGE - 2 : EDGE, :]


def rows_table_kernel(kern_rows, *table):
    band(kern_rows, table[2:4], table[0:2])


def halo_rows(ext, far, near):
    core = core_index()
    ext[pl.ds(pl.multiple_of(core * (HALF + ROWS), 8), HALF), :] = far
    ext[pl.ds(pl.multiple_of((1 - core) * (HALF + ROWS), 8), HALF), :] = near


def edge_kernel(
    dens, value, side, own_t, far, near, rows_hi, rows_lo,
    to_left, to_right, seams, around, tall, mixed, dens_8, ext,
):
    core = core_index()
    for ref, own, n in ((dens_8, dens, 0), (around, value, 1)):
        for q in range(COLS // 256):
            lanes = slice(256 * q, 256 * q + 256)
            at = RAW_AT + 4 * q + 2 * n
            f = far[at : at + 2, :]
            g = near[at : at + 2, :]
            ref[0:2, lanes] = jnp.where(core == 0, f, g)
            ref[6:8, lanes] = jnp.where(core == 0, g, f)
        ref[2:4, :] = own[0:2, :]
        ref[4:6, :] = own[ROWS - 2 : ROWS, :]
    seam = eight_rows(dens_8[...], around[...])
    seams[...] = seam
    f = far[TURNED_AT:FIRST_ROWS, :]
    g = near[TURNED_AT:FIRST_ROWS, :]
    tall[:, 0:ROWS] = jnp.where(core == 0, f, g)
    tall[:, ROWS : 2 * ROWS] = own_t[...]
    tall[:, 2 * ROWS : TALL] = jnp.where(core == 0, g, f)

    halo_rows(ext, far[0:HALF, :], near[0:HALF, :])
    ext[HALF : HALF + ROWS, :] = side[...]
    put_seams(ext, seams, ((slice(0, EDGE), slice(0, EDGE)), (slice(EDGE, 2 * EDGE), slice(FROM_R, COLS))))
    result = product((rows_hi[...], rows_lo[...]), split(ext[...]))
    mixed[...] = result
    for ref, lanes, at in ((to_left, slice(0, EDGE), 0), (to_right, slice(EDGE, 2 * EDGE), 2)):
        ref[0:ROWS, :] = result[:, lanes]
        for q in range(SEGMENTS):
            segment = slice(EDGE * q, EDGE * q + EDGE)
            ref[ROWS + 4 * q : ROWS + 4 * q + 2, :] = tall[at : at + 2, segment]
            ref[ROWS + 4 * q + 2 : ROWS + 4 * q + 4, :] = tall[at + 4 : at + 6, segment]


def put_seams(ext, seams, lane_pairs):
    for to, source in lane_pairs:
        ext[HALF - 1 : HALF, to] = seams[1:2, source]
        ext[HALF : HALF + 1, to] = seams[2:3, source]
        ext[HALF + ROWS - 1 : HALF + ROWS, to] = seams[5:6, source]
        ext[HALF + ROWS : HALF + ROWS + 1, to] = seams[6:7, source]


def middle_mix(
    new, seams, far, near, rows_hi, rows_lo, cols_hi, cols_lo, cong_s, cong_m, ext, mix_hi, mix_lo
):
    rows = (rows_hi[...], rows_lo[...])
    for b in range(MID // 256):
        lanes = slice(256 * b, 256 * b + 256)
        mix_hi[:, lanes], mix_lo[:, lanes] = split(product(rows, split(ext[:, lanes])))
    before = (cols_hi[0:KW, :], cols_lo[0:KW, :])
    after = (cols_hi[KW : 2 * KW, :], cols_lo[KW : 2 * KW, :])
    for b in range(COLS // 256):
        total = None
        for block, table in ((b - 1, before), (b, after)):
            if 0 <= block < MID // 256:
                lanes = slice(256 * block, 256 * block + 256)
                part = product((mix_hi[:, lanes], mix_lo[:, lanes]), table)
                total = part if total is None else total + part
        if b == 0:
            cong_s[:, 0:256] = total
        elif b == COLS // 256 - 1:
            cong_s[:, 256:512] = total
        else:
            cong_m[:, 256 * (b - 1) : 256 * b] = total


INSIDE = slice(2 * EDGE, COLS - 2 * EDGE)
INSIDE_N = COLS - 4 * EDGE


def middle_ext(new, seams, far, near, ext):
    halo_rows(ext, far[...], near[...])
    ext[HALF : HALF + ROWS, :] = new[...]
    put_seams(ext, seams, ((slice(0, MID), slice(EDGE, FROM_R)),))


def first_middle_kernel(*refs):
    new, seams, far, near, rows_hi, rows_lo, kern_cols, value, potential, around = refs[:10]
    cong_s, inner, cost_t, dens_out, value_out, cols_hi, cols_lo, ext, mix_hi, mix_lo, cong_m = refs[10:]
    band(kern_cols, (cols_hi, cols_lo))
    table = (rows_hi, rows_lo, cols_hi, cols_lo)
    middle_ext(new, seams, far, near, ext)
    middle_mix(new, seams, far, near, *table, cong_s, cong_m, ext, mix_hi, mix_lo)
    turned_cost(potential, cost_t)
    inner_value(value, potential, inner)
    end_rows(value, potential, around, inner)
    dens_out[:, EDGE:FROM_R] = ext[HALF : HALF + ROWS, :]
    value_out[:, INSIDE] = inner[:, INSIDE] + DT * cong_m[...]


def last_middle_kernel(*refs):
    new, seams, far, near = refs[:4]
    value, potential, around = refs[8:11]
    cong_s, inner, cost_t, dens_out, value_out, ext, mix_hi, mix_lo, cong_m, value_mid, semaphores = refs[11:]
    middle_ext(new, seams, far, near, ext)
    dens_copy = pltpu.make_async_copy(
        ext.at[HALF : HALF + ROWS, :], dens_out.at[:, EDGE:FROM_R], semaphores.at[0]
    )
    dens_copy.start()
    middle_mix(*refs[:8], cong_s, cong_m, ext, mix_hi, mix_lo)
    turned_cost(potential, cost_t)
    inner_value(value, potential, inner)
    end_rows(value, potential, around, inner)
    value_mid[...] = inner[:, INSIDE] + DT * cong_m[...]
    value_copy = pltpu.make_async_copy(value_mid, value_out.at[:, INSIDE], semaphores.at[1])
    value_copy.start()
    dens_copy.wait()
    value_copy.wait()


def finish(
    cost_t, side, seams, tall, left, right, mixed, cong, inner, turned_hi, turned_lo, cols_hi, cols_lo,
    put_dens, put_value, dens_t, value_t, turn,
):
    for ref, n in ((dens_t, 0), (value_t, 1)):
        for q in range(SEGMENTS):
            lanes = slice(EDGE * q, EDGE * q + EDGE)
            at = ROWS + 4 * q + 2 * n
            ref[0:2, lanes] = left[at : at + 2, :]
            ref[6:8, lanes] = right[at : at + 2, :]
        ref[2:6, :] = tall[4 * n : 4 * n + 4, :]
    u = value_t[...]
    new_t = eight_rows(dens_t[...], u)
    window = new_t[:, HALF : HALF + 2 * KW]
    window = jnp.concatenate([window, window], axis=0)
    turn[0:8, :] = product(split(window), (turned_hi[...], turned_lo[...]))[0:8, :]
    own = slice(ROWS, 2 * ROWS)
    turn[8:16, :] = new_t[:, own]
    right_t = pltpu.roll(u, 7, 0) - u
    left_t = u - pltpu.roll(u, 1, 0)
    down_t = pltpu.roll(u, TALL - 1, 1) - u
    up_t = u - pltpu.roll(u, 1, 1)
    cost = jnp.concatenate([cost_t[0:2, :], cost_t[0:4, :], cost_t[2:4, :]], axis=0)
    turn[16:24, :] = value_formula(
        u[:, own], down_t[:, own], up_t[:, own], right_t[:, own], left_t[:, own], cost
    )
    columns = turn[...].T

    def column(n):
        return columns[:, n : n + 1]

    lane = lax.broadcasted_iota(jnp.int32, (ROWS, EDGE), 1)
    row = lax.broadcasted_iota(jnp.int32, (ROWS, EDGE), 0)
    for block, lanes, from_side, at, n in (
        (0, slice(0, EDGE), slice(0, EDGE), 0, 10),
        (3, slice(FROM_R, COLS), slice(EDGE, 2 * EDGE), EDGE - 1, 13),
    ):
        x = jnp.where(row == 0, seams[2:3, lanes], side[:, from_side])
        x = jnp.where(row == ROWS - 1, seams[5:6, lanes], x)
        put_dens(block, jnp.where(lane == at, column(n), x))
    lane = lax.broadcasted_iota(jnp.int32, (ROWS, 2 * EDGE), 1)
    known = jnp.logical_and(lane != EDGE - 1, lane != EDGE)
    before = (cols_hi[0:KW, :], cols_lo[0:KW, :])
    after = (cols_hi[KW : 2 * KW, :], cols_lo[KW : 2 * KW, :])

    def table_row(n):
        base = n // 16 * 16
        rows = cols_hi[base : base + 16, :].astype(F32) + cols_lo[base : base + 16, :].astype(F32)
        return rows[n - base : n - base + 1, :]

    low = jnp.where(known, jnp.concatenate([left[0:ROWS, :], mixed[:, 0:EDGE]], axis=1), 0.0)
    low = cong[:, 0:256] + product(split(low), before)
    low = low + (column(1) * table_row(EDGE - 1) + column(2) * table_row(EDGE))
    half = lax.broadcasted_iota(jnp.int32, (ROWS, EDGE), 1)
    put_value(1, inner[:, EDGE : 2 * EDGE] + DT * low[:, EDGE : 2 * EDGE])
    put_value(0, jnp.where(half == 0, column(18), inner[:, 0:EDGE]) + DT * low[:, 0:EDGE])
    high = jnp.where(known, jnp.concatenate([mixed[:, EDGE : 2 * EDGE], right[0:ROWS, :]], axis=1), 0.0)
    high = cong[:, 256:512] + product(split(high), after)
    high = high + (column(5) * table_row(KW + EDGE - 1) + column(6) * table_row(KW + EDGE))
    put_value(2, inner[:, FROM_R - EDGE : FROM_R] + DT * high[:, 0:EDGE])
    put_value(
        3, jnp.where(half == EDGE - 1, column(21), inner[:, FROM_R:COLS]) + DT * high[:, EDGE : 2 * EDGE]
    )


FINISH_SCRATCH = [
    pltpu.VMEM((8, TALL), F32),
    pltpu.VMEM((8, TALL), F32),
    pltpu.VMEM((128, ROWS), F32),
]


def next_sides_kernel(*refs):
    dens, value = refs[15:17]
    starts = (0, EDGE, FROM_R - EDGE, FROM_R)

    def put(ref):
        def store(block, x):
            ref[:, starts[block] : starts[block] + EDGE] = x

        return store

    finish(*refs[:13], put(dens), put(value), *refs[21:])
    prepare_sides(dens, value, *refs[17:21])


def last_sides_kernel(*refs):
    dens_out, value_out = refs[15:17]
    dens_s, value_s, dens_t, value_t, turn, semaphores = refs[17:]
    starts = (0, EDGE, FROM_R - EDGE, FROM_R)
    copies = []

    def put(sides, out):
        def store(block, x):
            lanes = slice(EDGE * block, EDGE * block + EDGE)
            sides[:, lanes] = x
            target = out.at[:, starts[block] : starts[block] + EDGE]
            copy = pltpu.make_async_copy(sides.at[:, lanes], target, semaphores.at[len(copies)])
            copy.start()
            copies.append(copy)

        return store

    finish(*refs[:13], put(dens_s, dens_out), put(value_s, value_out), dens_t, value_t, turn)
    for copy in copies:
        copy.wait()


def row_pairs(count, first):
    pairs = []
    for a in range(first, count, 2):
        b = (a + 1) % count
        pairs += [(a, b), (b, a)]
    return pairs


def body(density, value_field, potential, kern_rows, kern_cols):
    n_rows = lax.axis_size("rows")
    n_cols = lax.axis_size("cols")
    far_pairs = row_pairs(n_rows, 1)
    near_pairs = row_pairs(n_rows, 0)
    to_right = [(c, (c + 1) % n_cols) for c in range(n_cols)]
    to_left = [(c, (c - 1) % n_cols) for c in range(n_cols)]
    dens, value, side, own_t, far_1, near_1 = call(
        first_sides_kernel,
        [BLOCK, BLOCK] + FIRST,
        [pltpu.SemaphoreType.DMA((8,))],
        1,
        density, value_field,
        hbm_in=(0, 1),
        mib=FIRST_MIB,
    )
    for step_index in range(STEPS):
        last = step_index == STEPS - 1
        new, far_2, near_2 = call(rest_kernel, SECOND, [], 1, dens, value)
        if step_index == 0:
            table = call(rows_table_kernel, ROWS_TABLE + TURNED_TABLE, [], TABLE_COST, kern_rows[None])
            rows_table, turned_table = table[0:2], table[2:4]
        far_1 = lax.ppermute(far_1, "rows", far_pairs)
        near_1 = lax.ppermute(near_1, "rows", near_pairs)
        far_2 = lax.ppermute(far_2, "rows", far_pairs)
        near_2 = lax.ppermute(near_2, "rows", near_pairs)
        left, right, seams, around, tall, mixed = call(
            edge_kernel,
            [shape(COL_ROWS, EDGE), shape(COL_ROWS, EDGE), shape(8, COLS), shape(8, COLS), shape(8, TALL), shape(ROWS, 2 * EDGE)],
            [pltpu.VMEM((8, COLS), F32), pltpu.VMEM((2 * KW, 2 * EDGE), F32)],
            EDGE_COST,
            dens, value, side, own_t, far_1, near_1, *rows_table,
        )
        right_in = lax.ppermute(left, "cols", to_left)
        left_in = lax.ppermute(right, "cols", to_right)
        scratch = [
            pltpu.VMEM((2 * KW, MID), F32),
            pltpu.VMEM((ROWS, MID), BF16),
            pltpu.VMEM((ROWS, MID), BF16),
            pltpu.VMEM((ROWS, INSIDE_N), F32),
        ]
        if last:
            scratch += [pltpu.VMEM((ROWS, INSIDE_N), F32), pltpu.SemaphoreType.DMA((2,))]
        if last:
            cong, inner, cost_t, *results = call(
                last_middle_kernel,
                [shape(ROWS, 4 * EDGE), BLOCK, shape(8, ROWS), BLOCK, BLOCK],
                scratch,
                3,
                new, seams, far_2, near_2, *rows_table, *cols_table, value, potential, around,
                hbm_out=(3, 4),
            )
        else:
            cong, inner, cost_t, dens_out, value_out, *cols_table = call(
                first_middle_kernel,
                [shape(ROWS, 4 * EDGE), BLOCK, shape(8, ROWS), BLOCK, BLOCK] + TURNED_TABLE,
                scratch,
                3,
                new, seams, far_2, near_2, *rows_table, kern_cols[None], value, potential, around,
            )
            results = [dens_out, value_out]
        operands = (cost_t, side, seams, tall, left_in, right_in, mixed, cong, inner, *turned_table, *cols_table, *results)
        if last:
            scratch = [pltpu.VMEM((ROWS, 4 * EDGE), F32), pltpu.VMEM((ROWS, 4 * EDGE), F32)]
            return tuple(
                call(
                    last_sides_kernel,
                    [BLOCK, BLOCK],
                    scratch + FINISH_SCRATCH + [pltpu.SemaphoreType.DMA((6,))],
                    1,
                    *operands,
                    hbm_in=(13, 14),
                    hbm_out=(0, 1),
                    aliases={13: 0, 14: 1},
                )
            )
        dens, value, side, own_t, far_1, near_1 = call(
            next_sides_kernel, [BLOCK, BLOCK] + FIRST, FINISH_SCRATCH, 1, *operands, aliases={13: 0, 14: 1}
        )


def solution(mesh):
    placed = (P("rows", "cols"), P("rows", "cols"), P("rows", "cols"), P(), P())
    return jax.shard_map(
        body,
        mesh=mesh,
        in_specs=placed,
        out_specs=(P("rows", "cols"), P("rows", "cols")),
        check_vma=False,
    )
```

```python
import functools

import jax
import jax.numpy as jnp
from jax import lax
from jax.experimental import pallas as pl
from jax.experimental.pallas import tpu as pltpu
from jax.sharding import PartitionSpec as P

STEPS = 2
EDGE_COST = 6
TABLE_COST = 0.3
FIRST_MIB = 51
NU = 0.5
DT = 0.1

ROWS = 256
COLS = 1024
KW = 256
HALF = KW // 2
EDGE = 128
MID = COLS - 2 * EDGE
FROM_R = COLS - EDGE
RAW_AT = HALF
TURNED_AT = RAW_AT + 16
FIRST_ROWS = TURNED_AT + 8
TALL = 3 * ROWS
SEGMENTS = TALL // EDGE
COL_ROWS = ROWS + 4 * SEGMENTS

VMEM = pl.BlockSpec(memory_space=pltpu.VMEM)
HBM = pl.BlockSpec(memory_space=pltpu.HBM)
F32 = jnp.float32
BF16 = jnp.bfloat16


def shape(*dims, kind=F32):
    return jax.ShapeDtypeStruct(dims, kind)


def call(kernel, out_shapes, scratch, micros, *operands, hbm_in=(), hbm_out=(), aliases=None, mib=24):
    return pl.pallas_call(
        kernel,
        out_shape=out_shapes,
        in_specs=[HBM if n in hbm_in else VMEM for n in range(len(operands))],
        out_specs=[HBM if n in hbm_out else VMEM for n in range(len(out_shapes))],
        scratch_shapes=scratch,
        input_output_aliases=aliases or {},
        compiler_params=pltpu.CompilerParams(vmem_limit_bytes=mib * 1024 * 1024),
        cost_estimate=pl.CostEstimate(
            flops=int(micros * 10**9), bytes_accessed=int(micros * 3 * 10**6), transcendentals=0
        ),
    )(*operands)


def core_index():
    return lax.rem(lax.axis_index("rows"), 2)


def split(x):
    hi = x.astype(BF16)
    return hi, (x - hi.astype(F32)).astype(BF16)


def product(left, right):
    dot = functools.partial(jnp.dot, preferred_element_type=F32)
    return dot(left[0], right[0]) + (dot(left[1], right[0]) + dot(left[0], right[1]))


def put_split(refs, x):
    refs[0][...], refs[1][...] = split(x)


def band(kern, turned, rows=None):
    row = jnp.concatenate([jnp.zeros((1, 2 * KW), F32), kern[...]], axis=1)
    full = jnp.broadcast_to(row, (2 * KW, 3 * KW))
    table = pltpu.roll(full, 0, 1, stride=1, stride_axis=0)[:, :KW]
    put_split(turned, table)
    if rows is not None:
        put_split(rows, table.T)


ROWS_TABLE = [shape(KW, 2 * KW, kind=BF16)] * 2
TURNED_TABLE = [shape(2 * KW, KW, kind=BF16)] * 2


def flux(a, here, there):
    c = DT * NU
    a = DT * a
    return here * jnp.maximum(a + c, c) + there * jnp.minimum(a - c, -c)


def eight_rows(m, u):
    width = m.shape[1]
    flux_x = flux(u - pltpu.roll(u, 7, 0), m, pltpu.roll(m, 7, 0))
    flux_y = flux(u - pltpu.roll(u, width - 1, 1), m, pltpu.roll(m, width - 1, 1))
    return m - ((flux_x - pltpu.roll(flux_x, 1, 0)) + (flux_y - pltpu.roll(flux_y, 1, 1)))


def middle_density(dens, value, out):
    own = slice(EDGE, FROM_R)
    tall = 64

    def step(i, flux_before):
        rows = pl.ds(pl.multiple_of(tall * i, tall), tall)
        after = pl.ds(pl.multiple_of(jnp.minimum(tall * i + tall, ROWS - 8), 8), 8)
        m_all = dens[rows, :]
        u_all = value[rows, :]
        m = m_all[:, own]
        u = u_all[:, own]
        m_down = jnp.concatenate([m[1:], dens[after, own][0:1]], axis=0)
        u_down = jnp.concatenate([u[1:], value[after, own][0:1]], axis=0)
        flux_x = flux(u - u_down, m, m_down)
        flux_up = jnp.concatenate([flux_before, flux_x[:-1]], axis=0)
        u_right = pltpu.roll(u_all, COLS - 1, 1)[:, 0:FROM_R]
        m_right = pltpu.roll(m_all, COLS - 1, 1)[:, 0:FROM_R]
        flux_y = flux(u_all[:, 0:FROM_R] - u_right, m_all[:, 0:FROM_R], m_right)
        flux_left = pltpu.roll(flux_y, 1, 1)[:, own]
        out[rows, :] = m - ((flux_x - flux_up) + (flux_y[:, own] - flux_left))
        return flux_x[-1:]

    lax.fori_loop(0, ROWS // tall, step, jnp.zeros((1, MID), F32))


def inner_value(value, potential, out):
    tall = 32

    def step(i, before):
        rows = pl.ds(pl.multiple_of(tall * i, tall), tall)
        after = pl.ds(pl.multiple_of(jnp.minimum(tall * i + tall, ROWS - 8), 8), 8)
        u = value[rows, :]
        down = jnp.concatenate([u[1:], value[after, :][0:1]], axis=0) - u
        up = jnp.concatenate([before, down[:-1]], axis=0)
        right = pltpu.roll(u, COLS - 1, 1) - u
        left = pltpu.roll(right, 1, 1)
        out[rows, :] = value_formula(u, down, up, right, left, potential[rows, :])
        return down[-1:]

    lax.fori_loop(0, ROWS // tall, step, jnp.zeros((1, COLS), F32), unroll=4)


def end_rows(value, potential, around, out):
    sub = lax.broadcasted_iota(jnp.int32, (8, COLS), 0)
    for rows, at, halo in ((slice(0, 8), 0, 1), (slice(ROWS - 8, ROWS), 7, 6)):
        u = value[rows, :]
        there = around[halo : halo + 1, :]
        down = pltpu.roll(u, 7, 0)
        up = pltpu.roll(u, 1, 0)
        if at == 0:
            up = jnp.where(sub == 0, there, up)
        else:
            down = jnp.where(sub == 7, there, down)
        right = pltpu.roll(u, COLS - 1, 1) - u
        result = value_formula(u, down - u, u - up, right, pltpu.roll(right, 1, 1), potential[rows, :])
        out[rows.start + at : rows.start + at + 1, :] = result[at : at + 1, :]


def value_formula(u, down, up, right, left, cost):
    grad_sq = (
        jnp.square(jnp.maximum(up, 0.0))
        + jnp.square(jnp.minimum(down, 0.0))
        + jnp.square(jnp.maximum(left, 0.0))
        + jnp.square(jnp.minimum(right, 0.0))
    )
    lap = (down - up) + (right - left)
    return u + DT * (NU * lap - 0.5 * grad_sq + cost)


def side_density(dens, value, out):
    lane = lax.broadcasted_iota(jnp.int32, (ROWS, EDGE), 1)
    blocks = [slice(at, at + EDGE) for at in (0, EDGE, FROM_R - EDGE, FROM_R)]

    def right(ref, here):
        there = pltpu.roll(ref[:, blocks[1]], EDGE - 1, 1)
        return jnp.where(lane == EDGE - 1, there, pltpu.roll(here, EDGE - 1, 1))

    def left(ref, here):
        there = pltpu.roll(ref[:, blocks[2]], 1, 1)
        return jnp.where(lane == 0, there, pltpu.roll(here, 1, 1))

    for n in (0, 3):
        m = dens[:, blocks[n]]
        u = value[:, blocks[n]]
        flux_x = flux(u - pltpu.roll(u, ROWS - 1, 0), m, pltpu.roll(m, ROWS - 1, 0))
        flux_up = pltpu.roll(flux_x, 1, 0)
        if n == 0:
            flux_right = flux(u - right(value, u), m, right(dens, m))
            flux_left = pltpu.roll(flux_right, 1, 1)
        else:
            flux_left = flux(left(value, u) - u, left(dens, m), m)
            flux_right = pltpu.roll(flux_left, EDGE - 1, 1)
        at = slice(0, EDGE) if n == 0 else slice(EDGE, 2 * EDGE)
        out[:, at] = m - ((flux_x - flux_up) + (flux_right - flux_left))


def prepare_sides(dens, value, side, own_t, far, near, wait_middle=None):
    core = core_index()
    side_density(dens, value, side)
    if wait_middle is not None:
        wait_middle()
    for n, ref in enumerate((dens, value)):
        own_t[4 * n : 4 * n + 2, :] = ref[:, 0:EDGE].T[0:2, :]
        own_t[4 * n + 2 : 4 * n + 4, :] = ref[:, FROM_R:COLS].T[EDGE - 2 : EDGE, :]
    for one, bottom in ((far, core), (near, 1 - core)):
        one[0:HALF, :] = side[pl.ds(pl.multiple_of(bottom * HALF, 8), HALF), :]
        for n, ref in enumerate((dens, value)):
            eight = ref[pl.ds(pl.multiple_of(bottom * (ROWS - 8), 8), 8), :]
            pair = jnp.where(bottom == 1, eight[6:8, :], eight[0:2, :])
            for q in range(COLS // 256):
                at = RAW_AT + 4 * q + 2 * n
                one[at : at + 2, :] = pair[:, 256 * q : 256 * q + 256]
        one[TURNED_AT:FIRST_ROWS, :] = own_t[...]


def rest_kernel(dens, value, new, far, near):
    core = core_index()
    middle_density(dens, value, new)
    for two, bottom in ((far, core), (near, 1 - core)):
        two[...] = new[pl.ds(pl.multiple_of(bottom * HALF, 8), HALF), :]


FIRST = [
    shape(ROWS, 2 * EDGE),
    shape(8, ROWS),
    shape(FIRST_ROWS, 2 * EDGE),
    shape(FIRST_ROWS, 2 * EDGE),
]
SECOND = [shape(ROWS, MID), shape(HALF, MID), shape(HALF, MID)]
BLOCK = shape(ROWS, COLS)


def first_sides_kernel(dens_in, value_in, dens, value, side, own_t, far, near, semaphores):
    outer = []
    inner = []
    quarter = 2 * EDGE
    for q in (0, 3, 1, 2):
        lanes = slice(quarter * q, quarter * q + quarter)
        for source, target in ((dens_in, dens), (value_in, value)):
            copies = outer if q in (0, 3) else inner
            n = len(outer) + len(inner)
            copies.append(pltpu.make_async_copy(source.at[:, lanes], target.at[:, lanes], semaphores.at[n]))
    for copy in outer + inner:
        copy.start()
    for copy in outer:
        copy.wait()

    def wait_middle():
        for copy in inner:
            copy.wait()

    prepare_sides(dens, value, side, own_t, far, near, wait_middle)


def turned_cost(potential, cost_t):
    cost_t[0:2, :] = potential[:, 0:EDGE].T[0:2, :]
    cost_t[2:4, :] = potential[:, FROM_R:COLS].T[EDGE - 2 : EDGE, :]


def rows_table_kernel(kern_rows, *table):
    band(kern_rows, table[2:4], table[0:2])


def halo_rows(ext, far, near):
    core = core_index()
    ext[pl.ds(pl.multiple_of(core * (HALF + ROWS), 8), HALF), :] = far
    ext[pl.ds(pl.multiple_of((1 - core) * (HALF + ROWS), 8), HALF), :] = near


def edge_kernel(
    dens, value, side, own_t, far, near, rows_hi, rows_lo,
    to_left, to_right, seams, around, tall, mixed, dens_8, ext,
):
    core = core_index()
    for ref, own, n in ((dens_8, dens, 0), (around, value, 1)):
        for q in range(COLS // 256):
            lanes = slice(256 * q, 256 * q + 256)
            at = RAW_AT + 4 * q + 2 * n
            f = far[at : at + 2, :]
            g = near[at : at + 2, :]
            ref[0:2, lanes] = jnp.where(core == 0, f, g)
            ref[6:8, lanes] = jnp.where(core == 0, g, f)
        ref[2:4, :] = own[0:2, :]
        ref[4:6, :] = own[ROWS - 2 : ROWS, :]
    seam = eight_rows(dens_8[...], around[...])
    seams[...] = seam
    f = far[TURNED_AT:FIRST_ROWS, :]
    g = near[TURNED_AT:FIRST_ROWS, :]
    tall[:, 0:ROWS] = jnp.where(core == 0, f, g)
    tall[:, ROWS : 2 * ROWS] = own_t[...]
    tall[:, 2 * ROWS : TALL] = jnp.where(core == 0, g, f)

    halo_rows(ext, far[0:HALF, :], near[0:HALF, :])
    ext[HALF : HALF + ROWS, :] = side[...]
    put_seams(ext, seams, ((slice(0, EDGE), slice(0, EDGE)), (slice(EDGE, 2 * EDGE), slice(FROM_R, COLS))))
    result = product((rows_hi[...], rows_lo[...]), split(ext[...]))
    mixed[...] = result
    for ref, lanes, at in ((to_left, slice(0, EDGE), 0), (to_right, slice(EDGE, 2 * EDGE), 2)):
        ref[0:ROWS, :] = result[:, lanes]
        for q in range(SEGMENTS):
            segment = slice(EDGE * q, EDGE * q + EDGE)
            ref[ROWS + 4 * q : ROWS + 4 * q + 2, :] = tall[at : at + 2, segment]
            ref[ROWS + 4 * q + 2 : ROWS + 4 * q + 4, :] = tall[at + 4 : at + 6, segment]


def put_seams(ext, seams, lane_pairs):
    for to, source in lane_pairs:
        ext[HALF - 1 : HALF, to] = seams[1:2, source]
        ext[HALF : HALF + 1, to] = seams[2:3, source]
        ext[HALF + ROWS - 1 : HALF + ROWS, to] = seams[5:6, source]
        ext[HALF + ROWS : HALF + ROWS + 1, to] = seams[6:7, source]


def middle_mix(
    new, seams, far, near, rows_hi, rows_lo, cols_hi, cols_lo, cong_s, cong_m, ext, mix_hi, mix_lo
):
    rows = (rows_hi[...], rows_lo[...])
    for b in range(MID // 256):
        lanes = slice(256 * b, 256 * b + 256)
        mix_hi[:, lanes], mix_lo[:, lanes] = split(product(rows, split(ext[:, lanes])))
    before = (cols_hi[0:KW, :], cols_lo[0:KW, :])
    after = (cols_hi[KW : 2 * KW, :], cols_lo[KW : 2 * KW, :])
    for b in range(COLS // 256):
        total = None
        for block, table in ((b - 1, before), (b, after)):
            if 0 <= block < MID // 256:
                lanes = slice(256 * block, 256 * block + 256)
                part = product((mix_hi[:, lanes], mix_lo[:, lanes]), table)
                total = part if total is None else total + part
        if b == 0:
            cong_s[:, 0:256] = total
        elif b == COLS // 256 - 1:
            cong_s[:, 256:512] = total
        else:
            cong_m[:, 256 * (b - 1) : 256 * b] = total


INSIDE = slice(2 * EDGE, COLS - 2 * EDGE)
INSIDE_N = COLS - 4 * EDGE


def middle_ext(new, seams, far, near, ext):
    halo_rows(ext, far[...], near[...])
    ext[HALF : HALF + ROWS, :] = new[...]
    put_seams(ext, seams, ((slice(0, MID), slice(EDGE, FROM_R)),))


def first_middle_kernel(*refs):
    new, seams, far, near, rows_hi, rows_lo, kern_cols, value, potential, around = refs[:10]
    cong_s, inner, cost_t, dens_out, value_out, cols_hi, cols_lo, ext, mix_hi, mix_lo, cong_m = refs[10:]
    band(kern_cols, (cols_hi, cols_lo))
    table = (rows_hi, rows_lo, cols_hi, cols_lo)
    middle_ext(new, seams, far, near, ext)
    middle_mix(new, seams, far, near, *table, cong_s, cong_m, ext, mix_hi, mix_lo)
    turned_cost(potential, cost_t)
    inner_value(value, potential, inner)
    end_rows(value, potential, around, inner)
    dens_out[:, EDGE:FROM_R] = ext[HALF : HALF + ROWS, :]
    value_out[:, INSIDE] = inner[:, INSIDE] + DT * cong_m[...]


def last_middle_kernel(*refs):
    new, seams, far, near = refs[:4]
    value, potential, around = refs[8:11]
    cong_s, inner, cost_t, dens_out, value_out, ext, mix_hi, mix_lo, cong_m, value_mid, semaphores = refs[11:]
    middle_ext(new, seams, far, near, ext)
    dens_copy = pltpu.make_async_copy(
        ext.at[HALF : HALF + ROWS, :], dens_out.at[:, EDGE:FROM_R], semaphores.at[0]
    )
    dens_copy.start()
    middle_mix(*refs[:8], cong_s, cong_m, ext, mix_hi, mix_lo)
    turned_cost(potential, cost_t)
    inner_value(value, potential, inner)
    end_rows(value, potential, around, inner)
    value_mid[...] = inner[:, INSIDE] + DT * cong_m[...]
    value_copy = pltpu.make_async_copy(value_mid, value_out.at[:, INSIDE], semaphores.at[1])
    value_copy.start()
    dens_copy.wait()
    value_copy.wait()


def finish(
    cost_t, side, seams, tall, right, left, mixed, cong, inner, turned_hi, turned_lo, cols_hi, cols_lo,
    put_dens, put_value, dens_t, value_t, turn,
):
    for ref, n in ((dens_t, 0), (value_t, 1)):
        for q in range(SEGMENTS):
            lanes = slice(EDGE * q, EDGE * q + EDGE)
            at = ROWS + 4 * q + 2 * n
            ref[0:2, lanes] = left[at : at + 2, :]
            ref[6:8, lanes] = right[at : at + 2, :]
        ref[2:6, :] = tall[4 * n : 4 * n + 4, :]
    u = value_t[...]
    new_t = eight_rows(dens_t[...], u)
    window = new_t[:, HALF : HALF + 2 * KW]
    window = jnp.concatenate([window, window], axis=0)
    turn[0:8, :] = product(split(window), (turned_hi[...], turned_lo[...]))[0:8, :]
    own = slice(ROWS, 2 * ROWS)
    turn[8:16, :] = new_t[:, own]
    right_t = pltpu.roll(u, 7, 0) - u
    left_t = u - pltpu.roll(u, 1, 0)
    down_t = pltpu.roll(u, TALL - 1, 1) - u
    up_t = u - pltpu.roll(u, 1, 1)
    cost = jnp.concatenate([cost_t[0:2, :], cost_t[0:4, :], cost_t[2:4, :]], axis=0)
    turn[16:24, :] = value_formula(
        u[:, own], down_t[:, own], up_t[:, own], right_t[:, own], left_t[:, own], cost
    )
    columns = turn[...].T

    def column(n):
        return columns[:, n : n + 1]

    lane = lax.broadcasted_iota(jnp.int32, (ROWS, EDGE), 1)
    row = lax.broadcasted_iota(jnp.int32, (ROWS, EDGE), 0)
    for block, lanes, from_side, at, n in (
        (0, slice(0, EDGE), slice(0, EDGE), 0, 10),
        (3, slice(FROM_R, COLS), slice(EDGE, 2 * EDGE), EDGE - 1, 13),
    ):
        x = jnp.where(row == 0, seams[2:3, lanes], side[:, from_side])
        x = jnp.where(row == ROWS - 1, seams[5:6, lanes], x)
        put_dens(block, jnp.where(lane == at, column(n), x))
    lane = lax.broadcasted_iota(jnp.int32, (ROWS, 2 * EDGE), 1)
    known = jnp.logical_and(lane != EDGE - 1, lane != EDGE)
    before = (cols_hi[0:KW, :], cols_lo[0:KW, :])
    after = (cols_hi[KW : 2 * KW, :], cols_lo[KW : 2 * KW, :])

    def table_row(n):
        base = n // 16 * 16
        rows = cols_hi[base : base + 16, :].astype(F32) + cols_lo[base : base + 16, :].astype(F32)
        return rows[n - base : n - base + 1, :]

    low = jnp.where(known, jnp.concatenate([left[0:ROWS, :], mixed[:, 0:EDGE]], axis=1), 0.0)
    low = cong[:, 0:256] + product(split(low), before)
    low = low + (column(1) * table_row(EDGE - 1) + column(2) * table_row(EDGE))
    half = lax.broadcasted_iota(jnp.int32, (ROWS, EDGE), 1)
    put_value(1, inner[:, EDGE : 2 * EDGE] + DT * low[:, EDGE : 2 * EDGE])
    put_value(0, jnp.where(half == 0, column(18), inner[:, 0:EDGE]) + DT * low[:, 0:EDGE])
    high = jnp.where(known, jnp.concatenate([mixed[:, EDGE : 2 * EDGE], right[0:ROWS, :]], axis=1), 0.0)
    high = cong[:, 256:512] + product(split(high), after)
    high = high + (column(5) * table_row(KW + EDGE - 1) + column(6) * table_row(KW + EDGE))
    put_value(2, inner[:, FROM_R - EDGE : FROM_R] + DT * high[:, 0:EDGE])
    put_value(
        3, jnp.where(half == EDGE - 1, column(21), inner[:, FROM_R:COLS]) + DT * high[:, EDGE : 2 * EDGE]
    )


FINISH_SCRATCH = [
    pltpu.VMEM((8, TALL), F32),
    pltpu.VMEM((8, TALL), F32),
    pltpu.VMEM((128, ROWS), F32),
]


def next_sides_kernel(*refs):
    dens, value = refs[15:17]
    starts = (0, EDGE, FROM_R - EDGE, FROM_R)

    def put(ref):
        def store(block, x):
            ref[:, starts[block] : starts[block] + EDGE] = x

        return store

    finish(*refs[:13], put(dens), put(value), *refs[21:])
    prepare_sides(dens, value, *refs[17:21])


def last_sides_kernel(*refs):
    dens_out, value_out = refs[15:17]
    dens_s, value_s, dens_t, value_t, turn, semaphores = refs[17:]
    starts = (0, EDGE, FROM_R - EDGE, FROM_R)
    copies = []

    def put(sides, out):
        def store(block, x):
            lanes = slice(EDGE * block, EDGE * block + EDGE)
            sides[:, lanes] = x
            target = out.at[:, starts[block] : starts[block] + EDGE]
            copy = pltpu.make_async_copy(sides.at[:, lanes], target, semaphores.at[len(copies)])
            copy.start()
            copies.append(copy)

        return store

    finish(*refs[:13], put(dens_s, dens_out), put(value_s, value_out), dens_t, value_t, turn)
    for copy in copies:
        copy.wait()


def row_pairs(count, first):
    pairs = []
    for a in range(first, count, 2):
        b = (a + 1) % count
        pairs += [(a, b), (b, a)]
    return pairs


def body(density, value_field, potential, kern_rows, kern_cols):
    n_rows = lax.axis_size("rows")
    n_cols = lax.axis_size("cols")
    far_pairs = row_pairs(n_rows, 1)
    near_pairs = row_pairs(n_rows, 0)
    to_right = [(c, (c + 1) % n_cols) for c in range(n_cols)]
    to_left = [(c, (c - 1) % n_cols) for c in range(n_cols)]
    dens, value, side, own_t, far_1, near_1 = call(
        first_sides_kernel,
        [BLOCK, BLOCK] + FIRST,
        [pltpu.SemaphoreType.DMA((8,))],
        1,
        density, value_field,
        hbm_in=(0, 1),
        mib=FIRST_MIB,
    )
    for step_index in range(STEPS):
        last = step_index == STEPS - 1
        new, far_2, near_2 = call(rest_kernel, SECOND, [], 1, dens, value)
        if step_index == 0:
            table = call(rows_table_kernel, ROWS_TABLE + TURNED_TABLE, [], TABLE_COST, kern_rows[None])
            rows_table, turned_table = table[0:2], table[2:4]
        far_1 = lax.ppermute(far_1, "rows", far_pairs)
        near_1 = lax.ppermute(near_1, "rows", near_pairs)
        far_2 = lax.ppermute(far_2, "rows", far_pairs)
        near_2 = lax.ppermute(near_2, "rows", near_pairs)
        left, right, seams, around, tall, mixed = call(
            edge_kernel,
            [shape(COL_ROWS, EDGE), shape(COL_ROWS, EDGE), shape(8, COLS), shape(8, COLS), shape(8, TALL), shape(ROWS, 2 * EDGE)],
            [pltpu.VMEM((8, COLS), F32), pltpu.VMEM((2 * KW, 2 * EDGE), F32)],
            EDGE_COST,
            dens, value, side, own_t, far_1, near_1, *rows_table,
        )
        right_in = lax.ppermute(left, "cols", to_left)
        left_in = lax.ppermute(right, "cols", to_right)
        scratch = [
            pltpu.VMEM((2 * KW, MID), F32),
            pltpu.VMEM((ROWS, MID), BF16),
            pltpu.VMEM((ROWS, MID), BF16),
            pltpu.VMEM((ROWS, INSIDE_N), F32),
        ]
        if last:
            scratch += [pltpu.VMEM((ROWS, INSIDE_N), F32), pltpu.SemaphoreType.DMA((2,))]
        if last:
            cong, inner, cost_t, *results = call(
                last_middle_kernel,
                [shape(ROWS, 4 * EDGE), BLOCK, shape(8, ROWS), BLOCK, BLOCK],
                scratch,
                3,
                new, seams, far_2, near_2, *rows_table, *cols_table, value, potential, around,
                hbm_out=(3, 4),
            )
        else:
            cong, inner, cost_t, dens_out, value_out, *cols_table = call(
                first_middle_kernel,
                [shape(ROWS, 4 * EDGE), BLOCK, shape(8, ROWS), BLOCK, BLOCK] + TURNED_TABLE,
                scratch,
                3,
                new, seams, far_2, near_2, *rows_table, kern_cols[None], value, potential, around,
            )
            results = [dens_out, value_out]
        operands = (cost_t, side, seams, tall, right_in, left_in, mixed, cong, inner, *turned_table, *cols_table, *results)
        if last:
            scratch = [pltpu.VMEM((ROWS, 4 * EDGE), F32), pltpu.VMEM((ROWS, 4 * EDGE), F32)]
            return tuple(
                call(
                    last_sides_kernel,
                    [BLOCK, BLOCK],
                    scratch + FINISH_SCRATCH + [pltpu.SemaphoreType.DMA((6,))],
                    1,
                    *operands,
                    hbm_in=(13, 14),
                    hbm_out=(0, 1),
                    aliases={13: 0, 14: 1},
                )
            )
        dens, value, side, own_t, far_1, near_1 = call(
            next_sides_kernel, [BLOCK, BLOCK] + FIRST, FINISH_SCRATCH, 1, *operands, aliases={13: 0, 14: 1}
        )


def solution(mesh):
    placed = (P("rows", "cols"), P("rows", "cols"), P("rows", "cols"), P(), P())
    return jax.shard_map(
        body,
        mesh=mesh,
        in_specs=placed,
        out_specs=(P("rows", "cols"), P("rows", "cols")),
        check_vma=False,
    )
```

```python
import functools

import jax
import jax.numpy as jnp
from jax import lax
from jax.experimental import pallas as pl
from jax.experimental.pallas import tpu as pltpu
from jax.sharding import PartitionSpec as P

STEPS = 2
EDGE_COST = 6
TABLE_COST = 0.3
FIRST_MIB = 51
NU = 0.5
DT = 0.1

ROWS = 256
COLS = 1024
KW = 256
HALF = KW // 2
EDGE = 128
MID = COLS - 2 * EDGE
FROM_R = COLS - EDGE
RAW_AT = HALF
TURNED_AT = RAW_AT + 16
FIRST_ROWS = TURNED_AT + 8
TALL = 3 * ROWS
SEGMENTS = TALL // EDGE
COL_ROWS = ROWS + 4 * SEGMENTS

VMEM = pl.BlockSpec(memory_space=pltpu.VMEM)
HBM = pl.BlockSpec(memory_space=pltpu.HBM)
F32 = jnp.float32
BF16 = jnp.bfloat16


def shape(*dims, kind=F32):
    return jax.ShapeDtypeStruct(dims, kind)


def call(kernel, out_shapes, scratch, micros, *operands, hbm_in=(), hbm_out=(), aliases=None, mib=24):
    return pl.pallas_call(
        kernel,
        out_shape=out_shapes,
        in_specs=[HBM if n in hbm_in else VMEM for n in range(len(operands))],
        out_specs=[HBM if n in hbm_out else VMEM for n in range(len(out_shapes))],
        scratch_shapes=scratch,
        input_output_aliases=aliases or {},
        compiler_params=pltpu.CompilerParams(vmem_limit_bytes=mib * 1024 * 1024),
        cost_estimate=pl.CostEstimate(
            flops=int(micros * 10**9), bytes_accessed=int(micros * 3 * 10**6), transcendentals=0
        ),
    )(*operands)


def core_index():
    return lax.rem(lax.axis_index("rows"), 2)


def split(x):
    hi = x.astype(BF16)
    return hi, (x - hi.astype(F32)).astype(BF16)


def product(left, right):
    dot = functools.partial(jnp.dot, preferred_element_type=F32)
    return dot(left[0], right[0]) + (dot(left[1], right[0]) + dot(left[0], right[1]))


def put_split(refs, x):
    refs[0][...], refs[1][...] = split(x)


def band(kern, turned, rows=None):
    row = jnp.concatenate([jnp.zeros((1, 2 * KW), F32), kern[...]], axis=1)
    full = jnp.broadcast_to(row, (2 * KW, 3 * KW))
    table = pltpu.roll(full, 0, 1, stride=1, stride_axis=0)[:, :KW]
    put_split(turned, table)
    if rows is not None:
        put_split(rows, table.T)


ROWS_TABLE = [shape(KW, 2 * KW, kind=BF16)] * 2
TURNED_TABLE = [shape(2 * KW, KW, kind=BF16)] * 2


def flux(a, here, there):
    c = DT * NU
    a = DT * a
    return here * jnp.maximum(a + c, c) + there * jnp.minimum(a - c, -c)


def eight_rows(m, u):
    width = m.shape[1]
    flux_x = flux(u - pltpu.roll(u, 7, 0), m, pltpu.roll(m, 7, 0))
    flux_y = flux(u - pltpu.roll(u, width - 1, 1), m, pltpu.roll(m, width - 1, 1))
    return m - ((flux_x - pltpu.roll(flux_x, 1, 0)) + (flux_y - pltpu.roll(flux_y, 1, 1)))


def middle_density(dens, value, out):
    own = slice(EDGE, FROM_R)
    tall = 64

    def step(i, flux_before):
        rows = pl.ds(pl.multiple_of(tall * i, tall), tall)
        after = pl.ds(pl.multiple_of(jnp.minimum(tall * i + tall, ROWS - 8), 8), 8)
        m_all = dens[rows, :]
        u_all = value[rows, :]
        m = m_all[:, own]
        u = u_all[:, own]
        m_down = jnp.concatenate([m[1:], dens[after, own][0:1]], axis=0)
        u_down = jnp.concatenate([u[1:], value[after, own][0:1]], axis=0)
        flux_x = flux(u - u_down, m, m_down)
        flux_up = jnp.concatenate([flux_before, flux_x[:-1]], axis=0)
        u_right = pltpu.roll(u_all, COLS - 1, 1)[:, 0:FROM_R]
        m_right = pltpu.roll(m_all, COLS - 1, 1)[:, 0:FROM_R]
        flux_y = flux(u_all[:, 0:FROM_R] - u_right, m_all[:, 0:FROM_R], m_right)
        flux_left = pltpu.roll(flux_y, 1, 1)[:, own]
        out[rows, :] = m - ((flux_x - flux_up) + (flux_y[:, own] - flux_left))
        return flux_x[-1:]

    lax.fori_loop(0, ROWS // tall, step, jnp.zeros((1, MID), F32))


def inner_value(value, potential, out):
    tall = 32

    def step(i, before):
        rows = pl.ds(pl.multiple_of(tall * i, tall), tall)
        after = pl.ds(pl.multiple_of(jnp.minimum(tall * i + tall, ROWS - 8), 8), 8)
        u = value[rows, :]
        down = jnp.concatenate([u[1:], value[after, :][0:1]], axis=0) - u
        up = jnp.concatenate([before, down[:-1]], axis=0)
        right = pltpu.roll(u, COLS - 1, 1) - u
        left = pltpu.roll(right, 1, 1)
        out[rows, :] = value_formula(u, down, up, right, left, potential[rows, :])
        return down[-1:]

    lax.fori_loop(0, ROWS // tall, step, jnp.zeros((1, COLS), F32), unroll=4)


def end_rows(value, potential, around, out):
    sub = lax.broadcasted_iota(jnp.int32, (8, COLS), 0)
    for rows, at, halo in ((slice(0, 8), 0, 1), (slice(ROWS - 8, ROWS), 7, 6)):
        u = value[rows, :]
        there = around[halo : halo + 1, :]
        down = pltpu.roll(u, 7, 0)
        up = pltpu.roll(u, 1, 0)
        if at == 0:
            up = jnp.where(sub == 0, there, up)
        else:
            down = jnp.where(sub == 7, there, down)
        right = pltpu.roll(u, COLS - 1, 1) - u
        result = value_formula(u, down - u, u - up, right, pltpu.roll(right, 1, 1), potential[rows, :])
        out[rows.start + at : rows.start + at + 1, :] = result[at : at + 1, :]


def value_formula(u, down, up, right, left, cost):
    grad_sq = (
        jnp.square(jnp.maximum(up, 0.0))
        + jnp.square(jnp.minimum(down, 0.0))
        + jnp.square(jnp.maximum(left, 0.0))
        + jnp.square(jnp.minimum(right, 0.0))
    )
    lap = (down - up) + (right - left)
    return u + DT * (NU * lap - 0.5 * grad_sq + cost)


def side_density(dens, value, out):
    lane = lax.broadcasted_iota(jnp.int32, (ROWS, EDGE), 1)
    blocks = [slice(at, at + EDGE) for at in (0, EDGE, FROM_R - EDGE, FROM_R)]

    def right(ref, here):
        there = pltpu.roll(ref[:, blocks[1]], EDGE - 1, 1)
        return jnp.where(lane == EDGE - 1, there, pltpu.roll(here, EDGE - 1, 1))

    def left(ref, here):
        there = pltpu.roll(ref[:, blocks[2]], 1, 1)
        return jnp.where(lane == 0, there, pltpu.roll(here, 1, 1))

    for n in (0, 3):
        m = dens[:, blocks[n]]
        u = value[:, blocks[n]]
        flux_x = flux(u - pltpu.roll(u, ROWS - 1, 0), m, pltpu.roll(m, ROWS - 1, 0))
        flux_up = pltpu.roll(flux_x, 1, 0)
        if n == 0:
            flux_right = flux(u - right(value, u), m, right(dens, m))
            flux_left = pltpu.roll(flux_right, 1, 1)
        else:
            flux_left = flux(left(value, u) - u, left(dens, m), m)
            flux_right = pltpu.roll(flux_left, EDGE - 1, 1)
        at = slice(0, EDGE) if n == 0 else slice(EDGE, 2 * EDGE)
        out[:, at] = m - ((flux_x - flux_up) + (flux_right - flux_left))


def prepare_sides(dens, value, side, own_t, far, near, wait_middle=None):
    core = core_index()
    side_density(dens, value, side)
    for n, ref in enumerate((dens, value)):
        own_t[4 * n : 4 * n + 2, :] = ref[:, 0:EDGE].T[0:2, :]
        own_t[4 * n + 2 : 4 * n + 4, :] = ref[:, FROM_R:COLS].T[EDGE - 2 : EDGE, :]
    if wait_middle is not None:
        wait_middle()
    for one, bottom in ((far, core), (near, 1 - core)):
        one[0:HALF, :] = side[pl.ds(pl.multiple_of(bottom * HALF, 8), HALF), :]
        for n, ref in enumerate((dens, value)):
            eight = ref[pl.ds(pl.multiple_of(bottom * (ROWS - 8), 8), 8), :]
            pair = jnp.where(bottom == 1, eight[6:8, :], eight[0:2, :])
            for q in range(COLS // 256):
                at = RAW_AT + 4 * q + 2 * n
                one[at : at + 2, :] = pair[:, 256 * q : 256 * q + 256]
        one[TURNED_AT:FIRST_ROWS, :] = own_t[...]


def rest_kernel(dens, value, new, far, near):
    core = core_index()
    middle_density(dens, value, new)
    for two, bottom in ((far, core), (near, 1 - core)):
        two[...] = new[pl.ds(pl.multiple_of(bottom * HALF, 8), HALF), :]


FIRST = [
    shape(ROWS, 2 * EDGE),
    shape(8, ROWS),
    shape(FIRST_ROWS, 2 * EDGE),
    shape(FIRST_ROWS, 2 * EDGE),
]
SECOND = [shape(ROWS, MID), shape(HALF, MID), shape(HALF, MID)]
BLOCK = shape(ROWS, COLS)


def first_sides_kernel(dens_in, value_in, dens, value, side, own_t, far, near, semaphores):
    outer = []
    inner = []
    quarter = 2 * EDGE
    for q in (0, 3, 1, 2):
        lanes = slice(quarter * q, quarter * q + quarter)
        for source, target in ((dens_in, dens), (value_in, value)):
            copies = outer if q in (0, 3) else inner
            n = len(outer) + len(inner)
            copies.append(pltpu.make_async_copy(source.at[:, lanes], target.at[:, lanes], semaphores.at[n]))
    for copy in outer + inner:
        copy.start()
    for copy in outer:
        copy.wait()

    def wait_middle():
        for copy in inner:
            copy.wait()

    prepare_sides(dens, value, side, own_t, far, near, wait_middle)


def turned_cost(potential, cost_t):
    cost_t[0:2, :] = potential[:, 0:EDGE].T[0:2, :]
    cost_t[2:4, :] = potential[:, FROM_R:COLS].T[EDGE - 2 : EDGE, :]


def rows_table_kernel(kern_rows, *table):
    band(kern_rows, table[2:4], table[0:2])


def halo_rows(ext, far, near):
    core = core_index()
    ext[pl.ds(pl.multiple_of(core * (HALF + ROWS), 8), HALF), :] = far
    ext[pl.ds(pl.multiple_of((1 - core) * (HALF + ROWS), 8), HALF), :] = near


def edge_kernel(
    dens, value, side, own_t, far, near, rows_hi, rows_lo,
    to_left, to_right, seams, around, tall, mixed, dens_8, ext,
):
    core = core_index()
    for ref, own, n in ((dens_8, dens, 0), (around, value, 1)):
        for q in range(COLS // 256):
            lanes = slice(256 * q, 256 * q + 256)
            at = RAW_AT + 4 * q + 2 * n
            f = far[at : at + 2, :]
            g = near[at : at + 2, :]
            ref[0:2, lanes] = jnp.where(core == 0, f, g)
            ref[6:8, lanes] = jnp.where(core == 0, g, f)
        ref[2:4, :] = own[0:2, :]
        ref[4:6, :] = own[ROWS - 2 : ROWS, :]
    seam = eight_rows(dens_8[...], around[...])
    seams[...] = seam
    f = far[TURNED_AT:FIRST_ROWS, :]
    g = near[TURNED_AT:FIRST_ROWS, :]
    tall[:, 0:ROWS] = jnp.where(core == 0, f, g)
    tall[:, ROWS : 2 * ROWS] = own_t[...]
    tall[:, 2 * ROWS : TALL] = jnp.where(core == 0, g, f)

    halo_rows(ext, far[0:HALF, :], near[0:HALF, :])
    ext[HALF : HALF + ROWS, :] = side[...]
    put_seams(ext, seams, ((slice(0, EDGE), slice(0, EDGE)), (slice(EDGE, 2 * EDGE), slice(FROM_R, COLS))))
    result = product((rows_hi[...], rows_lo[...]), split(ext[...]))
    mixed[...] = result
    for ref, lanes, at in ((to_left, slice(0, EDGE), 0), (to_right, slice(EDGE, 2 * EDGE), 2)):
        ref[0:ROWS, :] = result[:, lanes]
        for q in range(SEGMENTS):
            segment = slice(EDGE * q, EDGE * q + EDGE)
            ref[ROWS + 4 * q : ROWS + 4 * q + 2, :] = tall[at : at + 2, segment]
            ref[ROWS + 4 * q + 2 : ROWS + 4 * q + 4, :] = tall[at + 4 : at + 6, segment]


def put_seams(ext, seams, lane_pairs):
    for to, source in lane_pairs:
        ext[HALF - 1 : HALF, to] = seams[1:2, source]
        ext[HALF : HALF + 1, to] = seams[2:3, source]
        ext[HALF + ROWS - 1 : HALF + ROWS, to] = seams[5:6, source]
        ext[HALF + ROWS : HALF + ROWS + 1, to] = seams[6:7, source]


def middle_mix(
    new, seams, far, near, rows_hi, rows_lo, cols_hi, cols_lo, cong_s, cong_m, ext, mix_hi, mix_lo
):
    rows = (rows_hi[...], rows_lo[...])
    for b in range(MID // 256):
        lanes = slice(256 * b, 256 * b + 256)
        mix_hi[:, lanes], mix_lo[:, lanes] = split(product(rows, split(ext[:, lanes])))
    before = (cols_hi[0:KW, :], cols_lo[0:KW, :])
    after = (cols_hi[KW : 2 * KW, :], cols_lo[KW : 2 * KW, :])
    for b in range(COLS // 256):
        total = None
        for block, table in ((b - 1, before), (b, after)):
            if 0 <= block < MID // 256:
                lanes = slice(256 * block, 256 * block + 256)
                part = product((mix_hi[:, lanes], mix_lo[:, lanes]), table)
                total = part if total is None else total + part
        if b == 0:
            cong_s[:, 0:256] = total
        elif b == COLS // 256 - 1:
            cong_s[:, 256:512] = total
        else:
            cong_m[:, 256 * (b - 1) : 256 * b] = total


INSIDE = slice(2 * EDGE, COLS - 2 * EDGE)
INSIDE_N = COLS - 4 * EDGE


def middle_ext(new, seams, far, near, ext):
    halo_rows(ext, far[...], near[...])
    ext[HALF : HALF + ROWS, :] = new[...]
    put_seams(ext, seams, ((slice(0, MID), slice(EDGE, FROM_R)),))


def first_middle_kernel(*refs):
    new, seams, far, near, rows_hi, rows_lo, kern_cols, value, potential, around = refs[:10]
    cong_s, inner, cost_t, dens_out, value_out, cols_hi, cols_lo, ext, mix_hi, mix_lo, cong_m = refs[10:]
    band(kern_cols, (cols_hi, cols_lo))
    table = (rows_hi, rows_lo, cols_hi, cols_lo)
    middle_ext(new, seams, far, near, ext)
    middle_mix(new, seams, far, near, *table, cong_s, cong_m, ext, mix_hi, mix_lo)
    turned_cost(potential, cost_t)
    inner_value(value, potential, inner)
    end_rows(value, potential, around, inner)
    dens_out[:, EDGE:FROM_R] = ext[HALF : HALF + ROWS, :]
    value_out[:, INSIDE] = inner[:, INSIDE] + DT * cong_m[...]


def last_middle_kernel(*refs):
    new, seams, far, near = refs[:4]
    value, potential, around = refs[8:11]
    cong_s, inner, cost_t, dens_out, value_out, ext, mix_hi, mix_lo, cong_m, value_mid, semaphores = refs[11:]
    middle_ext(new, seams, far, near, ext)
    dens_copy = pltpu.make_async_copy(
        ext.at[HALF : HALF + ROWS, :], dens_out.at[:, EDGE:FROM_R], semaphores.at[0]
    )
    dens_copy.start()
    middle_mix(*refs[:8], cong_s, cong_m, ext, mix_hi, mix_lo)
    turned_cost(potential, cost_t)
    inner_value(value, potential, inner)
    end_rows(value, potential, around, inner)
    value_mid[...] = inner[:, INSIDE] + DT * cong_m[...]
    value_copy = pltpu.make_async_copy(value_mid, value_out.at[:, INSIDE], semaphores.at[1])
    value_copy.start()
    dens_copy.wait()
    value_copy.wait()


def finish(
    cost_t, side, seams, tall, left, right, mixed, cong, inner, turned_hi, turned_lo, cols_hi, cols_lo,
    put_dens, put_value, dens_t, value_t, turn,
):
    for ref, n in ((dens_t, 0), (value_t, 1)):
        for q in range(SEGMENTS):
            lanes = slice(EDGE * q, EDGE * q + EDGE)
            at = ROWS + 4 * q + 2 * n
            ref[0:2, lanes] = left[at : at + 2, :]
            ref[6:8, lanes] = right[at : at + 2, :]
        ref[2:6, :] = tall[4 * n : 4 * n + 4, :]
    u = value_t[...]
    new_t = eight_rows(dens_t[...], u)
    window = new_t[:, HALF : HALF + 2 * KW]
    window = jnp.concatenate([window, window], axis=0)
    turn[0:8, :] = product(split(window), (turned_hi[...], turned_lo[...]))[0:8, :]
    own = slice(ROWS, 2 * ROWS)
    turn[8:16, :] = new_t[:, own]
    right_t = pltpu.roll(u, 7, 0) - u
    left_t = u - pltpu.roll(u, 1, 0)
    down_t = pltpu.roll(u, TALL - 1, 1) - u
    up_t = u - pltpu.roll(u, 1, 1)
    cost = jnp.concatenate([cost_t[0:2, :], cost_t[0:4, :], cost_t[2:4, :]], axis=0)
    turn[16:24, :] = value_formula(
        u[:, own], down_t[:, own], up_t[:, own], right_t[:, own], left_t[:, own], cost
    )
    columns = turn[...].T

    def column(n):
        return columns[:, n : n + 1]

    lane = lax.broadcasted_iota(jnp.int32, (ROWS, EDGE), 1)
    row = lax.broadcasted_iota(jnp.int32, (ROWS, EDGE), 0)
    for block, lanes, from_side, at, n in (
        (0, slice(0, EDGE), slice(0, EDGE), 0, 10),
        (3, slice(FROM_R, COLS), slice(EDGE, 2 * EDGE), EDGE - 1, 13),
    ):
        x = jnp.where(row == 0, seams[2:3, lanes], side[:, from_side])
        x = jnp.where(row == ROWS - 1, seams[5:6, lanes], x)
        put_dens(block, jnp.where(lane == at, column(n), x))
    lane = lax.broadcasted_iota(jnp.int32, (ROWS, 2 * EDGE), 1)
    known = jnp.logical_and(lane != EDGE - 1, lane != EDGE)
    before = (cols_hi[0:KW, :], cols_lo[0:KW, :])
    after = (cols_hi[KW : 2 * KW, :], cols_lo[KW : 2 * KW, :])

    def table_row(n):
        base = n // 16 * 16
        rows = cols_hi[base : base + 16, :].astype(F32) + cols_lo[base : base + 16, :].astype(F32)
        return rows[n - base : n - base + 1, :]

    low = jnp.where(known, jnp.concatenate([left[0:ROWS, :], mixed[:, 0:EDGE]], axis=1), 0.0)
    low = cong[:, 0:256] + product(split(low), before)
    low = low + (column(1) * table_row(EDGE - 1) + column(2) * table_row(EDGE))
    half = lax.broadcasted_iota(jnp.int32, (ROWS, EDGE), 1)
    put_value(1, inner[:, EDGE : 2 * EDGE] + DT * low[:, EDGE : 2 * EDGE])
    put_value(0, jnp.where(half == 0, column(18), inner[:, 0:EDGE]) + DT * low[:, 0:EDGE])
    high = jnp.where(known, jnp.concatenate([mixed[:, EDGE : 2 * EDGE], right[0:ROWS, :]], axis=1), 0.0)
    high = cong[:, 256:512] + product(split(high), after)
    high = high + (column(5) * table_row(KW + EDGE - 1) + column(6) * table_row(KW + EDGE))
    put_value(2, inner[:, FROM_R - EDGE : FROM_R] + DT * high[:, 0:EDGE])
    put_value(
        3, jnp.where(half == EDGE - 1, column(21), inner[:, FROM_R:COLS]) + DT * high[:, EDGE : 2 * EDGE]
    )


FINISH_SCRATCH = [
    pltpu.VMEM((8, TALL), F32),
    pltpu.VMEM((8, TALL), F32),
    pltpu.VMEM((128, ROWS), F32),
]


def next_sides_kernel(*refs):
    dens, value = refs[15:17]
    starts = (0, EDGE, FROM_R - EDGE, FROM_R)

    def put(ref):
        def store(block, x):
            ref[:, starts[block] : starts[block] + EDGE] = x

        return store

    finish(*refs[:13], put(dens), put(value), *refs[21:])
    prepare_sides(dens, value, *refs[17:21])


def last_sides_kernel(*refs):
    dens_out, value_out = refs[15:17]
    dens_s, value_s, dens_t, value_t, turn, semaphores = refs[17:]
    starts = (0, EDGE, FROM_R - EDGE, FROM_R)
    copies = []

    def put(sides, out):
        def store(block, x):
            lanes = slice(EDGE * block, EDGE * block + EDGE)
            sides[:, lanes] = x
            target = out.at[:, starts[block] : starts[block] + EDGE]
            copy = pltpu.make_async_copy(sides.at[:, lanes], target, semaphores.at[len(copies)])
            copy.start()
            copies.append(copy)

        return store

    finish(*refs[:13], put(dens_s, dens_out), put(value_s, value_out), dens_t, value_t, turn)
    for copy in copies:
        copy.wait()


def row_pairs(count, first):
    pairs = []
    for a in range(first, count, 2):
        b = (a + 1) % count
        pairs += [(a, b), (b, a)]
    return pairs


def body(density, value_field, potential, kern_rows, kern_cols):
    n_rows = lax.axis_size("rows")
    n_cols = lax.axis_size("cols")
    far_pairs = row_pairs(n_rows, 1)
    near_pairs = row_pairs(n_rows, 0)
    to_right = [(c, (c + 1) % n_cols) for c in range(n_cols)]
    to_left = [(c, (c - 1) % n_cols) for c in range(n_cols)]
    dens, value, side, own_t, far_1, near_1 = call(
        first_sides_kernel,
        [BLOCK, BLOCK] + FIRST,
        [pltpu.SemaphoreType.DMA((8,))],
        1,
        density, value_field,
        hbm_in=(0, 1),
        mib=FIRST_MIB,
    )
    for step_index in range(STEPS):
        last = step_index == STEPS - 1
        new, far_2, near_2 = call(rest_kernel, SECOND, [], 1, dens, value)
        if step_index == 0:
            table = call(rows_table_kernel, ROWS_TABLE + TURNED_TABLE, [], TABLE_COST, kern_rows[None])
            rows_table, turned_table = table[0:2], table[2:4]
        far_1 = lax.ppermute(far_1, "rows", far_pairs)
        near_1 = lax.ppermute(near_1, "rows", near_pairs)
        far_2 = lax.ppermute(far_2, "rows", far_pairs)
        near_2 = lax.ppermute(near_2, "rows", near_pairs)
        left, right, seams, around, tall, mixed = call(
            edge_kernel,
            [shape(COL_ROWS, EDGE), shape(COL_ROWS, EDGE), shape(8, COLS), shape(8, COLS), shape(8, TALL), shape(ROWS, 2 * EDGE)],
            [pltpu.VMEM((8, COLS), F32), pltpu.VMEM((2 * KW, 2 * EDGE), F32)],
            EDGE_COST,
            dens, value, side, own_t, far_1, near_1, *rows_table,
        )
        right_in = lax.ppermute(left, "cols", to_left)
        left_in = lax.ppermute(right, "cols", to_right)
        scratch = [
            pltpu.VMEM((2 * KW, MID), F32),
            pltpu.VMEM((ROWS, MID), BF16),
            pltpu.VMEM((ROWS, MID), BF16),
            pltpu.VMEM((ROWS, INSIDE_N), F32),
        ]
        if last:
            scratch += [pltpu.VMEM((ROWS, INSIDE_N), F32), pltpu.SemaphoreType.DMA((2,))]
        if last:
            cong, inner, cost_t, *results = call(
                last_middle_kernel,
                [shape(ROWS, 4 * EDGE), BLOCK, shape(8, ROWS), BLOCK, BLOCK],
                scratch,
                3,
                new, seams, far_2, near_2, *rows_table, *cols_table, value, potential, around,
                hbm_out=(3, 4),
            )
        else:
            cong, inner, cost_t, dens_out, value_out, *cols_table = call(
                first_middle_kernel,
                [shape(ROWS, 4 * EDGE), BLOCK, shape(8, ROWS), BLOCK, BLOCK] + TURNED_TABLE,
                scratch,
                3,
                new, seams, far_2, near_2, *rows_table, kern_cols[None], value, potential, around,
            )
            results = [dens_out, value_out]
        operands = (cost_t, side, seams, tall, left_in, right_in, mixed, cong, inner, *turned_table, *cols_table, *results)
        if last:
            scratch = [pltpu.VMEM((ROWS, 4 * EDGE), F32), pltpu.VMEM((ROWS, 4 * EDGE), F32)]
            return tuple(
                call(
                    last_sides_kernel,
                    [BLOCK, BLOCK],
                    scratch + FINISH_SCRATCH + [pltpu.SemaphoreType.DMA((6,))],
                    1,
                    *operands,
                    hbm_in=(13, 14),
                    hbm_out=(0, 1),
                    aliases={13: 0, 14: 1},
                )
            )
        dens, value, side, own_t, far_1, near_1 = call(
            next_sides_kernel, [BLOCK, BLOCK] + FIRST, FINISH_SCRATCH, 1, *operands, aliases={13: 0, 14: 1}
        )


def solution(mesh):
    placed = (P("rows", "cols"), P("rows", "cols"), P("rows", "cols"), P(), P())
    return jax.shard_map(
        body,
        mesh=mesh,
        in_specs=placed,
        out_specs=(P("rows", "cols"), P("rows", "cols")),
        check_vma=False,
    )
```
